32 devices in a mesh: ctx: 8 (over z, x), exp: 4 (over y, core).
Axes of the slice: x: 2, y: 2, z: 4, core: 2. Of those that a mesh axis runs over, the one named last changes fastest.
Arguments:
- inputs: bfloat16 [2560, 2048], P(('ctx', 'exp')), may hold values from -6 to 6
- attn_gain: float32 [2048], replicated, may hold values from 0.1 to 1.9
- w_query: bfloat16 [2048, 2048], P(None, 'exp'), as said below
- w_key: bfloat16 [2048, 2048], P(None, 'exp'), as said below
- w_value: bfloat16 [2048, 2048], P(None, 'exp'), may hold values from -0.125 to 0.125
- w_out: bfloat16 [2048, 2048], P('exp'), may hold values from -0.125 to 0.125
- sel_blocks: int32 [2560, 16, 3], P('ctx', 'exp'), may hold values from 0 to 6, as said below
- ffn_gain: float32 [2048], replicated, may hold values from 0.1 to 1.9
- w_gate: bfloat16 [32, 2048, 704], P(('ctx', 'exp')), may hold values from -0.125 to 0.125
- w_up: bfloat16 [32, 2048, 704], P(('ctx', 'exp')), may hold values from -0.125 to 0.125
- w_down: bfloat16 [32, 704, 2048], P(('ctx', 'exp')), may hold values from -0.15625 to 0.15625
- routes: int32 [2560, 6], P(('ctx', 'exp')), may hold values from 0 to 15, all different within a row; in each aligned block of 80 rows (0 to 79, 80 to 159, ...) at most 40 rows name the same one
- gate_weights: float32 [2560, 6], P(('ctx', 'exp')), may hold values from 0.05 to 0.5
Outputs:
- layer_out: bfloat16 [2560, 2048], P(('ctx', 'exp'))
The draws below stay inside these ranges and needn't reach their ends.
Inputs may be any that keep to these rules, and one draw needn't show every extreme that they name: `sel_blocks`: for a query in block b = t // 320, the 3 entries of a head are distinct and lie below max(b, 3); entries below b name selected earlier blocks, and block b - 1 is always among them when b >= 1. `routes`: each row names 6 different experts; within the 80 rows of one device no expert is named by more than 40 rows. `w_query`: entries are bounded in magnitude by 8 * 2048 ** -0.5. `w_key`: entries are bounded in magnitude by 130 * 2048 ** -0.5.
All inputs are finite; a program needn't handle non-finite values.
Results may differ from the reference program's by a relative error of at most 0.014.
Values may be sent and summed in bfloat16 or wider, within the bound.
No kernel may reach another device: no remote copies, remote signals or barrier semaphores. Data moves between devices by JAX's collectives and lax.ppermute only.
A program may use at most 128 MiB of HBM per device.

```python
import math
import jax
import jax.numpy as jnp
import numpy as np
from jax import lax

D = 2048
H = 16
HD = 128
FF = 1408
TOPK = 6
SEL = 3
BLOCK = 320
TQ = 80
SEQ = 2560
FH = 704
EXPERTS = 16
CAP = 40


def draw_inputs(key, part):
    key = jax.random.fold_in(key, 11)
    first_key = jax.random.fold_in(key, 0)
    normal_rows = jnp.clip(jax.random.normal(first_key, (SEQ, D), jnp.float32), -6.0, 6.0)
    return (0.5 * normal_rows).astype(jnp.bfloat16)


def query_key(key):
    key = jax.random.fold_in(key, 23)
    first_key, second_key = jax.random.split(key, 2)
    columns = H * HD
    query_weight = jnp.clip(jax.random.normal(first_key, (D, columns), jnp.float32), -5.0, 5.0) * (1.6 / math.sqrt(D))
    other_weight = jnp.clip(jax.random.normal(second_key, (D, columns), jnp.float32), -5.0, 5.0) * (1.6 / math.sqrt(D))
    key_weight = other_weight
    return (query_weight, key_weight)


def draw_w_query(key, part):
    return query_key(key)[0].astype(jnp.bfloat16)


def draw_w_key(key, part):
    return query_key(key)[1].astype(jnp.bfloat16)


def draw_sel_blocks(key, part):
    key = jax.random.fold_in(key, 31)
    block_count = SEQ // BLOCK
    base_score = jax.random.randint(key, (SEQ, H, block_count), 0, 1024)
    own_index = (jnp.arange(SEQ, dtype=jnp.int32) // BLOCK)[:, None, None]
    block_ids = jnp.arange(block_count, dtype=jnp.int32)[None, None, :]
    priority = base_score + jnp.where(block_ids == own_index - 1, 4096, 0) + jnp.where(block_ids == 0, 384, 0)
    priority = jnp.where(block_ids < jnp.maximum(own_index, 3), priority, -1)
    ranked = priority * block_count + block_ids
    _, indices = lax.top_k(ranked, SEL)
    return indices.astype(jnp.int32)


def level_of(own_key, extent, cuts, least, largest):
    def one(axis_at, shards_of):
        draws = jax.random.uniform(jax.random.fold_in(jax.random.fold_in(own_key, 6), axis_at), (shards_of,), jnp.float32, least / len(cuts), largest / len(cuts))
        return jnp.repeat(jnp.exp(draws), extent[axis_at] // shards_of).reshape((-1,) + (1,) * (len(extent) - axis_at - 1))

    factor_of = one(*cuts[0])
    for cut in cuts[1:]:
        factor_of = factor_of * one(*cut)
    return factor_of


def shared_out(stream_key, own, number, rows, count, top, reach, lean):
    order = jax.random.permutation(stream_key, count)
    heavy_load, ordinary = load_shares(count, rows * top, reach, lean, True), load_shares(count, rows * top, reach, lean, False)
    places = jnp.arange(count)

    def named(lengths, rotation):
        used = int((lengths > 0).sum())
        fixed = max(1, used // 4)
        passed = fixed + (places - fixed + rotation * (used - fixed)) % max(1, count - fixed)
        return jnp.zeros((count,), jnp.int32).at[order[jnp.where(places < fixed, places, passed)]].set(jnp.asarray(lengths, jnp.int32))

    lengths = jnp.where(number % 4 == 0, named(heavy_load, number // 4), named(ordinary, number - number // 4 - 1))
    mixed = jax.random.permutation(jax.random.fold_in(own, 3), count)
    source_of, taker = mixed[0:count // 2 * 2:2], mixed[1:count // 2 * 2:2]
    slack = jnp.minimum(lengths[source_of] - 1, reach - lengths[taker]) // 2
    slack = jnp.where((source_of == order[0]) | (taker == order[0]) | (lengths[taker] == 0), 0, jnp.maximum(slack, 0))
    passed = jax.random.randint(jax.random.fold_in(own, 4), (count // 2,), 0, 1 << 20) % (slack + 1)
    lengths = lengths.at[source_of].add(-passed).at[taker].add(passed)
    members = jnp.searchsorted(jnp.cumsum(lengths), jnp.arange(rows * top), side="right").astype(jnp.int32)
    listing = members.reshape(top, rows).T
    listing = listing[jax.random.permutation(jax.random.fold_in(own, 1), rows)]
    rotation = jax.random.randint(jax.random.fold_in(own, 2), (rows, 1), 0, top)
    return jnp.take_along_axis(listing, (jnp.arange(top)[None, :] + rotation) % top, axis=1)


def load_shares(count, total, reach, lean, full):
    loads = [(1 << 20) // math.isqrt(grade ** lean) + 1 for grade in range(1, count + 1)]
    largest = reach if full else min(reach, max(-(-total // count), total * loads[0] // sum(loads)))
    least = 1 if total - largest >= count - 1 else 0
    counts, spare = [largest] + [least] * (count - 1), total - largest - least * (count - 1)
    while spare > 0:
        movable = [i for i in range(1, count) if counts[i] < largest] or [i for i in range(1, count) if counts[i] < reach]
        pool, left = sum([loads[i] for i in movable]), spare
        for i in movable:
            addition = min(reach - counts[i], max(1, left * loads[i] // pool), spare)
            counts[i] = counts[i] + addition
            spare = spare - addition
    return np.array(counts)


def scatter_about(key, extent, spread, limit, pieces=(), kind=jnp.bfloat16):
    drawn = spread * jax.random.normal(key, extent, jnp.float32)
    if pieces:
        drawn = drawn * level_of(key, extent, pieces, -0.22, 0.18)
    return jnp.clip(drawn, -limit, limit).astype(kind)


def setup_inputs(seed: int = 0) -> dict:
    key_list = jax.random.split(jax.random.key(seed), 14)
    inputs = draw_inputs(jax.random.fold_in(key_list[13], 71), 0)
    attn_gain = jnp.clip(1.0 + 0.18 * jax.random.normal(key_list[1], (D,), jnp.float32), 0.1, 1.9)
    w_query = draw_w_query(jax.random.fold_in(key_list[13], 71), 0)
    w_key = draw_w_key(jax.random.fold_in(key_list[13], 71), 0)
    w_value = scatter_about(key_list[4], (D, H * HD), D ** -0.5, 0.125, ((1, 4),))
    w_out = scatter_about(key_list[5], (H * HD, D), (H * HD) ** -0.5, 0.125, ((0, 4),))
    sel_blocks = draw_sel_blocks(jax.random.fold_in(key_list[13], 71), 0)
    ffn_gain = jnp.clip(1.0 + 0.18 * jax.random.normal(key_list[7], (D,), jnp.float32), 0.1, 1.9)
    w_gate = scatter_about(key_list[8], (2 * EXPERTS, D, FH), D ** -0.5, 0.125, ((0, 32),))
    w_up = scatter_about(key_list[9], (2 * EXPERTS, D, FH), D ** -0.5, 0.125, ((0, 32),))
    w_down = scatter_about(key_list[10], (2 * EXPERTS, FH, D), FF ** -0.5, 0.15625, ((0, 32),))
    routes_keys = jax.random.split(jax.random.fold_in(key_list[11], 1), SEQ // TQ)
    routes_turns = jax.random.permutation(jax.random.fold_in(key_list[11], 3), SEQ // TQ)
    routes = jax.vmap(lambda own, number: shared_out(jax.random.fold_in(key_list[11], 2), own, number, TQ, EXPERTS, TOPK, CAP, 2))(routes_keys, routes_turns).reshape((SEQ, TOPK))
    gate_weights = jnp.clip(jnp.exp(math.log(0.5) - 2.3025851 * jax.random.uniform(key_list[12], (SEQ, TOPK), jnp.float32) ** level_of(key_list[12], (SEQ, TOPK), ((0, 32),), -0.2, 0.2)), 0.05, 0.5)
    return dict(inputs=inputs, attn_gain=attn_gain, w_query=w_query, w_key=w_key, w_value=w_value, w_out=w_out, sel_blocks=sel_blocks, ffn_gain=ffn_gain, w_gate=w_gate, w_up=w_up, w_down=w_down, routes=routes, gate_weights=gate_weights)


def normalize(values, gain_vec):
    floats = values.astype(jnp.float32)
    factor = lax.rsqrt(lax.optimization_barrier(jnp.mean(floats * floats, axis=-1, keepdims=True)) + 1e-06)
    return (floats * factor * gain_vec).astype(jnp.bfloat16)

def reference(inputs, attn_gain, w_query, w_key, w_value, w_out, sel_blocks, ffn_gain, w_gate, w_up, w_down, routes, gate_weights):
    block_count = SEQ // BLOCK
    normed = normalize(inputs, attn_gain)

    def project(weight):
        rounded = lax.optimization_barrier(jnp.dot(normed, weight, preferred_element_type=jnp.float32).astype(jnp.bfloat16))
        return rounded.astype(jnp.float32)
    queries = project(w_query).reshape(block_count, BLOCK, H, HD)
    key_rows = project(w_key).reshape(SEQ, H, HD)
    value_rows = project(w_value).reshape(SEQ, H, HD)
    key_pos = jnp.arange(SEQ, dtype=jnp.int32)
    key_block = key_pos // BLOCK
    block_ids = jnp.arange(block_count, dtype=jnp.int32)
    selections = sel_blocks.reshape(block_count, BLOCK, H, SEL)
    scaling = 1.0 / math.sqrt(HD)

    def one_block(operands):
        block_queries, block_sel, block_index = operands
        scores = jnp.einsum('qhd,khd->hqk', block_queries, key_rows) * scaling
        chosen = jnp.any(block_sel[:, :, :, None] == block_ids, axis=2) & (block_ids < block_index)
        picked = jnp.transpose(jnp.take(chosen, key_block, axis=2), (1, 0, 2))
        query_pos = block_index * BLOCK + jnp.arange(BLOCK, dtype=jnp.int32)
        own_block = (key_block[None, :] == block_index) & (key_pos[None, :] <= query_pos[:, None])
        allowed = picked | own_block[None]
        row_max = lax.optimization_barrier(jnp.max(jnp.where(allowed, scores, -jnp.inf), axis=-1, keepdims=True))
        raw_weights = jnp.where(allowed, jnp.exp(scores - row_max), 0.0)
        row_sums = lax.optimization_barrier(jnp.sum(raw_weights, axis=-1))
        rounded = lax.optimization_barrier(raw_weights.astype(jnp.bfloat16)).astype(jnp.float32)
        summed = jnp.einsum('hqk,khd->qhd', rounded, value_rows) / jnp.transpose(row_sums)[:, :, None]
        return summed.astype(jnp.bfloat16).reshape(BLOCK, H * HD)
    attended = lax.map(one_block, (queries, selections, block_ids)).reshape(SEQ, H * HD)
    head_mixed = jnp.dot(attended, w_out, preferred_element_type=jnp.float32)
    residual = (inputs.astype(jnp.float32) + head_mixed).astype(jnp.bfloat16)
    ffn_in = normalize(residual, ffn_gain)
    row_limit = SEQ // TQ * CAP

    def expert_step(running, expert):
        hit = routes == expert
        weight_row = lax.optimization_barrier(jnp.sum(jnp.where(hit, gate_weights, 0.0), axis=1))
        used = jnp.any(hit, axis=1)
        row_index = jnp.nonzero(used, size=row_limit, fill_value=0)[0].astype(jnp.int32)
        valid = jnp.arange(row_limit, dtype=jnp.int32) < jnp.sum(used.astype(jnp.int32))
        chosen_rows = ffn_in[row_index]
        partial_value = jnp.zeros((row_limit, D), jnp.float32)
        for half_index in range(2):
            which_row = 2 * expert + half_index
            gate_part = jnp.dot(chosen_rows, w_gate[which_row], preferred_element_type=jnp.float32)
            up_part = jnp.dot(chosen_rows, w_up[which_row], preferred_element_type=jnp.float32)
            hidden = (jax.nn.silu(gate_part) * up_part).astype(jnp.bfloat16)
            partial_value = partial_value + jnp.dot(hidden, w_down[which_row], preferred_element_type=jnp.float32)
        expert_out = lax.optimization_barrier(partial_value.astype(jnp.bfloat16)).astype(jnp.float32)
        factor = jnp.where(valid, weight_row[row_index], 0.0)
        running = running.at[row_index].add(expert_out * factor[:, None])
        return (running, None)
    expert_mix, _ = lax.scan(expert_step, jnp.zeros((SEQ, D), jnp.float32), jnp.arange(EXPERTS, dtype=jnp.int32))
    return (residual.astype(jnp.float32) + expert_mix).astype(jnp.bfloat16)
```

```python
import functools
import math

import jax
import jax.numpy as jnp
from jax import lax
from jax.experimental import pallas as pl
from jax.experimental.pallas import tpu as pltpu
from jax.sharding import PartitionSpec as P

AXES = ("ctx", "exp")
PARAMS = pltpu.CompilerParams(vmem_limit_bytes=56 * 1024 * 1024)
VMEM = pl.BlockSpec(memory_space=pltpu.VMEM)
SMEM = pl.BlockSpec(memory_space=pltpu.SMEM)
PAD_ROWS = 16
LANES = 128


def move(block, target):
    ctx_count, exp_count = lax.axis_size("ctx"), lax.axis_size("exp")
    route = []
    for ctx in range(ctx_count):
        for exp in range(exp_count):
            z, x, y, c = target(ctx // 2, ctx % 2, exp // 2, exp % 2)
            route.append((ctx * exp_count + exp, (z * 2 + x) * exp_count + y * 2 + c))
    return lax.ppermute(block, AXES, route)


def swap_core(block):
    return move(block, lambda z, x, y, c: (z, x, y, c ^ 1))


def swap_layer(block, hop):
    return move(block, lambda z, x, y, c: (z, x ^ (hop >> 1), y ^ (hop & 1), c))


def turn_z(block, turn):
    depth = lax.axis_size("ctx") // 2
    return move(block, lambda z, x, y, c: ((z + turn) % depth, x, y, c))


def head_out(block, turn):
    depth = lax.axis_size("ctx") // 2
    return move(block, lambda z, x, y, c: ((z + turn) % depth, c, y, x))


def head_back(block, turn):
    depth = lax.axis_size("ctx") // 2
    return move(block, lambda z, x, y, c: ((z - turn) % depth, c, y, x))


def normalize(values, gain_vec):
    floats = values.astype(jnp.float32)
    factor = lax.rsqrt(jnp.mean(floats * floats, axis=-1, keepdims=True) + 1e-06)
    return (floats * factor * gain_vec).astype(jnp.bfloat16)


def f32_dot(left, right):
    return jnp.dot(left, right, preferred_element_type=jnp.float32)


def struct(*shape, dtype=jnp.bfloat16):
    return jax.ShapeDtypeStruct(shape, dtype)


def call(kernel, outs, operands, scratch=(), flops=0, smem=1):
    return pl.pallas_call(
        kernel,
        out_shape=outs,
        in_specs=[SMEM] * smem + [VMEM] * (len(operands) - smem),
        out_specs=jax.tree.map(lambda _: VMEM, outs),
        scratch_shapes=list(scratch),
        compiler_params=PARAMS,
        cost_estimate=pl.CostEstimate(
            flops=flops,
            bytes_accessed=sum(a.size * a.dtype.itemsize for a in operands),
            transcendentals=0,
        ),
    )(*operands)


def project_kernel(hops, depth, head_dim, place, *refs):
    row_refs, (gain, w_query, w_key, w_value, marks) = refs[:hops], refs[hops : hops + 5]
    outs, (rows, mixed) = refs[hops + 5 : hops + 5 + depth], refs[hops + 5 + depth :]
    exp_index, z_index = place[0], place[1]
    tok_rows = row_refs[0].shape[0]
    block_len = hops * tok_rows
    for hop, row_ref in enumerate(row_refs):
        start = pl.multiple_of((exp_index ^ hop) * tok_rows, 16)
        rows[pl.ds(start, tok_rows), :] = normalize(row_ref[...], gain[...])
    for part, weight in enumerate((w_query, w_key, w_value)):
        mixed[part] = f32_dot(rows[...], weight[...]).astype(jnp.bfloat16)
    for turn in range(depth):
        head = lax.rem(z_index + turn, depth)
        columns = pl.ds(pl.multiple_of(head * head_dim, head_dim), head_dim)
        for part in range(3):
            outs[turn][0:block_len, part * head_dim : (part + 1) * head_dim] = mixed[part, :, columns]
        outs[turn][block_len : block_len + PAD_ROWS, :] = marks[head]


def attend_kernel(depth, block_len, head_dim, place, *refs):
    own_refs, near_refs = refs[:depth], refs[depth : 2 * depth]
    outs, (own, near, mixed) = refs[2 * depth : 3 * depth], refs[3 * depth :]
    z_index, core = place[1], place[2]
    scaling = 1.0 / math.sqrt(head_dim)
    for turn in range(depth):
        source = lax.rem(z_index + depth - turn, depth)
        own[source] = own_refs[turn][...]
        near[source] = near_refs[turn][0:block_len, head_dim : 3 * head_dim]
    key_pos = lax.broadcasted_iota(jnp.int32, (block_len, block_len), 0)
    query_pos = lax.broadcasted_iota(jnp.int32, (block_len, block_len), 1)
    causal = jnp.where(key_pos <= query_pos, 0.0, -1e30)
    for level in range(depth):
        query = own[level, 0:block_len, 0:head_dim]
        marks = own[level, block_len : block_len + PAD_ROWS, 0:block_len].astype(jnp.float32)
        marks = marks[0:1].astype(jnp.int32)
        run_max = run_sum = total = None
        order = [(level, True)] + [(c, True) for c in range(level)] + [(c, False) for c in range(level + 1)]
        for c, mine in order:
            if mine:
                key = own[c, 0:block_len, head_dim : 2 * head_dim]
                value = own[c, 0:block_len, 2 * head_dim : 3 * head_dim]
            else:
                key, value = near[c, :, 0:head_dim], near[c, :, head_dim : 2 * head_dim]
            scores = scaling * lax.dot_general(
                key, query, (((1,), (1,)), ((), ())), preferred_element_type=jnp.float32
            )
            if mine and c == level:
                scores = scores + causal
            else:
                bit = 2 * c + (core if mine else 1 - core)
                chosen = lax.shift_right_logical(marks, jnp.broadcast_to(bit, marks.shape)) & 1
                scores = jnp.where(chosen == 1, scores, -1e30)
            top = jnp.max(scores, axis=0, keepdims=True)
            new_max = top if run_max is None else jnp.maximum(run_max, top)
            weights = jnp.exp(scores - new_max)
            added = jnp.sum(weights, axis=0, keepdims=True)
            product = lax.dot_general(
                value,
                weights.astype(jnp.bfloat16),
                (((0,), (0,)), ((), ())),
                preferred_element_type=jnp.float32,
            )
            if run_max is None:
                run_sum, total = added, product
            else:
                rescale = jnp.exp(run_max - new_max)
                run_sum, total = run_sum * rescale + added, total * rescale + product
            run_max = new_max
        mixed[level] = (total / run_sum).T.astype(jnp.bfloat16)
    for turn in range(depth):
        outs[turn][...] = mixed[lax.rem(z_index + depth - turn, depth)]


def attend_gathered(normed_block, w_query, w_key, w_value, sel_blocks):
    block_len, heads_here, _ = sel_blocks.shape
    hidden_cols = w_query.shape[1]
    head_dim = hidden_cols // heads_here
    ctx_count, ctx_index = lax.axis_size("ctx"), lax.axis_index("ctx")
    query_part, key_part, value_part = (
        f32_dot(normed_block, weight).astype(jnp.bfloat16) for weight in (w_query, w_key, w_value)
    )
    queries = query_part.reshape(block_len, heads_here, head_dim)
    keys_values = jnp.stack([key_part, value_part], axis=1)
    block_ids = jnp.arange(ctx_count, dtype=jnp.int32)
    chosen = jnp.any(sel_blocks[:, :, :, None] == block_ids, axis=2) & (block_ids < ctx_index)
    position = jnp.arange(block_len, dtype=jnp.int32)
    causal = position[None, :] <= position[:, None]
    scaling = 1.0 / math.sqrt(head_dim)

    def fold_step(running, operands):
        run_max, run_sum, totals = running
        piece, block = operands
        key_rows = piece[:, 0].reshape(block_len, heads_here, head_dim)
        value_rows = piece[:, 1].reshape(block_len, heads_here, head_dim)
        scores = (
            jnp.einsum("qhd,khd->hqk", queries, key_rows, preferred_element_type=jnp.float32)
            * scaling
        )
        picked = jnp.take(chosen, block, axis=2).T[:, :, None]
        allowed = picked | ((block == ctx_index) & causal)[None]
        new_max = jnp.maximum(run_max, jnp.max(jnp.where(allowed, scores, -jnp.inf), axis=-1))
        weights = jnp.where(allowed, jnp.exp(scores - new_max[..., None]), 0.0)
        rescale = jnp.exp(run_max - new_max)
        run_sum = run_sum * rescale + jnp.sum(weights, axis=-1)
        totals = totals * rescale[..., None] + jnp.einsum(
            "hqk,khd->hqd",
            weights.astype(jnp.bfloat16),
            value_rows,
            preferred_element_type=jnp.float32,
        )
        return (new_max, run_sum, totals), None

    initial = (
        jnp.full((heads_here, block_len), -1e30, jnp.float32),
        jnp.zeros((heads_here, block_len), jnp.float32),
        jnp.zeros((heads_here, block_len, head_dim), jnp.float32),
    )
    gathered = lax.all_gather(keys_values, "ctx", axis=0)
    (_, run_sum, totals), _ = lax.scan(fold_step, initial, (gathered, block_ids))
    attended = (totals / run_sum[..., None]).astype(jnp.bfloat16)
    return [attended[head] for head in range(heads_here)]


def mix_kernel(hops, heads, head_dim, place, *refs):
    head_refs, w_out = refs[:heads], refs[heads]
    kept, given, attended, mixed = refs[heads + 1 :]
    exp_index, turned = place[0], place[3]
    tok_rows = kept.shape[1]
    for turn, head_ref in enumerate(head_refs):
        head = lax.rem(turned + turn, heads)
        attended[:, pl.ds(pl.multiple_of(head * head_dim, head_dim), head_dim)] = head_ref[...]
    mixed[...] = f32_dot(attended[...], w_out[...]).astype(jnp.bfloat16)
    for hop in range(hops):
        start = pl.multiple_of((exp_index ^ hop) * tok_rows, 16)
        (given if hop & 1 else kept)[hop >> 1] = mixed[pl.ds(start, tok_rows), :]


def residual_kernel(inputs, kept, given, far, gain, residual, ffn_in):
    summed = kept[0].astype(jnp.float32) + given[0].astype(jnp.float32) + far[...].astype(jnp.float32)
    rounded = (inputs[...].astype(jnp.float32) + summed).astype(jnp.bfloat16)
    residual[...] = rounded
    ffn_in[...] = normalize(rounded, gain[...])


def pack_kernel(depth, capacity, place, routes, *refs):
    sources, outs, (rows,) = refs[:depth], refs[depth : depth + 4], refs[depth + 4 :]
    expert = place[4]
    tok_rows = sources[0].shape[0]
    total = depth * tok_rows
    for turn in range(depth):
        rows[turn * tok_rows : (turn + 1) * tok_rows, :] = sources[turn][...]
    earlier = lax.broadcasted_iota(jnp.int32, (total, total), 0)
    later = lax.broadcasted_iota(jnp.int32, (total, total), 1)
    before = ((earlier < later) & (earlier // tok_rows == later // tok_rows)).astype(jnp.bfloat16)
    first_slot = lax.broadcasted_iota(jnp.int32, (1, total), 1) // tok_rows * capacity
    slot = lax.broadcasted_iota(jnp.int32, (depth * capacity, total), 0)
    for hop in range(4):
        hit = jnp.where(routes[...] == (expert ^ hop).astype(jnp.float32), 1.0, 0.0)
        member = jnp.sum(hit, axis=0, keepdims=True)
        place_in = f32_dot(jnp.broadcast_to(member, (16, total)).astype(jnp.bfloat16), before)[0:1]
        target = jnp.where(member > 0.5, place_in.astype(jnp.int32) + first_slot, -1)
        placing = jnp.where(slot == target, 1.0, 0.0).astype(jnp.bfloat16)
        outs[hop][...] = f32_dot(placing, rows[...]).astype(jnp.bfloat16)


def expert_kernel(parts, *refs):
    row_refs, (w_gate, w_up, w_down), outs = refs[:parts], refs[parts : parts + 3], refs[parts + 3 :]
    across = (((1,), (1,)), ((), ()))
    for first in range(0, parts, 2):
        rows = jnp.concatenate([row_refs[first][...], row_refs[first + 1][...]], axis=0)
        gate_part = lax.dot_general(rows, w_gate[...], across, preferred_element_type=jnp.float32)
        up_part = lax.dot_general(rows, w_up[...], across, preferred_element_type=jnp.float32)
        hidden = (gate_part / (1.0 + jnp.exp(-gate_part)) * up_part).astype(jnp.bfloat16)
        result = f32_dot(hidden, w_down[...]).astype(jnp.bfloat16)
        half = row_refs[first].shape[0]
        outs[first][...] = result[:half]
        outs[first + 1][...] = result[half:]


def combine_kernel(depth, capacity, place, routes, gates, *refs):
    returned, outs = refs[:4], refs[4 : 4 + depth]
    expert = place[4]
    total = routes.shape[0]
    tok_rows = total // depth
    later = lax.broadcasted_iota(jnp.int32, (total, total), 0)
    earlier = lax.broadcasted_iota(jnp.int32, (total, total), 1)
    before = ((earlier < later) & (earlier // tok_rows == later // tok_rows)).astype(jnp.bfloat16)
    first_slot = lax.broadcasted_iota(jnp.int32, (total, 1), 0) // tok_rows * capacity
    slot = lax.broadcasted_iota(jnp.int32, (total, depth * capacity), 1)
    mixed = jnp.zeros((total, returned[0].shape[1]), jnp.float32)
    for hop in range(4):
        hit = routes[...] == (expert ^ hop).astype(jnp.float32)
        member = jnp.sum(jnp.where(hit, 1.0, 0.0), axis=1, keepdims=True)
        factor = jnp.sum(jnp.where(hit, gates[...], 0.0), axis=1, keepdims=True)
        place_in = f32_dot(before, jnp.broadcast_to(member, (total, LANES)).astype(jnp.bfloat16))[:, 0:1]
        target = jnp.where(member > 0.5, place_in.astype(jnp.int32) + first_slot, -1)
        placing = jnp.where(slot == target, factor, 0.0)
        upper = placing.astype(jnp.bfloat16)
        lower = (placing - upper.astype(jnp.float32)).astype(jnp.bfloat16)
        mixed = mixed + f32_dot(upper, returned[hop][...]) + f32_dot(lower, returned[hop][...])
    for turn in range(depth):
        outs[turn][...] = mixed[turn * tok_rows : (turn + 1) * tok_rows].astype(jnp.bfloat16)


def shards(
    inputs,
    attn_gain,
    w_query,
    w_key,
    w_value,
    w_out,
    sel_blocks,
    ffn_gain,
    w_gate,
    w_up,
    w_down,
    routes,
    gate_weights,
):
    tok_rows, model_width = inputs.shape
    block_len, heads_here, pick_count = sel_blocks.shape
    hidden_cols = w_query.shape[1]
    head_dim = hidden_cols // heads_here
    ctx_count, exp_count = lax.axis_size("ctx"), lax.axis_size("exp")
    depth = ctx_count // 2
    ctx_index, exp_index = lax.axis_index("ctx"), lax.axis_index("exp")
    z_index, x_index = ctx_index // 2, ctx_index % 2
    expert = (ctx_index * exp_count + exp_index) // 2
    by_head = heads_here == depth and block_len <= 3 * head_dim and head_dim == LANES
    place = jnp.stack(
        [exp_index, z_index, exp_index % 2, z_index if by_head else jnp.zeros_like(z_index), expert]
    ).astype(jnp.int32)

    noted = jnp.concatenate([routes.astype(jnp.float32), gate_weights], axis=1)
    noted = lax.all_gather(noted, "ctx", axis=0).reshape(depth, 2, tok_rows, -1)
    noted = lax.dynamic_index_in_dim(noted, x_index, 1, keepdims=False)
    sources = (z_index - jnp.arange(depth)) % depth
    noted = noted[sources].reshape(depth * tok_rows, -1)
    top_count = routes.shape[1]
    near_routes, near_gates = noted[:, :top_count], noted[:, top_count:]

    near = swap_core(inputs)
    far = move(inputs, lambda z, x, y, c: (z, x, y ^ 1, c))
    far_near = swap_core(far)
    if by_head:
        marks = jnp.sum(
            jnp.where(sel_blocks < ctx_index, jnp.left_shift(1, jnp.minimum(sel_blocks, 30)), 0), axis=2
        )
        marks = jnp.pad(marks.T.astype(jnp.bfloat16), ((0, 0), (0, 3 * head_dim - block_len)))
        marks = jnp.broadcast_to(marks[:, None], (heads_here, PAD_ROWS, 3 * head_dim))
        payload = struct(block_len + PAD_ROWS, 3 * head_dim)
        sent = call(
            functools.partial(project_kernel, exp_count, depth, head_dim),
            [payload] * depth,
            [place, inputs, near, far, far_near, attn_gain.reshape(1, -1), w_query, w_key, w_value, marks],
            [
                pltpu.VMEM((block_len, model_width), jnp.bfloat16),
                pltpu.VMEM((3, block_len, hidden_cols), jnp.bfloat16),
            ],
            flops=6 * block_len * model_width * hidden_cols,
        )
        own = [head_out(sent[turn], turn) for turn in range(depth)]
        beside = [swap_core(block) for block in own]
        mixed = call(
            functools.partial(attend_kernel, depth, block_len, head_dim),
            [struct(block_len, head_dim)] * depth,
            [place, *own, *beside],
            [
                pltpu.VMEM((depth, block_len + PAD_ROWS, 3 * head_dim), jnp.bfloat16),
                pltpu.VMEM((depth, block_len, 2 * head_dim), jnp.bfloat16),
                pltpu.VMEM((depth, block_len, head_dim), jnp.bfloat16),
            ],
            flops=4 * depth * ctx_count * block_len * block_len * head_dim,
        )
        heads = [head_back(mixed[turn], turn) for turn in range(depth)]
    else:
        block = jnp.stack([inputs, near, far, far_near])[exp_index ^ jnp.arange(exp_count)]
        normed = normalize(block.reshape(block_len, model_width), attn_gain)
        heads = attend_gathered(normed, w_query, w_key, w_value, sel_blocks)

    halves = struct(exp_count // 2, tok_rows, model_width)
    kept, given = call(
        functools.partial(mix_kernel, exp_count, heads_here, head_dim),
        [halves, halves],
        [place, *heads, w_out],
        [
            pltpu.VMEM((block_len, hidden_cols), jnp.bfloat16),
            pltpu.VMEM((block_len, model_width), jnp.bfloat16),
        ],
        flops=2 * block_len * model_width * hidden_cols,
    )
    given = swap_core(given)
    beyond = (kept[1].astype(jnp.float32) + given[1].astype(jnp.float32)).astype(jnp.bfloat16)
    beyond = move(beyond, lambda z, x, y, c: (z, x, y ^ 1, c))
    residual, ffn_in = call(
        residual_kernel,
        [struct(tok_rows, model_width)] * 2,
        [inputs, kept, given, beyond, ffn_gain.reshape(1, -1)],
        smem=0,
    )

    experts = ctx_count * exp_count // 2
    capacity = 2 * max(1, (tok_rows * top_count + experts - 1) // experts * 2 // 3)
    slots = depth * capacity
    column = [ffn_in] + [turn_z(ffn_in, turn) for turn in range(1, depth)]
    packed = call(
        functools.partial(pack_kernel, depth, capacity),
        [struct(slots, model_width)] * 4,
        [place, near_routes.T, *column],
        [pltpu.VMEM((depth * tok_rows, model_width), jnp.bfloat16)],
        flops=8 * slots * depth * tok_rows * model_width,
    )
    arrived = [packed[0]] + [swap_layer(packed[hop], hop) for hop in range(1, 4)]
    beside = [swap_core(rows) for rows in arrived]
    weights = [w_gate[0].T, w_up[0].T, w_down[0]]

    def expert_rows(rows):
        return call(
            functools.partial(expert_kernel, len(rows)),
            [struct(slots, model_width)] * len(rows),
            [*rows, *weights],
            flops=6 * len(rows) * slots * model_width * w_gate.shape[2],
            smem=0,
        )

    own_part = expert_rows(arrived)
    beside_part = expert_rows(beside)
    other_part = [swap_core(rows) for rows in beside_part]
    results = [
        (own.astype(jnp.float32) + other.astype(jnp.float32)).astype(jnp.bfloat16)
        for own, other in zip(own_part, other_part)
    ]
    returned = [results[0]] + [swap_layer(results[hop], hop) for hop in range(1, 4)]
    sums = call(
        functools.partial(combine_kernel, depth, capacity),
        [struct(tok_rows, model_width)] * depth,
        [place, near_routes, near_gates, *returned],
        flops=16 * slots * depth * tok_rows * model_width,
    )
    layer_out = residual.astype(jnp.float32) + sums[0].astype(jnp.float32)
    for turn in range(1, depth):
        layer_out = layer_out + turn_z(sums[turn], -turn).astype(jnp.float32)
    return layer_out.astype(jnp.bfloat16)


def solution(mesh):
    placed = (
        P(("ctx", "exp"), None),
        P(),
        P(None, "exp"),
        P(None, "exp"),
        P(None, "exp"),
        P("exp", None),
        P("ctx", "exp", None),
        P(),
        P(("ctx", "exp"), None, None),
        P(("ctx", "exp"), None, None),
        P(("ctx", "exp"), None, None),
        P(("ctx", "exp"), None),
        P(("ctx", "exp"), None),
    )
    return jax.shard_map(
        shards, mesh=mesh, in_specs=placed, out_specs=P(("ctx", "exp"), None), check_vma=False
    )
```

```python
import functools
import math

import jax
import jax.numpy as jnp
from jax import lax
from jax.experimental import pallas as pl
from jax.experimental.pallas import tpu as pltpu
from jax.sharding import PartitionSpec as P

AXES = ("ctx", "exp")
PARAMS = pltpu.CompilerParams(vmem_limit_bytes=24 * 1024 * 1024)
VMEM = pl.BlockSpec(memory_space=pltpu.VMEM)
SMEM = pl.BlockSpec(memory_space=pltpu.SMEM)
PAD_ROWS = 16
LANES = 128


def move(block, target):
    ctx_count, exp_count = lax.axis_size("ctx"), lax.axis_size("exp")
    route = []
    for ctx in range(ctx_count):
        for exp in range(exp_count):
            z, x, y, c = target(ctx // 2, ctx % 2, exp // 2, exp % 2)
            route.append((ctx * exp_count + exp, (z * 2 + x) * exp_count + y * 2 + c))
    return lax.ppermute(block, AXES, route)


def swap_core(block):
    return move(block, lambda z, x, y, c: (z, x, y, c ^ 1))


def swap_layer(block, hop):
    return move(block, lambda z, x, y, c: (z, x ^ (hop >> 1), y ^ (hop & 1), c))


def turn_z(block, turn):
    depth = lax.axis_size("ctx") // 2
    return move(block, lambda z, x, y, c: ((z + turn) % depth, x, y, c))


def gather_z(block):
    depth = lax.axis_size("ctx") // 2
    column = [block] + [None] * (depth - 1)
    for turn in range(1, depth // 2 + 1):
        column[turn] = turn_z(column[turn - 1], 1)
    for turn in range(depth - 1, depth // 2, -1):
        column[turn] = turn_z(column[(turn + 1) % depth], -1)
    return column


def scatter_z(sums):
    depth = len(sums)

    def added(left, right):
        return (left.astype(jnp.float32) + right.astype(jnp.float32)).astype(left.dtype)

    below, above = None, None
    for turn in range(depth // 2, 0, -1):
        below = turn_z(sums[turn] if below is None else added(below, sums[turn]), -1)
    for turn in range(depth // 2 + 1, depth):
        above = turn_z(sums[turn] if above is None else added(above, sums[turn]), 1)
    return [part for part in (below, above) if part is not None]


def head_out(block, turn):
    depth = lax.axis_size("ctx") // 2
    return move(block, lambda z, x, y, c: ((z + turn) % depth, c, y, x))


def head_back(block, turn):
    depth = lax.axis_size("ctx") // 2
    return move(block, lambda z, x, y, c: ((z - turn) % depth, c, y, x))


def normalize(values, gain_vec):
    floats = values.astype(jnp.float32)
    factor = lax.rsqrt(jnp.mean(floats * floats, axis=-1, keepdims=True) + 1e-06)
    return (floats * factor * gain_vec).astype(jnp.bfloat16)


def f32_dot(left, right):
    return jnp.dot(left, right, preferred_element_type=jnp.float32)


def struct(*shape, dtype=jnp.bfloat16):
    return pltpu.VMEM(shape, dtype)


def call(kernel, outs, operands, scratch=(), flops=0, smem=1):
    operands = operands[:smem] + [
        pltpu.with_memory_space_constraint(a, pltpu.VMEM) for a in operands[smem:]
    ]
    return pl.pallas_call(
        kernel,
        out_shape=outs,
        in_specs=[SMEM] * smem + [VMEM] * (len(operands) - smem),
        out_specs=jax.tree.map(lambda _: VMEM, outs),
        scratch_shapes=list(scratch),
        compiler_params=PARAMS,
        cost_estimate=pl.CostEstimate(
            flops=flops,
            bytes_accessed=sum(a.size * a.dtype.itemsize for a in operands),
            transcendentals=0,
        ),
    )(*operands)


def project_kernel(hops, depth, head_dim, place, *refs):
    row_refs, (gain, w_query, w_key, w_value, marks) = refs[:hops], refs[hops : hops + 5]
    outs, (rows, mixed) = refs[hops + 5 : hops + 5 + depth], refs[hops + 5 + depth :]
    exp_index, z_index = place[0], place[1]
    tok_rows = row_refs[0].shape[0]
    block_len = hops * tok_rows
    for hop, row_ref in enumerate(row_refs):
        start = pl.multiple_of((exp_index ^ hop) * tok_rows, 16)
        rows[pl.ds(start, tok_rows), :] = normalize(row_ref[...], gain[...])
    for part, weight in enumerate((w_query, w_key, w_value)):
        mixed[part] = f32_dot(rows[...], weight[...]).astype(jnp.bfloat16)
    for turn in range(depth):
        head = lax.rem(z_index + turn, depth)
        columns = pl.ds(pl.multiple_of(head * head_dim, head_dim), head_dim)
        for part in range(3):
            outs[turn][0:block_len, part * head_dim : (part + 1) * head_dim] = mixed[part, :, columns]
        outs[turn][block_len : block_len + PAD_ROWS, :] = marks[head]


def attend_kernel(depth, block_len, head_dim, place, *refs):
    own_refs, near_refs = refs[:depth], refs[depth : 2 * depth]
    outs, (own, near, mixed) = refs[2 * depth : 3 * depth], refs[3 * depth :]
    z_index, core = place[1], place[2]
    scaling = 1.0 / math.sqrt(head_dim)
    for turn in range(depth):
        source = lax.rem(z_index + depth - turn, depth)
        own[source] = own_refs[turn][...]
        near[source] = near_refs[turn][0:block_len, head_dim : 3 * head_dim]
    key_pos = lax.broadcasted_iota(jnp.int32, (block_len, block_len), 0)
    query_pos = lax.broadcasted_iota(jnp.int32, (block_len, block_len), 1)
    causal = jnp.where(key_pos <= query_pos, 0.0, -1e30)
    for level in range(depth):
        query = own[level, 0:block_len, 0:head_dim]
        marks = own[level, block_len : block_len + PAD_ROWS, 0:block_len].astype(jnp.float32)
        marks = marks[0:1].astype(jnp.int32)
        run_max = run_sum = total = None
        order = [(level, True)] + [(c, True) for c in range(level)] + [(c, False) for c in range(level + 1)]
        for c, mine in order:
            if mine:
                key = own[c, 0:block_len, head_dim : 2 * head_dim]
                value = own[c, 0:block_len, 2 * head_dim : 3 * head_dim]
            else:
                key, value = near[c, :, 0:head_dim], near[c, :, head_dim : 2 * head_dim]
            scores = scaling * lax.dot_general(
                key, query, (((1,), (1,)), ((), ())), preferred_element_type=jnp.float32
            )
            if mine and c == level:
                scores = scores + causal
            else:
                bit = 2 * c + (core if mine else 1 - core)
                chosen = lax.shift_right_logical(marks, jnp.broadcast_to(bit, marks.shape)) & 1
                scores = jnp.where(chosen == 1, scores, -1e30)
            top = jnp.max(scores, axis=0, keepdims=True)
            new_max = top if run_max is None else jnp.maximum(run_max, top)
            weights = jnp.exp(scores - new_max)
            added = jnp.sum(weights, axis=0, keepdims=True)
            product = lax.dot_general(
                value,
                weights.astype(jnp.bfloat16),
                (((0,), (0,)), ((), ())),
                preferred_element_type=jnp.float32,
            )
            if run_max is None:
                run_sum, total = added, product
            else:
                rescale = jnp.exp(run_max - new_max)
                run_sum, total = run_sum * rescale + added, total * rescale + product
            run_max = new_max
        mixed[level] = (total / run_sum).T.astype(jnp.bfloat16)
    for turn in range(depth):
        outs[turn][...] = mixed[lax.rem(z_index + depth - turn, depth)]


def attend_gathered(normed_block, w_query, w_key, w_value, sel_blocks):
    block_len, heads_here, _ = sel_blocks.shape
    hidden_cols = w_query.shape[1]
    head_dim = hidden_cols // heads_here
    ctx_count, ctx_index = lax.axis_size("ctx"), lax.axis_index("ctx")
    query_part, key_part, value_part = (
        f32_dot(normed_block, weight).astype(jnp.bfloat16) for weight in (w_query, w_key, w_value)
    )
    queries = query_part.reshape(block_len, heads_here, head_dim)
    keys_values = jnp.stack([key_part, value_part], axis=1)
    block_ids = jnp.arange(ctx_count, dtype=jnp.int32)
    chosen = jnp.any(sel_blocks[:, :, :, None] == block_ids, axis=2) & (block_ids < ctx_index)
    position = jnp.arange(block_len, dtype=jnp.int32)
    causal = position[None, :] <= position[:, None]
    scaling = 1.0 / math.sqrt(head_dim)

    def fold_step(running, operands):
        run_max, run_sum, totals = running
        piece, block = operands
        key_rows = piece[:, 0].reshape(block_len, heads_here, head_dim)
        value_rows = piece[:, 1].reshape(block_len, heads_here, head_dim)
        scores = (
            jnp.einsum("qhd,khd->hqk", queries, key_rows, preferred_element_type=jnp.float32)
            * scaling
        )
        picked = jnp.take(chosen, block, axis=2).T[:, :, None]
        allowed = picked | ((block == ctx_index) & causal)[None]
        new_max = jnp.maximum(run_max, jnp.max(jnp.where(allowed, scores, -jnp.inf), axis=-1))
        weights = jnp.where(allowed, jnp.exp(scores - new_max[..., None]), 0.0)
        rescale = jnp.exp(run_max - new_max)
        run_sum = run_sum * rescale + jnp.sum(weights, axis=-1)
        totals = totals * rescale[..., None] + jnp.einsum(
            "hqk,khd->hqd",
            weights.astype(jnp.bfloat16),
            value_rows,
            preferred_element_type=jnp.float32,
        )
        return (new_max, run_sum, totals), None

    initial = (
        jnp.full((heads_here, block_len), -1e30, jnp.float32),
        jnp.zeros((heads_here, block_len), jnp.float32),
        jnp.zeros((heads_here, block_len, head_dim), jnp.float32),
    )
    gathered = lax.all_gather(keys_values, "ctx", axis=0)
    (_, run_sum, totals), _ = lax.scan(fold_step, initial, (gathered, block_ids))
    attended = (totals / run_sum[..., None]).astype(jnp.bfloat16)
    return [attended[head] for head in range(heads_here)]


def mix_kernel(hops, heads, head_dim, place, *refs):
    head_refs, w_out = refs[:heads], refs[heads]
    kept, given, attended, mixed = refs[heads + 1 :]
    exp_index, turned = place[0], place[3]
    tok_rows = kept.shape[1]
    for turn, head_ref in enumerate(head_refs):
        head = lax.rem(turned + turn, heads)
        attended[:, pl.ds(pl.multiple_of(head * head_dim, head_dim), head_dim)] = head_ref[...]
    mixed[...] = f32_dot(attended[...], w_out[...]).astype(jnp.bfloat16)
    for hop in range(hops):
        start = pl.multiple_of((exp_index ^ hop) * tok_rows, 16)
        (given if hop & 1 else kept)[hop >> 1] = mixed[pl.ds(start, tok_rows), :]


def residual_kernel(inputs, kept, given, far, gain, residual, ffn_in):
    summed = kept[0].astype(jnp.float32) + given[0].astype(jnp.float32) + far[...].astype(jnp.float32)
    rounded = (inputs[...].astype(jnp.float32) + summed).astype(jnp.bfloat16)
    residual[...] = rounded
    ffn_in[...] = normalize(rounded, gain[...])


def pack_kernel(depth, capacity, place, routes, *refs):
    sources, outs, (rows,) = refs[:depth], refs[depth : depth + 4], refs[depth + 4 :]
    expert = place[4]
    tok_rows = sources[0].shape[0]
    total = depth * tok_rows
    for turn in range(depth):
        rows[turn * tok_rows : (turn + 1) * tok_rows, :] = sources[turn][...]
    earlier = lax.broadcasted_iota(jnp.int32, (total, total), 0)
    later = lax.broadcasted_iota(jnp.int32, (total, total), 1)
    before = ((earlier < later) & (earlier // tok_rows == later // tok_rows)).astype(jnp.bfloat16)
    first_slot = lax.broadcasted_iota(jnp.int32, (1, total), 1) // tok_rows * capacity
    slot = lax.broadcasted_iota(jnp.int32, (depth * capacity, total), 0)
    for hop in range(4):
        hit = jnp.where(routes[...] == (expert ^ hop).astype(jnp.float32), 1.0, 0.0)
        member = jnp.sum(hit, axis=0, keepdims=True)
        place_in = f32_dot(jnp.broadcast_to(member, (16, total)).astype(jnp.bfloat16), before)[0:1]
        target = jnp.where(member > 0.5, place_in.astype(jnp.int32) + first_slot, -1)
        placing = jnp.where(slot == target, 1.0, 0.0).astype(jnp.bfloat16)
        outs[hop][...] = f32_dot(placing, rows[...]).astype(jnp.bfloat16)


def expert_kernel(parts, *refs):
    row_refs, weights, outs = refs[:parts], refs[parts : parts + 6], refs[parts + 6 :]
    across = (((1,), (1,)), ((), ()))
    rows = jnp.concatenate([row_ref[...] for row_ref in row_refs], axis=0)
    result = None
    for w_gate, w_up, w_down in (weights[:3], weights[3:]):
        gate_part = lax.dot_general(rows, w_gate[...], across, preferred_element_type=jnp.float32)
        up_part = lax.dot_general(rows, w_up[...], across, preferred_element_type=jnp.float32)
        hidden = (gate_part / (1.0 + jnp.exp(-gate_part)) * up_part).astype(jnp.bfloat16)
        product = f32_dot(hidden, w_down[...])
        result = product if result is None else result + product
    count = row_refs[0].shape[0]
    for part, out in enumerate(outs):
        out[...] = result[part * count : (part + 1) * count].astype(jnp.bfloat16)


def combine_kernel(depth, capacity, place, routes, gates, *refs):
    returned, outs = refs[:4], refs[4 : 4 + depth]
    expert = place[4]
    total = routes.shape[0]
    tok_rows = total // depth
    later = lax.broadcasted_iota(jnp.int32, (total, total), 0)
    earlier = lax.broadcasted_iota(jnp.int32, (total, total), 1)
    before = ((earlier < later) & (earlier // tok_rows == later // tok_rows)).astype(jnp.bfloat16)
    first_slot = lax.broadcasted_iota(jnp.int32, (total, 1), 0) // tok_rows * capacity
    slot = lax.broadcasted_iota(jnp.int32, (total, depth * capacity), 1)
    mixed = jnp.zeros((total, returned[0].shape[1]), jnp.float32)
    for hop in range(4):
        hit = routes[...] == (expert ^ hop).astype(jnp.float32)
        member = jnp.sum(jnp.where(hit, 1.0, 0.0), axis=1, keepdims=True)
        factor = jnp.sum(jnp.where(hit, gates[...], 0.0), axis=1, keepdims=True)
        place_in = f32_dot(before, jnp.broadcast_to(member, (total, LANES)).astype(jnp.bfloat16))[:, 0:1]
        target = jnp.where(member > 0.5, place_in.astype(jnp.int32) + first_slot, -1)
        placing = jnp.where(slot == target, factor, 0.0)
        upper = placing.astype(jnp.bfloat16)
        lower = (placing - upper.astype(jnp.float32)).astype(jnp.bfloat16)
        mixed = mixed + f32_dot(upper, returned[hop][...]) + f32_dot(lower, returned[hop][...])
    for turn in range(depth):
        outs[turn][...] = mixed[turn * tok_rows : (turn + 1) * tok_rows].astype(jnp.bfloat16)


def shards(
    inputs,
    attn_gain,
    w_query,
    w_key,
    w_value,
    w_out,
    sel_blocks,
    ffn_gain,
    w_gate,
    w_up,
    w_down,
    routes,
    gate_weights,
):
    tok_rows, model_width = inputs.shape
    block_len, heads_here, pick_count = sel_blocks.shape
    hidden_cols = w_query.shape[1]
    head_dim = hidden_cols // heads_here
    ctx_count, exp_count = lax.axis_size("ctx"), lax.axis_size("exp")
    depth = ctx_count // 2
    ctx_index, exp_index = lax.axis_index("ctx"), lax.axis_index("exp")
    z_index, x_index = ctx_index // 2, ctx_index % 2
    expert = (ctx_index * exp_count + exp_index) // 2
    by_head = heads_here == depth and block_len <= 3 * head_dim and head_dim == LANES
    place = jnp.stack(
        [exp_index, z_index, exp_index % 2, z_index if by_head else jnp.zeros_like(z_index), expert]
    ).astype(jnp.int32)

    noted = gather_z(jnp.concatenate([routes.astype(jnp.float32), gate_weights], axis=1))
    top_count = routes.shape[1]

    weights = (w_gate, w_up, w_down)
    other_weights = tuple(swap_core(weight) for weight in weights)

    near = swap_core(inputs)
    far = move(inputs, lambda z, x, y, c: (z, x, y ^ 1, c))
    far, noted = lax.optimization_barrier((far, noted))
    far_near = swap_core(far)
    if by_head:
        marks = jnp.sum(
            jnp.where(sel_blocks < ctx_index, jnp.left_shift(1, jnp.minimum(sel_blocks, 30)), 0), axis=2
        )
        marks = jnp.pad(marks.T.astype(jnp.bfloat16), ((0, 0), (0, 3 * head_dim - block_len)))
        marks = jnp.broadcast_to(marks[:, None], (heads_here, PAD_ROWS, 3 * head_dim))
        payload = struct(block_len + PAD_ROWS, 3 * head_dim)
        sent = call(
            functools.partial(project_kernel, exp_count, depth, head_dim),
            [payload] * depth,
            [place, inputs, near, far, far_near, attn_gain.reshape(1, -1), w_query, w_key, w_value, marks],
            [
                pltpu.VMEM((block_len, model_width), jnp.bfloat16),
                pltpu.VMEM((3, block_len, hidden_cols), jnp.bfloat16),
            ],
            flops=6 * block_len * model_width * hidden_cols,
        )
        own = [head_out(sent[turn], turn) for turn in range(depth)]
        beside = [swap_core(block) for block in own]
        mixed = call(
            functools.partial(attend_kernel, depth, block_len, head_dim),
            [struct(block_len, head_dim)] * depth,
            [place, *own, *beside],
            [
                pltpu.VMEM((depth, block_len + PAD_ROWS, 3 * head_dim), jnp.bfloat16),
                pltpu.VMEM((depth, block_len, 2 * head_dim), jnp.bfloat16),
                pltpu.VMEM((depth, block_len, head_dim), jnp.bfloat16),
            ],
            flops=4 * depth * ctx_count * block_len * block_len * head_dim,
        )
        heads = [head_back(mixed[turn], turn) for turn in range(depth)]
    else:
        block = jnp.stack([inputs, near, far, far_near])[exp_index ^ jnp.arange(exp_count)]
        normed = normalize(block.reshape(block_len, model_width), attn_gain)
        heads = attend_gathered(normed, w_query, w_key, w_value, sel_blocks)

    heads, other_weights = lax.optimization_barrier((heads, other_weights))

    halves = struct(exp_count // 2, tok_rows, model_width)
    kept, given = call(
        functools.partial(mix_kernel, exp_count, heads_here, head_dim),
        [halves, halves],
        [place, *heads, w_out],
        [
            pltpu.VMEM((block_len, hidden_cols), jnp.bfloat16),
            pltpu.VMEM((block_len, model_width), jnp.bfloat16),
        ],
        flops=2 * block_len * model_width * hidden_cols,
    )
    given = swap_core(given)
    beyond = (kept[1].astype(jnp.float32) + given[1].astype(jnp.float32)).astype(jnp.bfloat16)
    beyond = move(beyond, lambda z, x, y, c: (z, x, y ^ 1, c))
    residual, ffn_in = call(
        residual_kernel,
        [struct(tok_rows, model_width)] * 2,
        [inputs, kept, given, beyond, ffn_gain.reshape(1, -1)],
        smem=0,
    )

    experts = ctx_count * exp_count // 2
    capacity = 2 * max(1, (tok_rows * top_count + experts - 1) // experts * 2 // 3)
    column = gather_z(ffn_in)
    nearest = sorted(range(depth), key=lambda turn: min(turn, depth - turn))
    group_size = depth // 2
    groups = [nearest[first : first + group_size] for first in range(0, depth, group_size)]
    notes = [jnp.concatenate([noted[turn] for turn in group], axis=0) for group in groups]
    slots = group_size * capacity
    expert_weights = [
        array
        for gate, up, down in (weights, other_weights)
        for array in (gate[0].T, up[0].T, down[0])
    ]
    arrived = []
    for group, note in zip(groups, notes):
        packed = call(
            functools.partial(pack_kernel, group_size, capacity),
            [struct(slots, model_width)] * 4,
            [place, note[:, :top_count].T, *[column[turn] for turn in group]],
            [pltpu.VMEM((group_size * tok_rows, model_width), jnp.bfloat16)],
            flops=8 * slots * group_size * tok_rows * model_width,
        )
        arrived.append([packed[0]] + [swap_layer(packed[hop], hop) for hop in range(1, 4)])
    sums = [None] * depth
    returned = []
    for rows in arrived:
        results = call(
            functools.partial(expert_kernel, 4),
            [struct(slots, model_width)] * 4,
            [*rows, *expert_weights],
            flops=48 * slots * model_width * w_gate.shape[2],
            smem=0,
        )
        returned.append([results[0]] + [swap_layer(results[hop], hop) for hop in range(1, 4)])
    for group, note, rows in zip(groups, notes, returned):
        parts = call(
            functools.partial(combine_kernel, group_size, capacity),
            [struct(tok_rows, model_width)] * group_size,
            [place, note[:, :top_count], note[:, top_count:], *rows],
            flops=16 * slots * group_size * tok_rows * model_width,
        )
        for turn, part in zip(group, parts):
            sums[turn] = part
    layer_out = residual.astype(jnp.float32) + sums[0].astype(jnp.float32)
    for part in scatter_z(sums):
        layer_out = layer_out + part.astype(jnp.float32)
    return layer_out.astype(jnp.bfloat16)


def solution(mesh):
    placed = (
        P(("ctx", "exp"), None),
        P(),
        P(None, "exp"),
        P(None, "exp"),
        P(None, "exp"),
        P("exp", None),
        P("ctx", "exp", None),
        P(),
        P(("ctx", "exp"), None, None),
        P(("ctx", "exp"), None, None),
        P(("ctx", "exp"), None, None),
        P(("ctx", "exp"), None),
        P(("ctx", "exp"), None),
    )
    return jax.shard_map(
        shards, mesh=mesh, in_specs=placed, out_specs=P(("ctx", "exp"), None), check_vma=False
    )
```

```python
import functools
import math

import jax
import jax.numpy as jnp
from jax import lax
from jax.experimental import pallas as pl
from jax.experimental.pallas import tpu as pltpu
from jax.sharding import PartitionSpec as P

AXES = ("ctx", "exp")
PARAMS = pltpu.CompilerParams(vmem_limit_bytes=20 * 1024 * 1024)
VMEM = pl.BlockSpec(memory_space=pltpu.VMEM)
SMEM = pl.BlockSpec(memory_space=pltpu.SMEM)
PAD_ROWS = 16
LANES = 128


def move(block, target):
    ctx_count, exp_count = lax.axis_size("ctx"), lax.axis_size("exp")
    route = []
    for ctx in range(ctx_count):
        for exp in range(exp_count):
            z, x, y, c = target(ctx // 2, ctx % 2, exp // 2, exp % 2)
            route.append((ctx * exp_count + exp, (z * 2 + x) * exp_count + y * 2 + c))
    return lax.ppermute(block, AXES, route)


def swap_core(block):
    return move(block, lambda z, x, y, c: (z, x, y, c ^ 1))


def swap_layer(block, hop):
    return move(block, lambda z, x, y, c: (z, x ^ (hop >> 1), y ^ (hop & 1), c))


def turn_z(block, turn):
    depth = lax.axis_size("ctx") // 2
    return move(block, lambda z, x, y, c: ((z + turn) % depth, x, y, c))


def gather_z(block):
    depth = lax.axis_size("ctx") // 2
    column = [block] + [None] * (depth - 1)
    for turn in range(1, depth // 2 + 1):
        column[turn] = turn_z(column[turn - 1], 1)
    for turn in range(depth - 1, depth // 2, -1):
        column[turn] = turn_z(column[(turn + 1) % depth], -1)
    return column


def head_out(block, turn):
    depth = lax.axis_size("ctx") // 2
    return move(block, lambda z, x, y, c: ((z + turn) % depth, c, y, x))


def head_back(block, turn):
    depth = lax.axis_size("ctx") // 2
    return move(block, lambda z, x, y, c: ((z - turn) % depth, c, y, x))


def normalize(values, gain_vec):
    floats = values.astype(jnp.float32)
    factor = lax.rsqrt(jnp.mean(floats * floats, axis=-1, keepdims=True) + 1e-06)
    return (floats * factor * gain_vec).astype(jnp.bfloat16)


def f32_dot(left, right):
    return jnp.dot(left, right, preferred_element_type=jnp.float32)


def struct(*shape, dtype=jnp.bfloat16):
    return pltpu.VMEM(shape, dtype)


def call(kernel, outs, operands, scratch=(), flops=0, smem=1):
    operands = operands[:smem] + [
        pltpu.with_memory_space_constraint(a, pltpu.VMEM) for a in operands[smem:]
    ]
    return pl.pallas_call(
        kernel,
        out_shape=outs,
        in_specs=[SMEM] * smem + [VMEM] * (len(operands) - smem),
        out_specs=jax.tree.map(lambda _: VMEM, outs),
        scratch_shapes=list(scratch),
        compiler_params=PARAMS,
        cost_estimate=pl.CostEstimate(
            flops=flops,
            bytes_accessed=sum(a.size * a.dtype.itemsize for a in operands),
            transcendentals=0,
        ),
    )(*operands)


def after(value, *others):
    return lax.optimization_barrier((value, *others))[0]


def load_kernel(count, *refs):
    sources, targets, sems = refs[:count], refs[count : 2 * count], refs[2 * count]
    copies = [
        pltpu.make_async_copy(sources[i], targets[i], sems.at[i]) for i in range(count)
    ]
    for copy in copies:
        copy.start()
    for copy in copies:
        copy.wait()


def load(arrays):
    count = len(arrays)
    return pl.pallas_call(
        functools.partial(load_kernel, count),
        out_shape=[struct(*a.shape) for a in arrays],
        in_specs=[pl.BlockSpec(memory_space=pltpu.HBM)] * count,
        out_specs=[VMEM] * count,
        scratch_shapes=[pltpu.SemaphoreType.DMA((count,))],
        compiler_params=PARAMS,
        cost_estimate=pl.CostEstimate(
            flops=0, bytes_accessed=sum(2 * a.size * 2 for a in arrays), transcendentals=0
        ),
    )(*[pltpu.with_memory_space_constraint(a, pltpu.HBM) for a in arrays])


def project_kernel(hops, depth, head_dim, place, *refs):
    row_refs, (gain, w_query, w_key, w_value, marks) = refs[:hops], refs[hops : hops + 5]
    outs, (rows, mixed) = refs[hops + 5 : hops + 5 + depth], refs[hops + 5 + depth :]
    exp_index, z_index = place[0], place[1]
    tok_rows = row_refs[0].shape[0]
    block_len = hops * tok_rows
    for hop, row_ref in enumerate(row_refs):
        start = pl.multiple_of((exp_index ^ hop) * tok_rows, 16)
        rows[pl.ds(start, tok_rows), :] = normalize(row_ref[...], gain[...])
    for part, weight in enumerate((w_query, w_key, w_value)):
        mixed[part] = f32_dot(rows[...], weight[...]).astype(jnp.bfloat16)
    for turn in range(depth):
        head = lax.rem(z_index + turn, depth)
        columns = pl.ds(pl.multiple_of(head * head_dim, head_dim), head_dim)
        for part in range(3):
            outs[turn][0:block_len, part * head_dim : (part + 1) * head_dim] = mixed[part, :, columns]
        outs[turn][block_len : block_len + PAD_ROWS, :] = marks[head]


def attend_kernel(depth, block_len, head_dim, place, *refs):
    own_refs, near_refs = refs[:depth], refs[depth : 2 * depth]
    outs, (own, near, mixed) = refs[2 * depth : 3 * depth], refs[3 * depth :]
    z_index, core = place[1], place[2]
    scaling = 1.0 / math.sqrt(head_dim)
    for turn in range(depth):
        source = lax.rem(z_index + depth - turn, depth)
        own[source] = own_refs[turn][...]
        near[source] = near_refs[turn][0:block_len, head_dim : 3 * head_dim]
    key_pos = lax.broadcasted_iota(jnp.int32, (block_len, block_len), 0)
    query_pos = lax.broadcasted_iota(jnp.int32, (block_len, block_len), 1)
    causal = jnp.where(key_pos <= query_pos, 0.0, -1e30)
    for level in range(depth):
        query = own[level, 0:block_len, 0:head_dim]
        marks = own[level, block_len : block_len + PAD_ROWS, 0:block_len].astype(jnp.float32)
        marks = marks[0:1].astype(jnp.int32)
        run_max = run_sum = total = None
        order = [(level, True)] + [(c, True) for c in range(level)] + [(c, False) for c in range(level + 1)]
        for c, mine in order:
            if mine:
                key = own[c, 0:block_len, head_dim : 2 * head_dim]
                value = own[c, 0:block_len, 2 * head_dim : 3 * head_dim]
            else:
                key, value = near[c, :, 0:head_dim], near[c, :, head_dim : 2 * head_dim]
            scores = scaling * lax.dot_general(
                key, query, (((1,), (1,)), ((), ())), preferred_element_type=jnp.float32
            )
            if mine and c == level:
                scores = scores + causal
            else:
                bit = 2 * c + (core if mine else 1 - core)
                chosen = lax.shift_right_logical(marks, jnp.broadcast_to(bit, marks.shape)) & 1
                scores = jnp.where(chosen == 1, scores, -1e30)
            top = jnp.max(scores, axis=0, keepdims=True)
            new_max = top if run_max is None else jnp.maximum(run_max, top)
            weights = jnp.exp(scores - new_max)
            added = jnp.sum(weights, axis=0, keepdims=True)
            product = lax.dot_general(
                value,
                weights.astype(jnp.bfloat16),
                (((0,), (0,)), ((), ())),
                preferred_element_type=jnp.float32,
            )
            if run_max is None:
                run_sum, total = added, product
            else:
                rescale = jnp.exp(run_max - new_max)
                run_sum, total = run_sum * rescale + added, total * rescale + product
            run_max = new_max
        mixed[level] = (total / run_sum).T.astype(jnp.bfloat16)
    for turn in range(depth):
        outs[turn][...] = mixed[lax.rem(z_index + depth - turn, depth)]


def attend_gathered(normed_block, w_query, w_key, w_value, sel_blocks):
    block_len, heads_here, _ = sel_blocks.shape
    hidden_cols = w_query.shape[1]
    head_dim = hidden_cols // heads_here
    ctx_count, ctx_index = lax.axis_size("ctx"), lax.axis_index("ctx")
    query_part, key_part, value_part = (
        f32_dot(normed_block, weight).astype(jnp.bfloat16) for weight in (w_query, w_key, w_value)
    )
    queries = query_part.reshape(block_len, heads_here, head_dim)
    keys_values = jnp.stack([key_part, value_part], axis=1)
    block_ids = jnp.arange(ctx_count, dtype=jnp.int32)
    chosen = jnp.any(sel_blocks[:, :, :, None] == block_ids, axis=2) & (block_ids < ctx_index)
    position = jnp.arange(block_len, dtype=jnp.int32)
    causal = position[None, :] <= position[:, None]
    scaling = 1.0 / math.sqrt(head_dim)

    def fold_step(running, operands):
        run_max, run_sum, totals = running
        piece, block = operands
        key_rows = piece[:, 0].reshape(block_len, heads_here, head_dim)
        value_rows = piece[:, 1].reshape(block_len, heads_here, head_dim)
        scores = (
            jnp.einsum("qhd,khd->hqk", queries, key_rows, preferred_element_type=jnp.float32)
            * scaling
        )
        picked = jnp.take(chosen, block, axis=2).T[:, :, None]
        allowed = picked | ((block == ctx_index) & causal)[None]
        new_max = jnp.maximum(run_max, jnp.max(jnp.where(allowed, scores, -jnp.inf), axis=-1))
        weights = jnp.where(allowed, jnp.exp(scores - new_max[..., None]), 0.0)
        rescale = jnp.exp(run_max - new_max)
        run_sum = run_sum * rescale + jnp.sum(weights, axis=-1)
        totals = totals * rescale[..., None] + jnp.einsum(
            "hqk,khd->hqd",
            weights.astype(jnp.bfloat16),
            value_rows,
            preferred_element_type=jnp.float32,
        )
        return (new_max, run_sum, totals), None

    initial = (
        jnp.full((heads_here, block_len), -1e30, jnp.float32),
        jnp.zeros((heads_here, block_len), jnp.float32),
        jnp.zeros((heads_here, block_len, head_dim), jnp.float32),
    )
    gathered = lax.all_gather(keys_values, "ctx", axis=0)
    (_, run_sum, totals), _ = lax.scan(fold_step, initial, (gathered, block_ids))
    attended = (totals / run_sum[..., None]).astype(jnp.bfloat16)
    return [attended[head] for head in range(heads_here)]


def mix_kernel(hops, heads, head_dim, place, *refs):
    head_refs, w_out = refs[:heads], refs[heads]
    kept, given, attended, mixed = refs[heads + 1 :]
    exp_index, turned = place[0], place[3]
    tok_rows = kept.shape[1]
    for turn, head_ref in enumerate(head_refs):
        head = lax.rem(turned + turn, heads)
        attended[:, pl.ds(pl.multiple_of(head * head_dim, head_dim), head_dim)] = head_ref[...]
    mixed[...] = f32_dot(attended[...], w_out[...]).astype(jnp.bfloat16)
    for hop in range(hops):
        start = pl.multiple_of((exp_index ^ hop) * tok_rows, 16)
        (given if hop & 1 else kept)[hop >> 1] = mixed[pl.ds(start, tok_rows), :]


def residual_kernel(inputs, kept, given, far, gain, residual, ffn_in):
    summed = kept[0].astype(jnp.float32) + given[0].astype(jnp.float32) + far[...].astype(jnp.float32)
    rounded = (inputs[...].astype(jnp.float32) + summed).astype(jnp.bfloat16)
    residual[...] = rounded
    ffn_in[...] = normalize(rounded, gain[...])


def pack_kernel(depth, capacity, place, routes, *refs):
    sources, outs, (rows,) = refs[:depth], refs[depth : depth + 4], refs[depth + 4 :]
    expert = place[4]
    tok_rows = sources[0].shape[0]
    total = depth * tok_rows
    for turn in range(depth):
        rows[turn * tok_rows : (turn + 1) * tok_rows, :] = sources[turn][...]
    earlier = lax.broadcasted_iota(jnp.int32, (total, total), 0)
    later = lax.broadcasted_iota(jnp.int32, (total, total), 1)
    before = ((earlier < later) & (earlier // tok_rows == later // tok_rows)).astype(jnp.bfloat16)
    first_slot = lax.broadcasted_iota(jnp.int32, (1, total), 1) // tok_rows * capacity
    slot = lax.broadcasted_iota(jnp.int32, (depth * capacity, total), 0)
    for hop in range(4):
        hit = jnp.where(routes[...] == (expert ^ hop).astype(jnp.float32), 1.0, 0.0)
        member = jnp.sum(hit, axis=0, keepdims=True)
        place_in = f32_dot(jnp.broadcast_to(member, (16, total)).astype(jnp.bfloat16), before)[0:1]
        target = jnp.where(member > 0.5, place_in.astype(jnp.int32) + first_slot, -1)
        placing = jnp.where(slot == target, 1.0, 0.0).astype(jnp.bfloat16)
        outs[hop][...] = f32_dot(placing, rows[...]).astype(jnp.bfloat16)


def expert_kernel(parts, *refs):
    row_refs, weights, outs = refs[:parts], refs[parts : parts + 6], refs[parts + 6 :]
    across = (((1,), (1,)), ((), ()))
    rows = jnp.concatenate([row_ref[...] for row_ref in row_refs], axis=0)
    result = None
    for w_gate, w_up, w_down in (weights[:3], weights[3:]):
        gate_part = lax.dot_general(rows, w_gate[...], across, preferred_element_type=jnp.float32)
        up_part = lax.dot_general(rows, w_up[...], across, preferred_element_type=jnp.float32)
        hidden = (gate_part / (1.0 + jnp.exp(-gate_part)) * up_part).astype(jnp.bfloat16)
        product = f32_dot(hidden, w_down[...])
        result = product if result is None else result + product
    count = row_refs[0].shape[0]
    for part, out in enumerate(outs):
        out[...] = result[part * count : (part + 1) * count].astype(jnp.bfloat16)


def combine_kernel(depth, capacity, place, routes, gates, *refs):
    returned, outs = refs[:4], refs[4 : 4 + depth]
    expert = place[4]
    total = routes.shape[0]
    tok_rows = total // depth
    later = lax.broadcasted_iota(jnp.int32, (total, total), 0)
    earlier = lax.broadcasted_iota(jnp.int32, (total, total), 1)
    before = ((earlier < later) & (earlier // tok_rows == later // tok_rows)).astype(jnp.bfloat16)
    first_slot = lax.broadcasted_iota(jnp.int32, (total, 1), 0) // tok_rows * capacity
    slot = lax.broadcasted_iota(jnp.int32, (total, depth * capacity), 1)
    mixed = jnp.zeros((total, returned[0].shape[1]), jnp.float32)
    for hop in range(4):
        hit = routes[...] == (expert ^ hop).astype(jnp.float32)
        member = jnp.sum(jnp.where(hit, 1.0, 0.0), axis=1, keepdims=True)
        factor = jnp.sum(jnp.where(hit, gates[...], 0.0), axis=1, keepdims=True)
        place_in = f32_dot(before, jnp.broadcast_to(member, (total, LANES)).astype(jnp.bfloat16))[:, 0:1]
        target = jnp.where(member > 0.5, place_in.astype(jnp.int32) + first_slot, -1)
        placing = jnp.where(slot == target, factor, 0.0)
        upper = placing.astype(jnp.bfloat16)
        lower = (placing - upper.astype(jnp.float32)).astype(jnp.bfloat16)
        mixed = mixed + f32_dot(upper, returned[hop][...]) + f32_dot(lower, returned[hop][...])
    for turn in range(depth):
        outs[turn][...] = mixed[turn * tok_rows : (turn + 1) * tok_rows].astype(jnp.bfloat16)


def shards(
    inputs,
    attn_gain,
    w_query,
    w_key,
    w_value,
    w_out,
    sel_blocks,
    ffn_gain,
    w_gate,
    w_up,
    w_down,
    routes,
    gate_weights,
):
    tok_rows, model_width = inputs.shape
    block_len, heads_here, pick_count = sel_blocks.shape
    hidden_cols = w_query.shape[1]
    head_dim = hidden_cols // heads_here
    ctx_count, exp_count = lax.axis_size("ctx"), lax.axis_size("exp")
    depth = ctx_count // 2
    ctx_index, exp_index = lax.axis_index("ctx"), lax.axis_index("exp")
    z_index, x_index = ctx_index // 2, ctx_index % 2
    expert = (ctx_index * exp_count + exp_index) // 2
    by_head = heads_here == depth and block_len <= 3 * head_dim and head_dim == LANES
    place = jnp.stack(
        [exp_index, z_index, exp_index % 2, z_index if by_head else jnp.zeros_like(z_index), expert]
    ).astype(jnp.int32)

    far = move(inputs, lambda z, x, y, c: (z, x, y ^ 1, c))
    near = swap_core(inputs)
    near, far, w_query, w_key, w_value, w_out = lax.optimization_barrier(
        (near, far, *load([w_query, w_key, w_value, w_out]))
    )
    far_near = swap_core(far)
    top_count = routes.shape[1]
    noted = jnp.concatenate([routes.astype(jnp.float32), gate_weights], axis=1)
    weights = (w_gate, w_up, w_down)
    if by_head:
        marks = jnp.sum(
            jnp.where(sel_blocks < ctx_index, jnp.left_shift(1, jnp.minimum(sel_blocks, 30)), 0), axis=2
        )
        marks = jnp.pad(marks.T.astype(jnp.bfloat16), ((0, 0), (0, 3 * head_dim - block_len)))
        marks = jnp.broadcast_to(marks[:, None], (heads_here, PAD_ROWS, 3 * head_dim))
        payload = struct(block_len + PAD_ROWS, 3 * head_dim)
        sent = call(
            functools.partial(project_kernel, exp_count, depth, head_dim),
            [payload] * depth,
            [place, inputs, near, far, far_near, attn_gain.reshape(1, -1), w_query, w_key, w_value, marks],
            [
                pltpu.VMEM((block_len, model_width), jnp.bfloat16),
                pltpu.VMEM((3, block_len, hidden_cols), jnp.bfloat16),
            ],
            flops=6 * block_len * model_width * hidden_cols,
        )
        own = [head_out(sent[turn], turn) for turn in range(depth)]
        noted = after(noted, sent[0])
        noted = [noted] + [turn_z(noted, turn) for turn in range(1, depth)]
        own[-1], noted = lax.optimization_barrier((own[-1], noted))
        beside = [swap_core(block) for block in own]
        other_weights = [swap_core(after(weight, *beside)) for weight in weights]
        mixed = call(
            functools.partial(attend_kernel, depth, block_len, head_dim),
            [struct(block_len, head_dim)] * depth,
            [place, *own, *beside],
            [
                pltpu.VMEM((depth, block_len + PAD_ROWS, 3 * head_dim), jnp.bfloat16),
                pltpu.VMEM((depth, block_len, 2 * head_dim), jnp.bfloat16),
                pltpu.VMEM((depth, block_len, head_dim), jnp.bfloat16),
            ],
            flops=4 * depth * ctx_count * block_len * block_len * head_dim,
        )
        heads = [head_back(mixed[turn], turn) for turn in range(depth)]
    else:
        block = jnp.stack([inputs, near, far, far_near])[exp_index ^ jnp.arange(exp_count)]
        normed = normalize(block.reshape(block_len, model_width), attn_gain)
        heads = attend_gathered(normed, w_query, w_key, w_value, sel_blocks)
        noted = [noted] + [turn_z(noted, turn) for turn in range(1, depth)]
        other_weights = [swap_core(weight) for weight in weights]

    halves = struct(exp_count // 2, tok_rows, model_width)
    kept, given = call(
        functools.partial(mix_kernel, exp_count, heads_here, head_dim),
        [halves, halves],
        [place, *heads, w_out],
        [
            pltpu.VMEM((block_len, hidden_cols), jnp.bfloat16),
            pltpu.VMEM((block_len, model_width), jnp.bfloat16),
        ],
        flops=2 * block_len * model_width * hidden_cols,
    )
    given = swap_core(given)
    beyond = (kept[1].astype(jnp.float32) + given[1].astype(jnp.float32)).astype(jnp.bfloat16)
    own_weights, other_weights = (
        [gate[0].T, up[0].T, down[0]] for gate, up, down in (weights, other_weights)
    )
    expert_weights = [*load([after(weight, beyond) for weight in own_weights]), *other_weights]
    beyond = move(beyond, lambda z, x, y, c: (z, x, y ^ 1, c))
    beyond, expert_weights = lax.optimization_barrier((beyond, expert_weights))
    residual, ffn_in = call(
        residual_kernel,
        [struct(tok_rows, model_width)] * 2,
        [inputs, kept, given, beyond, ffn_gain.reshape(1, -1)],
        smem=0,
    )

    experts = ctx_count * exp_count // 2
    capacity = 2 * max(1, (tok_rows * top_count + experts - 1) // experts * 2 // 3)
    column = gather_z(ffn_in)
    nearest = sorted(range(depth), key=lambda turn: min(turn, depth - turn))
    group_size = depth // 2
    groups = [nearest[first : first + group_size] for first in range(0, depth, group_size)]
    notes = [jnp.concatenate([noted[turn] for turn in group], axis=0) for group in groups]
    slots = group_size * capacity
    arrived = []
    for group, note in zip(groups, notes):
        if arrived:
            note = after(note, arrived[-1][0])
        packed = call(
            functools.partial(pack_kernel, group_size, capacity),
            [struct(slots, model_width)] * 4,
            [place, note[:, :top_count].T, *[column[turn] for turn in group]],
            [pltpu.VMEM((group_size * tok_rows, model_width), jnp.bfloat16)],
            flops=8 * slots * group_size * tok_rows * model_width,
        )
        arrived.append([packed[0]] + [swap_layer(packed[hop], hop) for hop in range(1, 4)])
    sums = [None] * depth
    returned = []
    for rows in arrived:
        if returned:
            rows = [after(rows[0], returned[-1][0])] + rows[1:]
        results = call(
            functools.partial(expert_kernel, 4),
            [struct(slots, model_width)] * 4,
            [*rows, *expert_weights],
            flops=48 * slots * model_width * w_gate.shape[2],
            smem=0,
        )
        returned.append([results[0]] + [swap_layer(results[hop], hop) for hop in range(1, 4)])
    for group, note, rows in zip(groups, notes, returned):
        parts = call(
            functools.partial(combine_kernel, group_size, capacity),
            [struct(tok_rows, model_width)] * group_size,
            [place, note[:, :top_count], note[:, top_count:], *rows],
            flops=16 * slots * group_size * tok_rows * model_width,
        )
        for turn, part in zip(group, parts):
            sums[turn] = part
    layer_out = residual.astype(jnp.float32) + sums[0].astype(jnp.float32)
    for turn in range(1, depth):
        layer_out = layer_out + turn_z(sums[turn], -turn).astype(jnp.float32)
    return layer_out.astype(jnp.bfloat16)


def solution(mesh):
    placed = (
        P(("ctx", "exp"), None),
        P(),
        P(None, "exp"),
        P(None, "exp"),
        P(None, "exp"),
        P("exp", None),
        P("ctx", "exp", None),
        P(),
        P(("ctx", "exp"), None, None),
        P(("ctx", "exp"), None, None),
        P(("ctx", "exp"), None, None),
        P(("ctx", "exp"), None),
        P(("ctx", "exp"), None),
    )
    return jax.shard_map(
        shards, mesh=mesh, in_specs=placed, out_specs=P(("ctx", "exp"), None), check_vma=False
    )
```

```python
import functools
import math

import jax
import jax.numpy as jnp
from jax import lax
from jax.experimental import pallas as pl
from jax.experimental.pallas import tpu as pltpu
from jax.sharding import PartitionSpec as P

AXES = ("ctx", "exp")
MIB = 1024 * 1024
VMEM = pl.BlockSpec(memory_space=pltpu.VMEM)
SMEM = pl.BlockSpec(memory_space=pltpu.SMEM)
HBM = pl.BlockSpec(memory_space=pltpu.HBM)
PAD_ROWS = 16
LANES = 128


def move(block, target):
    ctx_count, exp_count = lax.axis_size("ctx"), lax.axis_size("exp")
    route = []
    for ctx in range(ctx_count):
        for exp in range(exp_count):
            z, x, y, c = target(ctx // 2, ctx % 2, exp // 2, exp % 2)
            route.append((ctx * exp_count + exp, (z * 2 + x) * exp_count + y * 2 + c))
    return lax.ppermute(block, AXES, route)


def swap_core(block):
    return move(block, lambda z, x, y, c: (z, x, y, c ^ 1))


def swap_layer(block, hop):
    return move(block, lambda z, x, y, c: (z, x ^ (hop >> 1), y ^ (hop & 1), c))


def turn_z(block, turn):
    depth = lax.axis_size("ctx") // 2
    return move(block, lambda z, x, y, c: ((z + turn) % depth, x, y, c))


def gather_z(block):
    depth = lax.axis_size("ctx") // 2
    column = [block] + [None] * (depth - 1)
    for turn in range(1, depth // 2 + 1):
        column[turn] = turn_z(column[turn - 1], 1)
    for turn in range(depth - 1, depth // 2, -1):
        column[turn] = turn_z(column[(turn + 1) % depth], -1)
    return column


def head_out(block, turn):
    depth = lax.axis_size("ctx") // 2
    return move(block, lambda z, x, y, c: ((z + turn) % depth, c, y, x))


def head_back(block, turn):
    depth = lax.axis_size("ctx") // 2
    return move(block, lambda z, x, y, c: ((z - turn) % depth, c, y, x))


def normalize(values, gain_vec):
    floats = values.astype(jnp.float32)
    factor = lax.rsqrt(jnp.mean(floats * floats, axis=-1, keepdims=True) + 1e-06)
    return (floats * factor * gain_vec).astype(jnp.bfloat16)


def f32_dot(left, right):
    return jnp.dot(left, right, preferred_element_type=jnp.float32)


def struct(*shape, dtype=jnp.bfloat16):
    return pltpu.VMEM(shape, dtype)


def call(kernel, outs, operands, scratch=(), flops=0, smem=1, hbm=0, limit=16 * MIB):
    last = len(operands) - hbm
    operands = [
        a if i < smem else pltpu.with_memory_space_constraint(a, pltpu.VMEM if i < last else pltpu.HBM)
        for i, a in enumerate(operands)
    ]
    return pl.pallas_call(
        kernel,
        out_shape=outs,
        in_specs=[SMEM] * smem + [VMEM] * (last - smem) + [HBM] * hbm,
        out_specs=jax.tree.map(lambda _: VMEM, outs),
        scratch_shapes=list(scratch),
        compiler_params=pltpu.CompilerParams(vmem_limit_bytes=limit),
        cost_estimate=pl.CostEstimate(
            flops=flops,
            bytes_accessed=sum(a.size * a.dtype.itemsize for a in operands),
            transcendentals=0,
        ),
    )(*operands)


def after(value, *others):
    return lax.optimization_barrier((value, *others))[0]


def load_kernel(count, *refs):
    sources, targets, sems = refs[:count], refs[count : 2 * count], refs[2 * count]
    copies = [
        pltpu.make_async_copy(sources[i], targets[i], sems.at[i]) for i in range(count)
    ]
    for copy in copies:
        copy.start()
    for copy in copies:
        copy.wait()


def load(arrays):
    return call(
        functools.partial(load_kernel, len(arrays)),
        [struct(*a.shape) for a in arrays],
        arrays,
        [pltpu.SemaphoreType.DMA((len(arrays),))],
        smem=0,
        hbm=len(arrays),
        limit=MIB,
    )


def project_kernel(hops, depth, head_dim, place, *refs):
    row_refs, (gain, marks), weights = refs[:hops], refs[hops : hops + 2], refs[hops + 2 : hops + 5]
    outs, (rows, mixed, held, sems) = refs[hops + 5 : hops + 5 + depth], refs[hops + 5 + depth :]
    exp_index, z_index = place[0], place[1]
    tok_rows = row_refs[0].shape[0]
    block_len = hops * tok_rows
    copies = [pltpu.make_async_copy(weights[i], held.at[i], sems.at[i]) for i in range(3)]
    for copy in copies:
        copy.start()
    for hop, row_ref in enumerate(row_refs):
        start = pl.multiple_of((exp_index ^ hop) * tok_rows, 16)
        rows[pl.ds(start, tok_rows), :] = normalize(row_ref[...], gain[...])
    for part, copy in enumerate(copies):
        copy.wait()
        mixed[part] = f32_dot(rows[...], held[part]).astype(jnp.bfloat16)
    for turn in range(depth):
        head = lax.rem(z_index + turn, depth)
        columns = pl.ds(pl.multiple_of(head * head_dim, head_dim), head_dim)
        for part in range(3):
            outs[turn][0:block_len, part * head_dim : (part + 1) * head_dim] = mixed[part, :, columns]
        outs[turn][block_len : block_len + PAD_ROWS, :] = marks[head]


def attend_kernel(depth, block_len, head_dim, place, *refs):
    own_refs, near_refs = refs[:depth], refs[depth : 2 * depth]
    outs, (own, near, mixed) = refs[2 * depth : 3 * depth], refs[3 * depth :]
    z_index, core = place[1], place[2]
    scaling = math.log2(math.e) / math.sqrt(head_dim)
    for turn in range(depth):
        source = lax.rem(z_index + depth - turn, depth)
        own[source] = own_refs[turn][...]
        near[source] = near_refs[turn][0:block_len, head_dim : 3 * head_dim]
    key_pos = lax.broadcasted_iota(jnp.int32, (block_len, block_len), 0)
    query_pos = lax.broadcasted_iota(jnp.int32, (block_len, block_len), 1)
    causal = jnp.where(key_pos <= query_pos, 0.0, -1e30)
    for level in range(depth):
        query = own[level, 0:block_len, 0:head_dim]
        marks = own[level, block_len : block_len + PAD_ROWS, 0:block_len].astype(jnp.float32)
        marks = marks[0:1].astype(jnp.int32)
        run_max = run_sum = total = None
        order = [(level, True)] + [(c, True) for c in range(level)] + [(c, False) for c in range(level + 1)]
        for c, mine in order:
            if mine:
                key = own[c, 0:block_len, head_dim : 2 * head_dim]
                value = own[c, 0:block_len, 2 * head_dim : 3 * head_dim]
            else:
                key, value = near[c, :, 0:head_dim], near[c, :, head_dim : 2 * head_dim]
            scores = lax.dot_general(
                key, query, (((1,), (1,)), ((), ())), preferred_element_type=jnp.float32
            )
            if run_max is None:
                scores = scores + causal
                shift = run_max = jnp.max(scores, axis=0, keepdims=True)
            else:
                bit = 2 * c + (core if mine else 1 - core)
                chosen = lax.shift_right_logical(marks, jnp.broadcast_to(bit, marks.shape)) & 1
                top = jnp.where(chosen == 1, jnp.max(scores, axis=0, keepdims=True), -1e30)
                new_max = jnp.maximum(run_max, top)
                rescale = jnp.exp2((run_max - new_max) * scaling)
                run_max = new_max
                shift = jnp.where(chosen == 1, new_max, 1e30)
            weights = jnp.exp2((scores - shift) * scaling)
            added = jnp.sum(weights, axis=0, keepdims=True)
            product = lax.dot_general(
                value,
                weights.astype(jnp.bfloat16),
                (((0,), (0,)), ((), ())),
                preferred_element_type=jnp.float32,
            )
            if total is None:
                run_sum, total = added, product
            else:
                run_sum, total = run_sum * rescale + added, total * rescale + product
        mixed[level] = (total / run_sum).T.astype(jnp.bfloat16)
    for turn in range(depth):
        outs[turn][...] = mixed[lax.rem(z_index + depth - turn, depth)]


def attend_gathered(normed_block, w_query, w_key, w_value, sel_blocks):
    block_len, heads_here, _ = sel_blocks.shape
    hidden_cols = w_query.shape[1]
    head_dim = hidden_cols // heads_here
    ctx_count, ctx_index = lax.axis_size("ctx"), lax.axis_index("ctx")
    query_part, key_part, value_part = (
        f32_dot(normed_block, weight).astype(jnp.bfloat16) for weight in (w_query, w_key, w_value)
    )
    queries = query_part.reshape(block_len, heads_here, head_dim)
    keys_values = jnp.stack([key_part, value_part], axis=1)
    block_ids = jnp.arange(ctx_count, dtype=jnp.int32)
    chosen = jnp.any(sel_blocks[:, :, :, None] == block_ids, axis=2) & (block_ids < ctx_index)
    position = jnp.arange(block_len, dtype=jnp.int32)
    causal = position[None, :] <= position[:, None]
    scaling = 1.0 / math.sqrt(head_dim)

    def fold_step(running, operands):
        run_max, run_sum, totals = running
        piece, block = operands
        key_rows = piece[:, 0].reshape(block_len, heads_here, head_dim)
        value_rows = piece[:, 1].reshape(block_len, heads_here, head_dim)
        scores = (
            jnp.einsum("qhd,khd->hqk", queries, key_rows, preferred_element_type=jnp.float32)
            * scaling
        )
        picked = jnp.take(chosen, block, axis=2).T[:, :, None]
        allowed = picked | ((block == ctx_index) & causal)[None]
        new_max = jnp.maximum(run_max, jnp.max(jnp.where(allowed, scores, -jnp.inf), axis=-1))
        weights = jnp.where(allowed, jnp.exp(scores - new_max[..., None]), 0.0)
        rescale = jnp.exp(run_max - new_max)
        run_sum = run_sum * rescale + jnp.sum(weights, axis=-1)
        totals = totals * rescale[..., None] + jnp.einsum(
            "hqk,khd->hqd",
            weights.astype(jnp.bfloat16),
            value_rows,
            preferred_element_type=jnp.float32,
        )
        return (new_max, run_sum, totals), None

    initial = (
        jnp.full((heads_here, block_len), -1e30, jnp.float32),
        jnp.zeros((heads_here, block_len), jnp.float32),
        jnp.zeros((heads_here, block_len, head_dim), jnp.float32),
    )
    gathered = lax.all_gather(keys_values, "ctx", axis=0)
    (_, run_sum, totals), _ = lax.scan(fold_step, initial, (gathered, block_ids))
    attended = (totals / run_sum[..., None]).astype(jnp.bfloat16)
    return [attended[head] for head in range(heads_here)]


def mix_kernel(hops, heads, head_dim, place, *refs):
    head_refs, w_out = refs[:heads], refs[heads]
    kept, given, attended, mixed = refs[heads + 1 :]
    exp_index, turned = place[0], place[3]
    tok_rows = kept.shape[1]
    for turn, head_ref in enumerate(head_refs):
        head = lax.rem(turned + turn, heads)
        attended[:, pl.ds(pl.multiple_of(head * head_dim, head_dim), head_dim)] = head_ref[...]
    mixed[...] = f32_dot(attended[...], w_out[...]).astype(jnp.bfloat16)
    for hop in range(hops):
        start = pl.multiple_of((exp_index ^ hop) * tok_rows, 16)
        (given if hop & 1 else kept)[hop >> 1] = mixed[pl.ds(start, tok_rows), :]


def residual_kernel(top_count, inputs, kept, given, far, gain, noted, residual, ffn_in):
    summed = kept[0].astype(jnp.float32) + given[0].astype(jnp.float32) + far[...].astype(jnp.float32)
    rounded = (inputs[...].astype(jnp.float32) + summed).astype(jnp.bfloat16)
    residual[...] = rounded
    model_width = rounded.shape[1]
    ffn_in[:, 0:model_width] = normalize(rounded, gain[...])
    lane = lax.broadcasted_iota(jnp.int32, noted.shape, 1)
    left = noted[...]
    upper = left.astype(jnp.bfloat16).astype(jnp.float32)
    left = left - upper
    middle = left.astype(jnp.bfloat16).astype(jnp.float32)
    lower = left - middle
    parts = jnp.where(lane < 2 * top_count, upper, jnp.where(lane < 3 * top_count, middle, lower))
    ffn_in[:, model_width:] = parts.astype(jnp.bfloat16)


def pack_kernel(count, capacity, top_count, place, *refs):
    sources, outs, (notes, rows) = refs[:count], refs[count : count + 4], refs[count + 4 :]
    expert = place[4]
    tok_rows = sources[0].shape[0]
    total = count * tok_rows
    model_width = rows.shape[1]
    for turn in range(count):
        part = slice(turn * tok_rows, (turn + 1) * tok_rows)
        rows[part, :] = sources[turn][:, 0:model_width]
        notes[part, :] = sources[turn][:, model_width:]
    routes = notes[...].astype(jnp.float32).T[0:8]
    routes = jnp.where(lax.broadcasted_iota(jnp.int32, routes.shape, 0) < top_count, routes, -1.0)
    earlier = lax.broadcasted_iota(jnp.int32, (total, total), 0)
    later = lax.broadcasted_iota(jnp.int32, (total, total), 1)
    before = ((earlier < later) & (earlier // tok_rows == later // tok_rows)).astype(jnp.bfloat16)
    first_slot = lax.broadcasted_iota(jnp.int32, (1, total), 1) // tok_rows * capacity
    slot = lax.broadcasted_iota(jnp.int32, (count * capacity, total), 0)
    for hop in range(4):
        hit = jnp.where(routes == (expert ^ hop).astype(jnp.float32), 1.0, 0.0)
        member = jnp.sum(hit, axis=0, keepdims=True)
        place_in = f32_dot(jnp.broadcast_to(member, (16, total)).astype(jnp.bfloat16), before)[0:1]
        target = jnp.where(member > 0.5, place_in.astype(jnp.int32) + first_slot, -1)
        placing = jnp.where(slot == target, 1.0, 0.0).astype(jnp.bfloat16)
        outs[hop][...] = f32_dot(placing, rows[...]).astype(jnp.bfloat16)


def expert_kernel(parts, stride, *refs):
    row_refs, weights = refs[:parts], refs[parts : parts + 6]
    outs, (held,) = refs[parts + 6 : 2 * parts + 6], refs[2 * parts + 6 :]
    across = (((1,), (1,)), ((), ()))
    count = row_refs[0].shape[0]
    for part, row_ref in enumerate(row_refs):
        held[part * stride : part * stride + count, :] = row_ref[...]
    rows = held[...]
    result = None
    for w_gate, w_up, w_down in (weights[:3], weights[3:]):
        gate_part = lax.dot_general(rows, w_gate[...], across, preferred_element_type=jnp.float32)
        up_part = lax.dot_general(rows, w_up[...], across, preferred_element_type=jnp.float32)
        hidden = (gate_part / (1.0 + jnp.exp(-gate_part)) * up_part).astype(jnp.bfloat16)
        product = f32_dot(hidden, w_down[...])
        result = product if result is None else result + product
    for part, out in enumerate(outs):
        out[...] = result[part * stride : part * stride + count].astype(jnp.bfloat16)


def combine_kernel(count, capacity, top_count, place, notes, *refs):
    returned, outs = refs[:4], refs[4 : 4 + count]
    expert = place[4]
    total = notes.shape[0]
    tok_rows = total // count
    row = lax.broadcasted_iota(jnp.int32, (LANES, LANES), 0)
    lane = lax.broadcasted_iota(jnp.int32, (LANES, LANES), 1)
    added = (lane < top_count) & (row >= top_count) & (row < 4 * top_count) & (row % top_count == lane)
    gates = f32_dot(notes[...], jnp.where(added, 1.0, 0.0).astype(jnp.bfloat16))
    routes = notes[...].astype(jnp.float32)
    routes = jnp.where(lax.broadcasted_iota(jnp.int32, routes.shape, 1) < top_count, routes, -1.0)
    later = lax.broadcasted_iota(jnp.int32, (total, total), 0)
    earlier = lax.broadcasted_iota(jnp.int32, (total, total), 1)
    before = ((earlier < later) & (earlier // tok_rows == later // tok_rows)).astype(jnp.bfloat16)
    first_slot = lax.broadcasted_iota(jnp.int32, (total, 1), 0) // tok_rows * capacity
    slot = lax.broadcasted_iota(jnp.int32, (total, count * capacity), 1)
    mixed = jnp.zeros((total, returned[0].shape[1]), jnp.float32)
    for hop in range(4):
        hit = routes == (expert ^ hop).astype(jnp.float32)
        member = jnp.sum(jnp.where(hit, 1.0, 0.0), axis=1, keepdims=True)
        factor = jnp.sum(jnp.where(hit, gates, 0.0), axis=1, keepdims=True)
        place_in = f32_dot(before, jnp.broadcast_to(member, (total, LANES)).astype(jnp.bfloat16))[:, 0:1]
        target = jnp.where(member > 0.5, place_in.astype(jnp.int32) + first_slot, -1)
        placing = jnp.where(slot == target, factor, 0.0)
        upper = placing.astype(jnp.bfloat16)
        lower = (placing - upper.astype(jnp.float32)).astype(jnp.bfloat16)
        mixed = mixed + f32_dot(upper, returned[hop][...]) + f32_dot(lower, returned[hop][...])
    for turn in range(count):
        outs[turn][...] = mixed[turn * tok_rows : (turn + 1) * tok_rows].astype(jnp.bfloat16)


def shards(
    inputs,
    attn_gain,
    w_query,
    w_key,
    w_value,
    w_out,
    sel_blocks,
    ffn_gain,
    w_gate,
    w_up,
    w_down,
    routes,
    gate_weights,
):
    tok_rows, model_width = inputs.shape
    block_len, heads_here, pick_count = sel_blocks.shape
    hidden_cols = w_query.shape[1]
    head_dim = hidden_cols // heads_here
    ctx_count, exp_count = lax.axis_size("ctx"), lax.axis_size("exp")
    depth = ctx_count // 2
    ctx_index, exp_index = lax.axis_index("ctx"), lax.axis_index("exp")
    z_index, x_index = ctx_index // 2, ctx_index % 2
    expert = (ctx_index * exp_count + exp_index) // 2
    by_head = heads_here == depth and block_len <= 3 * head_dim and head_dim == LANES
    place = jnp.stack(
        [exp_index, z_index, exp_index % 2, z_index if by_head else jnp.zeros_like(z_index), expert]
    ).astype(jnp.int32)

    far = move(inputs, lambda z, x, y, c: (z, x, y ^ 1, c))
    near = swap_core(inputs)
    far_near = swap_core(far)
    weights = (w_gate, w_up, w_down)
    top_count = routes.shape[1]
    noted = jnp.concatenate([routes.astype(jnp.float32)] + [gate_weights] * 3, axis=1)
    noted = jnp.pad(noted, ((0, 0), (0, LANES - noted.shape[1])))
    if by_head:
        marks = jnp.sum(
            jnp.where(sel_blocks < ctx_index, jnp.left_shift(1, jnp.minimum(sel_blocks, 30)), 0), axis=2
        )
        marks = jnp.pad(marks.T.astype(jnp.bfloat16), ((0, 0), (0, 3 * head_dim - block_len)))
        marks = jnp.broadcast_to(marks[:, None], (heads_here, PAD_ROWS, 3 * head_dim))
        payload = struct(block_len + PAD_ROWS, 3 * head_dim)
        sent = call(
            functools.partial(project_kernel, exp_count, depth, head_dim),
            [payload] * depth,
            [place, inputs, near, far, far_near, attn_gain.reshape(1, -1), marks, w_query, w_key, w_value],
            [
                pltpu.VMEM((block_len, model_width), jnp.bfloat16),
                pltpu.VMEM((3, block_len, hidden_cols), jnp.bfloat16),
                pltpu.VMEM((3, model_width, hidden_cols), jnp.bfloat16),
                pltpu.SemaphoreType.DMA((3,)),
            ],
            flops=6 * block_len * model_width * hidden_cols,
            hbm=3,
        )
        own = [head_out(sent[turn], turn) for turn in range(depth)]
        beside = [swap_core(block) for block in own]
        other_weights = [swap_core(after(weight, *beside)) for weight in weights]
        mixed = call(
            functools.partial(attend_kernel, depth, block_len, head_dim),
            [struct(block_len, head_dim)] * depth,
            [place, *own, *beside],
            [
                pltpu.VMEM((depth, block_len + PAD_ROWS, 3 * head_dim), jnp.bfloat16),
                pltpu.VMEM((depth, block_len, 2 * head_dim), jnp.bfloat16),
                pltpu.VMEM((depth, block_len, head_dim), jnp.bfloat16),
            ],
            flops=4 * depth * ctx_count * block_len * block_len * head_dim,
        )
        heads = [head_back(mixed[turn], turn) for turn in range(depth)]
    else:
        block = jnp.stack([inputs, near, far, far_near])[exp_index ^ jnp.arange(exp_count)]
        normed = normalize(block.reshape(block_len, model_width), attn_gain)
        heads = attend_gathered(normed, w_query, w_key, w_value, sel_blocks)
        other_weights = [swap_core(weight) for weight in weights]

    halves = struct(exp_count // 2, tok_rows, model_width)
    kept, given = call(
        functools.partial(mix_kernel, exp_count, heads_here, head_dim),
        [halves, halves],
        [place, *heads, w_out],
        [
            pltpu.VMEM((block_len, hidden_cols), jnp.bfloat16),
            pltpu.VMEM((block_len, model_width), jnp.bfloat16),
        ],
        flops=2 * block_len * model_width * hidden_cols,
    )
    given = swap_core(given)
    beyond = (kept[1].astype(jnp.float32) + given[1].astype(jnp.float32)).astype(jnp.bfloat16)
    own_weights, other_weights = (
        [gate[0].T, up[0].T, down[0]] for gate, up, down in (weights, other_weights)
    )
    expert_weights = [*load([after(weight, beyond) for weight in own_weights]), *other_weights]
    beyond = move(beyond, lambda z, x, y, c: (z, x, y ^ 1, c))
    beyond, expert_weights = lax.optimization_barrier((beyond, expert_weights))
    residual, ffn_in = call(
        functools.partial(residual_kernel, top_count),
        [struct(tok_rows, model_width), struct(tok_rows, model_width + LANES)],
        [inputs, kept, given, beyond, ffn_gain.reshape(1, -1), noted],
        smem=0,
    )

    experts = ctx_count * exp_count // 2
    capacity = 2 * max(1, (tok_rows * top_count + experts - 1) // experts * 2 // 3)
    column = gather_z(ffn_in)
    groups = [[0], [1, depth - 1], list(range(2, depth - 1))]
    arrived, notes = [], []
    for group in groups:
        count = len(group)
        first = column[group[0]]
        *packed, note = call(
            functools.partial(pack_kernel, count, capacity, top_count),
            [struct(count * capacity, model_width)] * 4 + [struct(count * tok_rows, LANES)],
            [place, after(first, arrived[-1][0]) if arrived else first, *[column[t] for t in group[1:]]],
            [pltpu.VMEM((count * tok_rows, model_width), jnp.bfloat16)],
            flops=8 * count * capacity * count * tok_rows * model_width,
            limit=8 * MIB + 16 * (count * tok_rows) ** 2 + 8 * count * tok_rows * model_width,
        )
        arrived.append([packed[0]] + [swap_layer(packed[hop], hop) for hop in range(1, 4)])
        notes.append(note)
    results = []
    for group, rows in zip(groups, arrived):
        slots = len(group) * capacity
        stride = -(-slots // 16) * 16
        if results:
            rows = [after(rows[0], results[-1][0])] + rows[1:]
        results.append(
            call(
                functools.partial(expert_kernel, 4, stride),
                [struct(slots, model_width)] * 4,
                [*rows, *expert_weights],
                [pltpu.VMEM((4 * stride, model_width), jnp.bfloat16)],
                flops=48 * slots * model_width * w_gate.shape[2],
                smem=0,
                limit=8 * MIB + 4 * stride * (12 * model_width + 16 * w_gate.shape[2]),
            )
        )
    sums = [None] * depth
    sent_last = None
    for index in (0, 2, 1):
        group, rows = groups[index], list(results[index])
        if sent_last is not None:
            rows[1:] = [after(row, sent_last) for row in rows[1:]]
        sent_last = rows[3]
        rows = [rows[0]] + [swap_layer(rows[hop], hop) for hop in range(1, 4)]
        count = len(group)
        total = count * tok_rows
        parts = call(
            functools.partial(combine_kernel, count, capacity, top_count),
            [struct(tok_rows, model_width)] * count,
            [place, notes[index], *rows],
            flops=16 * count * capacity * total * model_width,
            limit=8 * MIB + 16 * total * total + 16 * total * model_width,
        )
        for turn, part in zip(group, parts):
            sums[turn] = part
    layer_out = residual.astype(jnp.float32) + sums[0].astype(jnp.float32)
    for turn in range(1, depth):
        layer_out = layer_out + turn_z(sums[turn], -turn).astype(jnp.float32)
    return layer_out.astype(jnp.bfloat16)


def solution(mesh):
    placed = (
        P(("ctx", "exp"), None),
        P(),
        P(None, "exp"),
        P(None, "exp"),
        P(None, "exp"),
        P("exp", None),
        P("ctx", "exp", None),
        P(),
        P(("ctx", "exp"), None, None),
        P(("ctx", "exp"), None, None),
        P(("ctx", "exp"), None, None),
        P(("ctx", "exp"), None),
        P(("ctx", "exp"), None),
    )
    return jax.shard_map(
        shards, mesh=mesh, in_specs=placed, out_specs=P(("ctx", "exp"), None), check_vma=False
    )
```

```python
import functools
import math

import jax
import jax.numpy as jnp
from jax import lax
from jax.experimental import pallas as pl
from jax.experimental.pallas import tpu as pltpu
from jax.sharding import PartitionSpec as P

AXES = ("ctx", "exp")
MIB = 1024 * 1024
VMEM = pl.BlockSpec(memory_space=pltpu.VMEM)
SMEM = pl.BlockSpec(memory_space=pltpu.SMEM)
HBM = pl.BlockSpec(memory_space=pltpu.HBM)
PAD_ROWS = 16
LANES = 128


def move(block, target):
    ctx_count, exp_count = lax.axis_size("ctx"), lax.axis_size("exp")
    route = []
    for ctx in range(ctx_count):
        for exp in range(exp_count):
            z, x, y, c = target(ctx // 2, ctx % 2, exp // 2, exp % 2)
            route.append((ctx * exp_count + exp, (z * 2 + x) * exp_count + y * 2 + c))
    return lax.ppermute(block, AXES, route)


def swap_core(block):
    return move(block, lambda z, x, y, c: (z, x, y, c ^ 1))


def swap_layer(block, hop):
    return move(block, lambda z, x, y, c: (z, x ^ (hop >> 1), y ^ (hop & 1), c))


def turn_z(block, turn):
    depth = lax.axis_size("ctx") // 2
    return move(block, lambda z, x, y, c: ((z + turn) % depth, x, y, c))


def gather_z(block):
    depth = lax.axis_size("ctx") // 2
    column = [block] + [None] * (depth - 1)
    for turn in range(1, depth // 2 + 1):
        column[turn] = turn_z(column[turn - 1], 1)
    for turn in range(depth - 1, depth // 2, -1):
        column[turn] = turn_z(column[(turn + 1) % depth], -1)
    return column


def head_out(block, turn):
    depth = lax.axis_size("ctx") // 2
    return move(block, lambda z, x, y, c: ((z + turn) % depth, c, y, x))


def head_back(block, turn):
    depth = lax.axis_size("ctx") // 2
    return move(block, lambda z, x, y, c: ((z - turn) % depth, c, y, x))


def normalize(values, gain_vec):
    floats = values.astype(jnp.float32)
    factor = lax.rsqrt(jnp.mean(floats * floats, axis=-1, keepdims=True) + 1e-06)
    return (floats * factor * gain_vec).astype(jnp.bfloat16)


def f32_dot(left, right):
    return jnp.dot(left, right, preferred_element_type=jnp.float32)


def struct(*shape, dtype=jnp.bfloat16):
    return pltpu.VMEM(shape, dtype)


def call(kernel, outs, operands, scratch=(), flops=0, smem=1, hbm=0, limit=16 * MIB):
    last = len(operands) - hbm
    operands = [
        a if i < smem else pltpu.with_memory_space_constraint(a, pltpu.VMEM if i < last else pltpu.HBM)
        for i, a in enumerate(operands)
    ]
    return pl.pallas_call(
        kernel,
        out_shape=outs,
        in_specs=[SMEM] * smem + [VMEM] * (last - smem) + [HBM] * hbm,
        out_specs=jax.tree.map(lambda _: VMEM, outs),
        scratch_shapes=list(scratch),
        compiler_params=pltpu.CompilerParams(vmem_limit_bytes=limit),
        cost_estimate=pl.CostEstimate(
            flops=flops,
            bytes_accessed=sum(a.size * a.dtype.itemsize for a in operands),
            transcendentals=0,
        ),
    )(*operands)


def after(value, *others):
    return lax.optimization_barrier((value, *others))[0]


def load_kernel(count, *refs):
    sources, targets, sems = refs[:count], refs[count : 2 * count], refs[2 * count]
    copies = [
        pltpu.make_async_copy(sources[i], targets[i], sems.at[i]) for i in range(count)
    ]
    for copy in copies:
        copy.start()
    for copy in copies:
        copy.wait()


def load(arrays):
    count = len(arrays)
    return pl.pallas_call(
        functools.partial(load_kernel, count),
        out_shape=[struct(*a.shape) for a in arrays],
        in_specs=[pl.BlockSpec(memory_space=pl.ANY)] * count,
        out_specs=[VMEM] * count,
        scratch_shapes=[pltpu.SemaphoreType.DMA((count,))],
        compiler_params=pltpu.CompilerParams(vmem_limit_bytes=MIB),
        cost_estimate=pl.CostEstimate(
            flops=0, bytes_accessed=sum(2 * a.size * a.dtype.itemsize for a in arrays), transcendentals=0
        ),
    )(*arrays)


def project_kernel(hops, depth, head_dim, place, *refs):
    row_refs, marks, sources = refs[: hops - 1], refs[hops - 1], refs[hops : hops + 5]
    outs, (rows, mixed, own, gain, held, sems) = refs[hops + 5 : hops + 5 + depth], refs[hops + 5 + depth :]
    exp_index, z_index = place[0], place[1]
    tok_rows = row_refs[0].shape[0]
    block_len = hops * tok_rows
    targets = [own, gain, *(held.at[i] for i in range(3))]
    copies = [pltpu.make_async_copy(sources[i], targets[i], sems.at[i]) for i in range(5)]
    for copy in copies:
        copy.start()
    copies[0].wait()
    copies[1].wait()
    for hop, row_ref in enumerate((own, *row_refs)):
        start = pl.multiple_of((exp_index ^ hop) * tok_rows, 16)
        rows[pl.ds(start, tok_rows), :] = normalize(row_ref[...], gain[...])
    for part, copy in enumerate(copies[2:]):
        copy.wait()
        mixed[part] = f32_dot(rows[...], held[part]).astype(jnp.bfloat16)
    for turn in range(depth):
        head = lax.rem(z_index + turn, depth)
        columns = pl.ds(pl.multiple_of(head * head_dim, head_dim), head_dim)
        for part in range(3):
            outs[turn][0:block_len, part * head_dim : (part + 1) * head_dim] = mixed[part, :, columns]
        outs[turn][block_len : block_len + PAD_ROWS, :] = marks[head]


def attend_kernel(depth, block_len, head_dim, place, *refs):
    own_refs, near_refs = refs[:depth], refs[depth : 2 * depth]
    outs, (own, near, mixed) = refs[2 * depth : 3 * depth], refs[3 * depth :]
    z_index, core = place[1], place[2]
    scaling = math.log2(math.e) / math.sqrt(head_dim)
    for turn in range(depth):
        source = lax.rem(z_index + depth - turn, depth)
        own[source] = own_refs[turn][...]
        near[source] = near_refs[turn][0:block_len, head_dim : 3 * head_dim]
    key_pos = lax.broadcasted_iota(jnp.int32, (block_len, block_len), 0)
    query_pos = lax.broadcasted_iota(jnp.int32, (block_len, block_len), 1)
    causal = jnp.where(key_pos <= query_pos, 0.0, -1e30)
    for level in range(depth):
        query = own[level, 0:block_len, 0:head_dim]
        marks = own[level, block_len : block_len + PAD_ROWS, 0:block_len].astype(jnp.float32)
        marks = marks[0:1].astype(jnp.int32)
        run_max = run_sum = total = None
        order = [(level, True)] + [(c, True) for c in range(level)] + [(c, False) for c in range(level + 1)]
        for c, mine in order:
            if mine:
                key = own[c, 0:block_len, head_dim : 2 * head_dim]
                value = own[c, 0:block_len, 2 * head_dim : 3 * head_dim]
            else:
                key, value = near[c, :, 0:head_dim], near[c, :, head_dim : 2 * head_dim]
            scores = lax.dot_general(
                key, query, (((1,), (1,)), ((), ())), preferred_element_type=jnp.float32
            )
            if run_max is None:
                scores = scores + causal
                shift = run_max = jnp.max(scores, axis=0, keepdims=True)
            else:
                bit = 2 * c + (core if mine else 1 - core)
                chosen = lax.shift_right_logical(marks, jnp.broadcast_to(bit, marks.shape)) & 1
                top = jnp.where(chosen == 1, jnp.max(scores, axis=0, keepdims=True), -1e30)
                new_max = jnp.maximum(run_max, top)
                rescale = jnp.exp2((run_max - new_max) * scaling)
                run_max = new_max
                shift = jnp.where(chosen == 1, new_max, 1e30)
            weights = jnp.exp2((scores - shift) * scaling)
            added = jnp.sum(weights, axis=0, keepdims=True)
            product = lax.dot_general(
                value,
                weights.astype(jnp.bfloat16),
                (((0,), (0,)), ((), ())),
                preferred_element_type=jnp.float32,
            )
            if total is None:
                run_sum, total = added, product
            else:
                run_sum, total = run_sum * rescale + added, total * rescale + product
        mixed[level] = (total / run_sum).T.astype(jnp.bfloat16)
    for turn in range(depth):
        outs[turn][...] = mixed[lax.rem(z_index + depth - turn, depth)]


def attend_gathered(normed_block, w_query, w_key, w_value, sel_blocks):
    block_len, heads_here, _ = sel_blocks.shape
    hidden_cols = w_query.shape[1]
    head_dim = hidden_cols // heads_here
    ctx_count, ctx_index = lax.axis_size("ctx"), lax.axis_index("ctx")
    query_part, key_part, value_part = (
        f32_dot(normed_block, weight).astype(jnp.bfloat16) for weight in (w_query, w_key, w_value)
    )
    queries = query_part.reshape(block_len, heads_here, head_dim)
    keys_values = jnp.stack([key_part, value_part], axis=1)
    block_ids = jnp.arange(ctx_count, dtype=jnp.int32)
    chosen = jnp.any(sel_blocks[:, :, :, None] == block_ids, axis=2) & (block_ids < ctx_index)
    position = jnp.arange(block_len, dtype=jnp.int32)
    causal = position[None, :] <= position[:, None]
    scaling = 1.0 / math.sqrt(head_dim)

    def fold_step(running, operands):
        run_max, run_sum, totals = running
        piece, block = operands
        key_rows = piece[:, 0].reshape(block_len, heads_here, head_dim)
        value_rows = piece[:, 1].reshape(block_len, heads_here, head_dim)
        scores = (
            jnp.einsum("qhd,khd->hqk", queries, key_rows, preferred_element_type=jnp.float32)
            * scaling
        )
        picked = jnp.take(chosen, block, axis=2).T[:, :, None]
        allowed = picked | ((block == ctx_index) & causal)[None]
        new_max = jnp.maximum(run_max, jnp.max(jnp.where(allowed, scores, -jnp.inf), axis=-1))
        weights = jnp.where(allowed, jnp.exp(scores - new_max[..., None]), 0.0)
        rescale = jnp.exp(run_max - new_max)
        run_sum = run_sum * rescale + jnp.sum(weights, axis=-1)
        totals = totals * rescale[..., None] + jnp.einsum(
            "hqk,khd->hqd",
            weights.astype(jnp.bfloat16),
            value_rows,
            preferred_element_type=jnp.float32,
        )
        return (new_max, run_sum, totals), None

    initial = (
        jnp.full((heads_here, block_len), -1e30, jnp.float32),
        jnp.zeros((heads_here, block_len), jnp.float32),
        jnp.zeros((heads_here, block_len, head_dim), jnp.float32),
    )
    gathered = lax.all_gather(keys_values, "ctx", axis=0)
    (_, run_sum, totals), _ = lax.scan(fold_step, initial, (gathered, block_ids))
    attended = (totals / run_sum[..., None]).astype(jnp.bfloat16)
    return [attended[head] for head in range(heads_here)]


def mix_kernel(hops, heads, head_dim, place, *refs):
    head_refs, w_out = refs[:heads], refs[heads]
    kept, given, attended, mixed = refs[heads + 1 :]
    exp_index, turned = place[0], place[3]
    tok_rows = kept.shape[1]
    for turn, head_ref in enumerate(head_refs):
        head = lax.rem(turned + turn, heads)
        attended[:, pl.ds(pl.multiple_of(head * head_dim, head_dim), head_dim)] = head_ref[...]
    mixed[...] = f32_dot(attended[...], w_out[...]).astype(jnp.bfloat16)
    for hop in range(hops):
        start = pl.multiple_of((exp_index ^ hop) * tok_rows, 16)
        (given if hop & 1 else kept)[hop >> 1] = mixed[pl.ds(start, tok_rows), :]


def halves_kernel(inputs, kept, given, here, beyond):
    summed = kept[0].astype(jnp.float32) + given[0].astype(jnp.float32)
    here[...] = inputs[...].astype(jnp.float32) + summed
    beyond[...] = (kept[1].astype(jnp.float32) + given[1].astype(jnp.float32)).astype(jnp.bfloat16)


def residual_kernel(top_count, here, far, gain, noted, residual, ffn_in):
    rounded = (here[...] + far[...].astype(jnp.float32)).astype(jnp.bfloat16)
    residual[...] = rounded
    model_width = rounded.shape[1]
    ffn_in[:, 0:model_width] = normalize(rounded, gain[...])
    lane = lax.broadcasted_iota(jnp.int32, noted.shape, 1)
    left = noted[...]
    upper = left.astype(jnp.bfloat16).astype(jnp.float32)
    left = left - upper
    middle = left.astype(jnp.bfloat16).astype(jnp.float32)
    lower = left - middle
    parts = jnp.where(lane < 2 * top_count, upper, jnp.where(lane < 3 * top_count, middle, lower))
    ffn_in[:, model_width:] = parts.astype(jnp.bfloat16)


def pack_kernel(count, capacity, top_count, place, *refs):
    sources, outs, (notes, rows) = refs[:count], refs[count : count + 4], refs[count + 4 :]
    expert = place[4]
    tok_rows = sources[0].shape[0]
    total = count * tok_rows
    model_width = rows.shape[1]
    for turn in range(count):
        part = slice(turn * tok_rows, (turn + 1) * tok_rows)
        rows[part, :] = sources[turn][:, 0:model_width]
        notes[part, :] = sources[turn][:, model_width:]
    routes = notes[...].astype(jnp.float32).T[0:8]
    routes = jnp.where(lax.broadcasted_iota(jnp.int32, routes.shape, 0) < top_count, routes, -1.0)
    earlier = lax.broadcasted_iota(jnp.int32, (total, total), 0)
    later = lax.broadcasted_iota(jnp.int32, (total, total), 1)
    before = ((earlier < later) & (earlier // tok_rows == later // tok_rows)).astype(jnp.bfloat16)
    first_slot = lax.broadcasted_iota(jnp.int32, (1, total), 1) // tok_rows * capacity
    slot = lax.broadcasted_iota(jnp.int32, (count * capacity, total), 0)
    for hop in range(4):
        hit = jnp.where(routes == (expert ^ hop).astype(jnp.float32), 1.0, 0.0)
        member = jnp.sum(hit, axis=0, keepdims=True)
        place_in = f32_dot(jnp.broadcast_to(member, (16, total)).astype(jnp.bfloat16), before)[0:1]
        target = jnp.where(member > 0.5, place_in.astype(jnp.int32) + first_slot, -1)
        placing = jnp.where(slot == target, 1.0, 0.0).astype(jnp.bfloat16)
        outs[hop][...] = f32_dot(placing, rows[...]).astype(jnp.bfloat16)


def expert_kernel(starts, *refs):
    parts = len(starts)
    row_refs, weights = refs[:parts], refs[parts : parts + 6]
    outs, (held,) = refs[parts + 6 : 2 * parts + 6], refs[2 * parts + 6 :]
    across = (((1,), (1,)), ((), ()))
    for start, row_ref in zip(starts, row_refs):
        held[start : start + row_ref.shape[0], :] = row_ref[...]
    rows = held[...]
    result = None
    for w_gate, w_up, w_down in (weights[:3], weights[3:]):
        gate_part = lax.dot_general(rows, w_gate[...], across, preferred_element_type=jnp.float32)
        up_part = lax.dot_general(rows, w_up[...], across, preferred_element_type=jnp.float32)
        hidden = (gate_part / (1.0 + jnp.exp(-gate_part)) * up_part).astype(jnp.bfloat16)
        product = f32_dot(hidden, w_down[...])
        result = product if result is None else result + product
    for start, out in zip(starts, outs):
        out[...] = result[start : start + out.shape[0]].astype(jnp.bfloat16)


def combine_kernel(count, capacity, top_count, place, notes, *refs):
    returned, outs = refs[:4], refs[4 : 4 + count]
    expert = place[4]
    total = notes.shape[0]
    tok_rows = total // count
    row = lax.broadcasted_iota(jnp.int32, (LANES, LANES), 0)
    lane = lax.broadcasted_iota(jnp.int32, (LANES, LANES), 1)
    added = (lane < top_count) & (row >= top_count) & (row < 4 * top_count) & (row % top_count == lane)
    gates = f32_dot(notes[...], jnp.where(added, 1.0, 0.0).astype(jnp.bfloat16))
    routes = notes[...].astype(jnp.float32)
    routes = jnp.where(lax.broadcasted_iota(jnp.int32, routes.shape, 1) < top_count, routes, -1.0)
    later = lax.broadcasted_iota(jnp.int32, (total, total), 0)
    earlier = lax.broadcasted_iota(jnp.int32, (total, total), 1)
    before = ((earlier < later) & (earlier // tok_rows == later // tok_rows)).astype(jnp.bfloat16)
    first_slot = lax.broadcasted_iota(jnp.int32, (total, 1), 0) // tok_rows * capacity
    slot = lax.broadcasted_iota(jnp.int32, (total, count * capacity), 1)
    mixed = jnp.zeros((total, returned[0].shape[1]), jnp.float32)
    for hop in range(4):
        hit = routes == (expert ^ hop).astype(jnp.float32)
        member = jnp.sum(jnp.where(hit, 1.0, 0.0), axis=1, keepdims=True)
        factor = jnp.sum(jnp.where(hit, gates, 0.0), axis=1, keepdims=True)
        place_in = f32_dot(before, jnp.broadcast_to(member, (total, LANES)).astype(jnp.bfloat16))[:, 0:1]
        target = jnp.where(member > 0.5, place_in.astype(jnp.int32) + first_slot, -1)
        placing = jnp.where(slot == target, factor, 0.0)
        upper = placing.astype(jnp.bfloat16)
        lower = (placing - upper.astype(jnp.float32)).astype(jnp.bfloat16)
        mixed = mixed + f32_dot(upper, returned[hop][...]) + f32_dot(lower, returned[hop][...])
    for turn in range(count):
        outs[turn][...] = mixed[turn * tok_rows : (turn + 1) * tok_rows].astype(jnp.bfloat16)


def shards(
    inputs,
    attn_gain,
    w_query,
    w_key,
    w_value,
    w_out,
    sel_blocks,
    ffn_gain,
    w_gate,
    w_up,
    w_down,
    routes,
    gate_weights,
):
    tok_rows, model_width = inputs.shape
    block_len, heads_here, pick_count = sel_blocks.shape
    hidden_cols = w_query.shape[1]
    head_dim = hidden_cols // heads_here
    ctx_count, exp_count = lax.axis_size("ctx"), lax.axis_size("exp")
    depth = ctx_count // 2
    ctx_index, exp_index = lax.axis_index("ctx"), lax.axis_index("exp")
    z_index, x_index = ctx_index // 2, ctx_index % 2
    expert = (ctx_index * exp_count + exp_index) // 2
    by_head = heads_here == depth and block_len <= 3 * head_dim and head_dim == LANES
    place = jnp.stack(
        [exp_index, z_index, exp_index % 2, z_index if by_head else jnp.zeros_like(z_index), expert]
    ).astype(jnp.int32)

    far = move(inputs, lambda z, x, y, c: (z, x, y ^ 1, c))
    near = swap_core(inputs)
    far_near = swap_core(far)
    weights = (w_gate, w_up, w_down)
    top_count = routes.shape[1]
    noted = jnp.concatenate([routes.astype(jnp.float32)] + [gate_weights] * 3, axis=1)
    noted = jnp.pad(noted, ((0, 0), (0, LANES - noted.shape[1])))
    if by_head:
        marks = jnp.sum(
            jnp.where(sel_blocks < ctx_index, jnp.left_shift(1, jnp.minimum(sel_blocks, 30)), 0), axis=2
        )
        marks = jnp.pad(marks.T.astype(jnp.bfloat16), ((0, 0), (0, 3 * head_dim - block_len)))
        marks = jnp.broadcast_to(marks[:, None], (heads_here, PAD_ROWS, 3 * head_dim))
        payload = struct(block_len + PAD_ROWS, 3 * head_dim)
        sent = call(
            functools.partial(project_kernel, exp_count, depth, head_dim),
            [payload] * depth,
            [place, near, far, far_near, marks, inputs, attn_gain.reshape(1, -1), w_query, w_key, w_value],
            [
                pltpu.VMEM((block_len, model_width), jnp.bfloat16),
                pltpu.VMEM((3, block_len, hidden_cols), jnp.bfloat16),
                pltpu.VMEM((tok_rows, model_width), jnp.bfloat16),
                pltpu.VMEM((1, model_width), jnp.float32),
                pltpu.VMEM((3, model_width, hidden_cols), jnp.bfloat16),
                pltpu.SemaphoreType.DMA((5,)),
            ],
            flops=6 * block_len * model_width * hidden_cols,
            hbm=5,
        )
        own = [head_out(sent[turn], turn) for turn in range(depth)]
        beside = [swap_core(block) for block in own]
        early = [swap_core(after(weight, sent[0])) for weight in weights[:2]]
        other_weights = [*early, swap_core(after(weights[2], *beside))]
        mixed = call(
            functools.partial(attend_kernel, depth, block_len, head_dim),
            [struct(block_len, head_dim)] * depth,
            [place, *own, *beside],
            [
                pltpu.VMEM((depth, block_len + PAD_ROWS, 3 * head_dim), jnp.bfloat16),
                pltpu.VMEM((depth, block_len, 2 * head_dim), jnp.bfloat16),
                pltpu.VMEM((depth, block_len, head_dim), jnp.bfloat16),
            ],
            flops=4 * depth * ctx_count * block_len * block_len * head_dim,
        )
        heads = [head_back(mixed[turn], turn) for turn in range(depth)]
    else:
        block = jnp.stack([inputs, near, far, far_near])[exp_index ^ jnp.arange(exp_count)]
        normed = normalize(block.reshape(block_len, model_width), attn_gain)
        heads = attend_gathered(normed, w_query, w_key, w_value, sel_blocks)
        other_weights = [swap_core(weight) for weight in weights]

    halves = struct(exp_count // 2, tok_rows, model_width)
    kept, given = call(
        functools.partial(mix_kernel, exp_count, heads_here, head_dim),
        [halves, halves],
        [place, *heads, w_out],
        [
            pltpu.VMEM((block_len, hidden_cols), jnp.bfloat16),
            pltpu.VMEM((block_len, model_width), jnp.bfloat16),
        ],
        flops=2 * block_len * model_width * hidden_cols,
    )
    given = swap_core(given)
    here, beyond = call(
        halves_kernel,
        [struct(tok_rows, model_width, dtype=jnp.float32), struct(tok_rows, model_width)],
        [inputs, kept, given],
        smem=0,
    )
    own_weights, other_weights = (
        [gate[0].T, up[0].T, down[0]] for gate, up, down in (weights, other_weights)
    )
    expert_weights = load([after(weight, beyond) for weight in own_weights + other_weights])
    beyond = move(beyond, lambda z, x, y, c: (z, x, y ^ 1, c))
    beyond, expert_weights = lax.optimization_barrier((beyond, expert_weights))
    residual, ffn_in = call(
        functools.partial(residual_kernel, top_count),
        [struct(tok_rows, model_width), struct(tok_rows, model_width + LANES)],
        [here, beyond, ffn_gain.reshape(1, -1), noted],
        smem=0,
    )

    experts = ctx_count * exp_count // 2
    capacity = 2 * max(1, (tok_rows * top_count + experts - 1) // experts * 2 // 3)
    column = gather_z(ffn_in)
    groups = [[0], [1, depth - 1], list(range(2, depth - 1))]
    arrived, notes = [], []
    for group in groups:
        count = len(group)
        first = column[group[0]]
        *packed, note = call(
            functools.partial(pack_kernel, count, capacity, top_count),
            [struct(count * capacity, model_width)] * 4 + [struct(count * tok_rows, LANES)],
            [place, after(first, arrived[-1][0]) if arrived else first, *[column[t] for t in group[1:]]],
            [pltpu.VMEM((count * tok_rows, model_width), jnp.bfloat16)],
            flops=8 * count * capacity * count * tok_rows * model_width,
            limit=8 * MIB + 16 * (count * tok_rows) ** 2 + 8 * count * tok_rows * model_width,
        )
        arrived.append([packed[0]] + [swap_layer(packed[hop], hop) for hop in range(1, 4)])
        notes.append(note)

    def expert_rows(rows):
        starts, total = [], 0
        for row in rows:
            starts.append(total)
            total += -(-row.shape[0] // 16) * 16
        return call(
            functools.partial(expert_kernel, starts),
            [struct(*row.shape) for row in rows],
            [*rows, *expert_weights],
            [pltpu.VMEM((total, model_width), jnp.bfloat16)],
            flops=12 * total * model_width * w_gate.shape[2],
            smem=0,
            limit=4 * MIB + 32 * 1024 * total,
        )

    results = [None, expert_rows(arrived[1]), None]
    far_rows = [after(arrived[2][0], results[1][0])] + arrived[2][1:]
    both = expert_rows(arrived[0] + far_rows)
    results[0], results[2] = both[:4], both[4:]
    sums = [None] * depth
    for index in (1, 2, 0):
        group, rows = groups[index], list(results[index])
        if index == 0:
            rows[1:] = [after(row, sums[1]) for row in rows[1:]]
        rows = [rows[0]] + [swap_layer(rows[hop], hop) for hop in range(1, 4)]
        count = len(group)
        total = count * tok_rows
        parts = call(
            functools.partial(combine_kernel, count, capacity, top_count),
            [struct(tok_rows, model_width)] * count,
            [place, notes[index], *rows],
            flops=16 * count * capacity * total * model_width,
            limit=8 * MIB + 16 * total * total + 16 * total * model_width,
        )
        for turn, part in zip(group, parts):
            sums[turn] = part
    layer_out = residual.astype(jnp.float32) + sums[0].astype(jnp.float32)
    for turn in range(1, depth):
        layer_out = layer_out + turn_z(sums[turn], -turn).astype(jnp.float32)
    return layer_out.astype(jnp.bfloat16)


def solution(mesh):
    placed = (
        P(("ctx", "exp"), None),
        P(),
        P(None, "exp"),
        P(None, "exp"),
        P(None, "exp"),
        P("exp", None),
        P("ctx", "exp", None),
        P(),
        P(("ctx", "exp"), None, None),
        P(("ctx", "exp"), None, None),
        P(("ctx", "exp"), None, None),
        P(("ctx", "exp"), None),
        P(("ctx", "exp"), None),
    )
    return jax.shard_map(
        shards, mesh=mesh, in_specs=placed, out_specs=P(("ctx", "exp"), None), check_vma=False
    )
```

```python
import functools
import math

import jax
import jax.numpy as jnp
from jax import lax
from jax.experimental import pallas as pl
from jax.experimental.pallas import tpu as pltpu
from jax.sharding import PartitionSpec as P

AXES = ("ctx", "exp")
MIB = 1024 * 1024
VMEM = pl.BlockSpec(memory_space=pltpu.VMEM)
SMEM = pl.BlockSpec(memory_space=pltpu.SMEM)
ANY = pl.BlockSpec(memory_space=pl.ANY)
HBM = pl.BlockSpec(memory_space=pltpu.HBM)
PAD_ROWS = 16
LANES = 128


def move(block, target):
    ctx_count, exp_count = lax.axis_size("ctx"), lax.axis_size("exp")
    route = []
    for ctx in range(ctx_count):
        for exp in range(exp_count):
            z, x, y, c = target(ctx // 2, ctx % 2, exp // 2, exp % 2)
            route.append((ctx * exp_count + exp, (z * 2 + x) * exp_count + y * 2 + c))
    return lax.ppermute(block, AXES, route)


def swap_core(block):
    return move(block, lambda z, x, y, c: (z, x, y, c ^ 1))


def swap_layer(block, hop):
    return move(block, lambda z, x, y, c: (z, x ^ (hop >> 1), y ^ (hop & 1), c))


def turn_z(block, turn):
    depth = lax.axis_size("ctx") // 2
    return move(block, lambda z, x, y, c: ((z + turn) % depth, x, y, c))


def gather_z(block):
    depth = lax.axis_size("ctx") // 2
    column = [block] + [None] * (depth - 1)
    for turn in range(1, depth // 2 + 1):
        column[turn] = turn_z(column[turn - 1], 1)
    for turn in range(depth - 1, depth // 2, -1):
        column[turn] = turn_z(column[(turn + 1) % depth], -1)
    return column


def head_out(block, turn):
    depth = lax.axis_size("ctx") // 2
    return move(block, lambda z, x, y, c: ((z + turn) % depth, c, y, x))


def head_back(block, turn):
    depth = lax.axis_size("ctx") // 2
    return move(block, lambda z, x, y, c: ((z - turn) % depth, c, y, x))


def normalize(values, gain_vec):
    floats = values.astype(jnp.float32)
    factor = lax.rsqrt(jnp.mean(floats * floats, axis=-1, keepdims=True) + 1e-06)
    return (floats * factor * gain_vec).astype(jnp.bfloat16)


def f32_dot(left, right):
    return jnp.dot(left, right, preferred_element_type=jnp.float32)


def struct(*shape, dtype=jnp.bfloat16):
    return pltpu.VMEM(shape, dtype)


def call(kernel, outs, operands, scratch=(), flops=0, smem=1, anywhere=0, hbm=0, limit=16 * MIB):
    far = len(operands) - hbm
    last = far - anywhere
    operands = [
        pltpu.with_memory_space_constraint(a, pltpu.VMEM if i < last else pltpu.HBM)
        if smem <= i < last or i >= far
        else a
        for i, a in enumerate(operands)
    ]
    return pl.pallas_call(
        kernel,
        out_shape=outs,
        in_specs=[SMEM] * smem + [VMEM] * (last - smem) + [ANY] * anywhere + [HBM] * hbm,
        out_specs=jax.tree.map(lambda _: VMEM, outs),
        scratch_shapes=list(scratch),
        compiler_params=pltpu.CompilerParams(vmem_limit_bytes=limit),
        cost_estimate=pl.CostEstimate(
            flops=flops,
            bytes_accessed=sum(a.size * a.dtype.itemsize for a in operands),
            transcendentals=0,
        ),
    )(*operands)


def after(value, *others):
    return lax.optimization_barrier((value, *others))[0]


def load_kernel(count, *refs):
    sources, targets, sems = refs[:count], refs[count : 2 * count], refs[2 * count]
    copies = [
        pltpu.make_async_copy(sources[i], targets[i], sems.at[i]) for i in range(count)
    ]
    for copy in copies:
        copy.start()
    for copy in copies:
        copy.wait()


def load(received, held):
    arrays = [*received, *held]
    return call(
        functools.partial(load_kernel, len(arrays)),
        [struct(*a.shape) for a in arrays],
        arrays,
        [pltpu.SemaphoreType.DMA((len(arrays),))],
        smem=0,
        anywhere=len(received),
        hbm=len(held),
        limit=MIB,
    )


def project_kernel(hops, depth, head_dim, place, marks, *refs):
    sources, outs = refs[: hops + 4], refs[hops + 4 : hops + 4 + depth]
    given, rows, mixed, gain, held, sems = refs[hops + 4 + depth :]
    exp_index, z_index = place[0], place[1]
    tok_rows = given.shape[1]
    block_len = hops * tok_rows
    targets = [*(given.at[i] for i in range(1, hops)), gain, given.at[0], *(held.at[i] for i in range(3))]
    copies = [pltpu.make_async_copy(sources[i], targets[i], sems.at[i]) for i in range(hops + 4)]
    for copy in copies:
        copy.start()
    for copy in copies[: hops + 1]:
        copy.wait()
    for hop in range(hops):
        start = pl.multiple_of((exp_index ^ hop) * tok_rows, 16)
        rows[pl.ds(start, tok_rows), :] = normalize(given[hop], gain[...])
    for part, copy in enumerate(copies[hops + 1 :]):
        copy.wait()
        mixed[part] = f32_dot(rows[...], held[part]).astype(jnp.bfloat16)
    for turn in range(depth):
        head = lax.rem(z_index + turn, depth)
        columns = pl.ds(pl.multiple_of(head * head_dim, head_dim), head_dim)
        for part in range(3):
            outs[turn][0:block_len, part * head_dim : (part + 1) * head_dim] = mixed[part, :, columns]
        outs[turn][block_len : block_len + PAD_ROWS, :] = marks[head]


def attend_kernel(depth, block_len, head_dim, place, *refs):
    own_refs, near_refs = refs[:depth], refs[depth : 2 * depth]
    outs, (own, near, mixed) = refs[2 * depth : 3 * depth], refs[3 * depth :]
    z_index, core = place[1], place[2]
    scaling = math.log2(math.e) / math.sqrt(head_dim)
    for turn in range(depth):
        source = lax.rem(z_index + depth - turn, depth)
        own[source] = own_refs[turn][...]
        near[source] = near_refs[turn][0:block_len, head_dim : 3 * head_dim]
    key_pos = lax.broadcasted_iota(jnp.int32, (block_len, block_len), 0)
    query_pos = lax.broadcasted_iota(jnp.int32, (block_len, block_len), 1)
    causal = jnp.where(key_pos <= query_pos, 0.0, -1e30)
    for level in range(depth):
        query = own[level, 0:block_len, 0:head_dim]
        marks = own[level, block_len : block_len + PAD_ROWS, 0:block_len].astype(jnp.float32)
        marks = marks[0:1].astype(jnp.int32)
        run_max = run_sum = total = None
        order = [(level, True)] + [(c, True) for c in range(level)] + [(c, False) for c in range(level + 1)]
        for c, mine in order:
            if mine:
                key = own[c, 0:block_len, head_dim : 2 * head_dim]
                value = own[c, 0:block_len, 2 * head_dim : 3 * head_dim]
            else:
                key, value = near[c, :, 0:head_dim], near[c, :, head_dim : 2 * head_dim]
            scores = lax.dot_general(
                key, query, (((1,), (1,)), ((), ())), preferred_element_type=jnp.float32
            )
            if run_max is None:
                scores = scores + causal
                shift = run_max = jnp.max(scores, axis=0, keepdims=True)
            else:
                bit = 2 * c + (core if mine else 1 - core)
                chosen = lax.shift_right_logical(marks, jnp.broadcast_to(bit, marks.shape)) & 1
                top = jnp.where(chosen == 1, jnp.max(scores, axis=0, keepdims=True), -1e30)
                new_max = jnp.maximum(run_max, top)
                rescale = jnp.exp2((run_max - new_max) * scaling)
                run_max = new_max
                shift = jnp.where(chosen == 1, new_max, 1e30)
            weights = jnp.exp2((scores - shift) * scaling)
            added = jnp.sum(weights, axis=0, keepdims=True)
            product = lax.dot_general(
                value,
                weights.astype(jnp.bfloat16),
                (((0,), (0,)), ((), ())),
                preferred_element_type=jnp.float32,
            )
            if total is None:
                run_sum, total = added, product
            else:
                run_sum, total = run_sum * rescale + added, total * rescale + product
        mixed[level] = (total / run_sum).T.astype(jnp.bfloat16)
    for turn in range(depth):
        outs[turn][...] = mixed[lax.rem(z_index + depth - turn, depth)]


def attend_gathered(normed_block, w_query, w_key, w_value, sel_blocks):
    block_len, heads_here, _ = sel_blocks.shape
    hidden_cols = w_query.shape[1]
    head_dim = hidden_cols // heads_here
    ctx_count, ctx_index = lax.axis_size("ctx"), lax.axis_index("ctx")
    query_part, key_part, value_part = (
        f32_dot(normed_block, weight).astype(jnp.bfloat16) for weight in (w_query, w_key, w_value)
    )
    queries = query_part.reshape(block_len, heads_here, head_dim)
    keys_values = jnp.stack([key_part, value_part], axis=1)
    block_ids = jnp.arange(ctx_count, dtype=jnp.int32)
    chosen = jnp.any(sel_blocks[:, :, :, None] == block_ids, axis=2) & (block_ids < ctx_index)
    position = jnp.arange(block_len, dtype=jnp.int32)
    causal = position[None, :] <= position[:, None]
    scaling = 1.0 / math.sqrt(head_dim)

    def fold_step(running, operands):
        run_max, run_sum, totals = running
        piece, block = operands
        key_rows = piece[:, 0].reshape(block_len, heads_here, head_dim)
        value_rows = piece[:, 1].reshape(block_len, heads_here, head_dim)
        scores = (
            jnp.einsum("qhd,khd->hqk", queries, key_rows, preferred_element_type=jnp.float32)
            * scaling
        )
        picked = jnp.take(chosen, block, axis=2).T[:, :, None]
        allowed = picked | ((block == ctx_index) & causal)[None]
        new_max = jnp.maximum(run_max, jnp.max(jnp.where(allowed, scores, -jnp.inf), axis=-1))
        weights = jnp.where(allowed, jnp.exp(scores - new_max[..., None]), 0.0)
        rescale = jnp.exp(run_max - new_max)
        run_sum = run_sum * rescale + jnp.sum(weights, axis=-1)
        totals = totals * rescale[..., None] + jnp.einsum(
            "hqk,khd->hqd",
            weights.astype(jnp.bfloat16),
            value_rows,
            preferred_element_type=jnp.float32,
        )
        return (new_max, run_sum, totals), None

    initial = (
        jnp.full((heads_here, block_len), -1e30, jnp.float32),
        jnp.zeros((heads_here, block_len), jnp.float32),
        jnp.zeros((heads_here, block_len, head_dim), jnp.float32),
    )
    gathered = lax.all_gather(keys_values, "ctx", axis=0)
    (_, run_sum, totals), _ = lax.scan(fold_step, initial, (gathered, block_ids))
    attended = (totals / run_sum[..., None]).astype(jnp.bfloat16)
    return [attended[head] for head in range(heads_here)]


def mix_kernel(hops, heads, head_dim, place, *refs):
    head_refs, w_out = refs[:heads], refs[heads]
    kept, given, attended, mixed = refs[heads + 1 :]
    exp_index, turned = place[0], place[3]
    tok_rows = kept.shape[1]
    for turn, head_ref in enumerate(head_refs):
        head = lax.rem(turned + turn, heads)
        attended[:, pl.ds(pl.multiple_of(head * head_dim, head_dim), head_dim)] = head_ref[...]
    mixed[...] = f32_dot(attended[...], w_out[...]).astype(jnp.bfloat16)
    for hop in range(hops):
        start = pl.multiple_of((exp_index ^ hop) * tok_rows, 16)
        (given if hop & 1 else kept)[hop >> 1] = mixed[pl.ds(start, tok_rows), :]


def halves_kernel(inputs, kept, given, here, beyond):
    summed = kept[0].astype(jnp.float32) + given[0].astype(jnp.float32)
    here[...] = inputs[...].astype(jnp.float32) + summed
    beyond[...] = (kept[1].astype(jnp.float32) + given[1].astype(jnp.float32)).astype(jnp.bfloat16)


def residual_kernel(top_count, here, far, gain, noted, residual, ffn_in):
    rounded = (here[...] + far[...].astype(jnp.float32)).astype(jnp.bfloat16)
    residual[...] = rounded
    model_width = rounded.shape[1]
    ffn_in[:, 0:model_width] = normalize(rounded, gain[...])
    lane = lax.broadcasted_iota(jnp.int32, noted.shape, 1)
    left = noted[...]
    upper = left.astype(jnp.bfloat16).astype(jnp.float32)
    left = left - upper
    middle = left.astype(jnp.bfloat16).astype(jnp.float32)
    lower = left - middle
    parts = jnp.where(lane < 2 * top_count, upper, jnp.where(lane < 3 * top_count, middle, lower))
    ffn_in[:, model_width:] = parts.astype(jnp.bfloat16)


def pack_kernel(count, capacity, top_count, place, *refs):
    sources, outs, (notes, rows) = refs[:count], refs[count : count + 4], refs[count + 4 :]
    expert = place[4]
    tok_rows = sources[0].shape[0]
    total = count * tok_rows
    model_width = rows.shape[1]
    for turn in range(count):
        part = slice(turn * tok_rows, (turn + 1) * tok_rows)
        rows[part, :] = sources[turn][:, 0:model_width]
        notes[part, :] = sources[turn][:, model_width:]
    routes = notes[...].astype(jnp.float32).T[0:8]
    routes = jnp.where(lax.broadcasted_iota(jnp.int32, routes.shape, 0) < top_count, routes, -1.0)
    earlier = lax.broadcasted_iota(jnp.int32, (total, total), 0)
    later = lax.broadcasted_iota(jnp.int32, (total, total), 1)
    before = ((earlier < later) & (earlier // tok_rows == later // tok_rows)).astype(jnp.bfloat16)
    first_slot = lax.broadcasted_iota(jnp.int32, (1, total), 1) // tok_rows * capacity
    slot = lax.broadcasted_iota(jnp.int32, (count * capacity, total), 0)
    for hop in range(4):
        hit = jnp.where(routes == (expert ^ hop).astype(jnp.float32), 1.0, 0.0)
        member = jnp.sum(hit, axis=0, keepdims=True)
        place_in = f32_dot(jnp.broadcast_to(member, (16, total)).astype(jnp.bfloat16), before)[0:1]
        target = jnp.where(member > 0.5, place_in.astype(jnp.int32) + first_slot, -1)
        placing = jnp.where(slot == target, 1.0, 0.0).astype(jnp.bfloat16)
        outs[hop][...] = f32_dot(placing, rows[...]).astype(jnp.bfloat16)


def expert_kernel(starts, *refs):
    parts = len(starts)
    row_refs, weights = refs[:parts], refs[parts : parts + 6]
    outs, (held,) = refs[parts + 6 : 2 * parts + 6], refs[2 * parts + 6 :]
    across = (((1,), (1,)), ((), ()))
    for start, row_ref in zip(starts, row_refs):
        held[start : start + row_ref.shape[0], :] = row_ref[...]
    rows = held[...]
    result = None
    for w_gate, w_up, w_down in (weights[:3], weights[3:]):
        gate_part = lax.dot_general(rows, w_gate[...], across, preferred_element_type=jnp.float32)
        up_part = lax.dot_general(rows, w_up[...], across, preferred_element_type=jnp.float32)
        hidden = (gate_part / (1.0 + jnp.exp(-gate_part)) * up_part).astype(jnp.bfloat16)
        product = f32_dot(hidden, w_down[...])
        result = product if result is None else result + product
    for start, out in zip(starts, outs):
        out[...] = result[start : start + out.shape[0]].astype(jnp.bfloat16)


def combine_kernel(count, capacity, top_count, place, notes, *refs):
    returned, outs = refs[:4], refs[4 : 4 + count]
    expert = place[4]
    total = notes.shape[0]
    tok_rows = total // count
    row = lax.broadcasted_iota(jnp.int32, (LANES, LANES), 0)
    lane = lax.broadcasted_iota(jnp.int32, (LANES, LANES), 1)
    added = (lane < top_count) & (row >= top_count) & (row < 4 * top_count) & (row % top_count == lane)
    gates = f32_dot(notes[...], jnp.where(added, 1.0, 0.0).astype(jnp.bfloat16))
    routes = notes[...].astype(jnp.float32)
    routes = jnp.where(lax.broadcasted_iota(jnp.int32, routes.shape, 1) < top_count, routes, -1.0)
    later = lax.broadcasted_iota(jnp.int32, (total, total), 0)
    earlier = lax.broadcasted_iota(jnp.int32, (total, total), 1)
    before = ((earlier < later) & (earlier // tok_rows == later // tok_rows)).astype(jnp.bfloat16)
    first_slot = lax.broadcasted_iota(jnp.int32, (total, 1), 0) // tok_rows * capacity
    slot = lax.broadcasted_iota(jnp.int32, (total, count * capacity), 1)
    mixed = jnp.zeros((total, returned[0].shape[1]), jnp.float32)
    for hop in range(4):
        hit = routes == (expert ^ hop).astype(jnp.float32)
        member = jnp.sum(jnp.where(hit, 1.0, 0.0), axis=1, keepdims=True)
        factor = jnp.sum(jnp.where(hit, gates, 0.0), axis=1, keepdims=True)
        place_in = f32_dot(before, jnp.broadcast_to(member, (total, LANES)).astype(jnp.bfloat16))[:, 0:1]
        target = jnp.where(member > 0.5, place_in.astype(jnp.int32) + first_slot, -1)
        placing = jnp.where(slot == target, factor, 0.0)
        upper = placing.astype(jnp.bfloat16)
        lower = (placing - upper.astype(jnp.float32)).astype(jnp.bfloat16)
        mixed = mixed + f32_dot(upper, returned[hop][...]) + f32_dot(lower, returned[hop][...])
    for turn in range(count):
        outs[turn][...] = mixed[turn * tok_rows : (turn + 1) * tok_rows].astype(jnp.bfloat16)


def shards(
    inputs,
    attn_gain,
    w_query,
    w_key,
    w_value,
    w_out,
    sel_blocks,
    ffn_gain,
    w_gate,
    w_up,
    w_down,
    routes,
    gate_weights,
):
    tok_rows, model_width = inputs.shape
    block_len, heads_here, pick_count = sel_blocks.shape
    hidden_cols = w_query.shape[1]
    head_dim = hidden_cols // heads_here
    ctx_count, exp_count = lax.axis_size("ctx"), lax.axis_size("exp")
    depth = ctx_count // 2
    ctx_index, exp_index = lax.axis_index("ctx"), lax.axis_index("exp")
    z_index, x_index = ctx_index // 2, ctx_index % 2
    expert = (ctx_index * exp_count + exp_index) // 2
    by_head = heads_here == depth and block_len <= 3 * head_dim and head_dim == LANES
    place = jnp.stack(
        [exp_index, z_index, exp_index % 2, z_index if by_head else jnp.zeros_like(z_index), expert]
    ).astype(jnp.int32)

    far = move(inputs, lambda z, x, y, c: (z, x, y ^ 1, c))
    near = swap_core(inputs)
    far_near = swap_core(far)
    weights = (w_gate, w_up, w_down)
    other_gate, other_up, other_down = swap_core(w_gate), None, None
    far_near, other_gate = lax.optimization_barrier((far_near, other_gate))
    top_count = routes.shape[1]
    noted = jnp.concatenate([routes.astype(jnp.float32)] + [gate_weights] * 3, axis=1)
    noted = jnp.pad(noted, ((0, 0), (0, LANES - noted.shape[1])))
    if by_head:
        marks = jnp.sum(
            jnp.where(sel_blocks < ctx_index, jnp.left_shift(1, jnp.minimum(sel_blocks, 30)), 0), axis=2
        )
        marks = jnp.pad(marks.T.astype(jnp.bfloat16), ((0, 0), (0, 3 * head_dim - block_len)))
        marks = jnp.broadcast_to(marks[:, None], (heads_here, PAD_ROWS, 3 * head_dim))
        payload = struct(block_len + PAD_ROWS, 3 * head_dim)
        sent = call(
            functools.partial(project_kernel, exp_count, depth, head_dim),
            [payload] * depth,
            [
                place,
                marks,
                *(near, far, far_near),
                *(attn_gain.reshape(1, -1), inputs, w_query, w_key, w_value),
            ],
            [
                pltpu.VMEM((exp_count, tok_rows, model_width), jnp.bfloat16),
                pltpu.VMEM((block_len, model_width), jnp.bfloat16),
                pltpu.VMEM((3, block_len, hidden_cols), jnp.bfloat16),
                pltpu.VMEM((1, model_width), jnp.float32),
                pltpu.VMEM((3, model_width, hidden_cols), jnp.bfloat16),
                pltpu.SemaphoreType.DMA((exp_count + 4,)),
            ],
            flops=6 * block_len * model_width * hidden_cols,
            anywhere=exp_count - 1,
            hbm=5,
        )
        own = [head_out(sent[turn], turn) for turn in range(depth)]
        beside = [swap_core(block) for block in own]
        other_down = swap_core(after(w_down, sent[0]))
        beside[-1], other_down = lax.optimization_barrier((beside[-1], other_down))
        other_up = swap_core(after(w_up, *beside))
        mixed = call(
            functools.partial(attend_kernel, depth, block_len, head_dim),
            [struct(block_len, head_dim)] * depth,
            [place, *own, *beside],
            [
                pltpu.VMEM((depth, block_len + PAD_ROWS, 3 * head_dim), jnp.bfloat16),
                pltpu.VMEM((depth, block_len, 2 * head_dim), jnp.bfloat16),
                pltpu.VMEM((depth, block_len, head_dim), jnp.bfloat16),
            ],
            flops=4 * depth * ctx_count * block_len * block_len * head_dim,
        )
        *mixed, other_up = lax.optimization_barrier((*mixed, other_up))
        heads = [head_back(mixed[turn], turn) for turn in range(depth)]
    else:
        block = jnp.stack([inputs, near, far, far_near])[exp_index ^ jnp.arange(exp_count)]
        normed = normalize(block.reshape(block_len, model_width), attn_gain)
        heads = attend_gathered(normed, w_query, w_key, w_value, sel_blocks)
        other_up, other_down = swap_core(w_up), swap_core(w_down)

    halves = struct(exp_count // 2, tok_rows, model_width)
    kept, given = call(
        functools.partial(mix_kernel, exp_count, heads_here, head_dim),
        [halves, halves],
        [place, *heads, w_out],
        [
            pltpu.VMEM((block_len, hidden_cols), jnp.bfloat16),
            pltpu.VMEM((block_len, model_width), jnp.bfloat16),
        ],
        flops=2 * block_len * model_width * hidden_cols,
    )
    given = swap_core(given)
    here, beyond = call(
        halves_kernel,
        [struct(tok_rows, model_width, dtype=jnp.float32), struct(tok_rows, model_width)],
        [inputs, kept, given],
        smem=0,
    )
    own_weights, other_weights = (
        [gate[0].T, up[0].T, down[0]] for gate, up, down in (weights, (other_gate, other_up, other_down))
    )
    expert_weights = load(other_weights, [after(weight, beyond) for weight in own_weights])
    beyond = move(beyond, lambda z, x, y, c: (z, x, y ^ 1, c))
    beyond, expert_weights = lax.optimization_barrier((beyond, expert_weights))
    residual, ffn_in = call(
        functools.partial(residual_kernel, top_count),
        [struct(tok_rows, model_width), struct(tok_rows, model_width + LANES)],
        [here, beyond, ffn_gain.reshape(1, -1), noted],
        smem=0,
    )

    experts = ctx_count * exp_count // 2
    capacity = 2 * max(1, (tok_rows * top_count + experts - 1) // experts * 2 // 3)
    column = gather_z(ffn_in)
    groups = [[0], [1, depth - 1], list(range(2, depth - 1))]
    arrived, notes = [], []
    for group in groups:
        count = len(group)
        first = column[group[0]]
        if len(arrived) == 1:
            first = after(first, *arrived[0])
        elif arrived:
            first = after(first, arrived[-1][0])
        *packed, note = call(
            functools.partial(pack_kernel, count, capacity, top_count),
            [struct(count * capacity, model_width)] * 4 + [struct(count * tok_rows, LANES)],
            [place, first, *[column[t] for t in group[1:]]],
            [pltpu.VMEM((count * tok_rows, model_width), jnp.bfloat16)],
            flops=8 * count * capacity * count * tok_rows * model_width,
            limit=8 * MIB + 16 * (count * tok_rows) ** 2 + 8 * count * tok_rows * model_width,
        )
        arrived.append([packed[0]] + [swap_layer(packed[hop], hop) for hop in range(1, 4)])
        notes.append(note)

    def expert_rows(rows):
        starts, total = [], 0
        for row in rows:
            starts.append(total)
            total += -(-row.shape[0] // 16) * 16
        return call(
            functools.partial(expert_kernel, starts),
            [struct(*row.shape) for row in rows],
            [*rows, *expert_weights],
            [pltpu.VMEM((total, model_width), jnp.bfloat16)],
            flops=12 * total * model_width * w_gate.shape[2],
            smem=0,
            limit=4 * MIB + 32 * 1024 * total,
        )

    results = [None, expert_rows(arrived[1]), None]
    far_rows = [after(arrived[2][0], results[1][0])] + arrived[2][1:]
    both = expert_rows(arrived[0] + far_rows)
    results[0], results[2] = both[:4], both[4:]
    sums = [None] * depth
    for index in (1, 2, 0):
        group, rows = groups[index], list(results[index])
        if index == 0:
            rows[1:] = [after(row, sums[1]) for row in rows[1:]]
        rows = [rows[0]] + [swap_layer(rows[hop], hop) for hop in range(1, 4)]
        count = len(group)
        total = count * tok_rows
        parts = call(
            functools.partial(combine_kernel, count, capacity, top_count),
            [struct(tok_rows, model_width)] * count,
            [place, notes[index], *rows],
            flops=16 * count * capacity * total * model_width,
            limit=8 * MIB + 16 * total * total + 16 * total * model_width,
        )
        for turn, part in zip(group, parts):
            sums[turn] = part
    layer_out = residual.astype(jnp.float32) + sums[0].astype(jnp.float32)
    for turn in range(1, depth):
        layer_out = layer_out + turn_z(sums[turn], -turn).astype(jnp.float32)
    return layer_out.astype(jnp.bfloat16)


def solution(mesh):
    placed = (
        P(("ctx", "exp"), None),
        P(),
        P(None, "exp"),
        P(None, "exp"),
        P(None, "exp"),
        P("exp", None),
        P("ctx", "exp", None),
        P(),
        P(("ctx", "exp"), None, None),
        P(("ctx", "exp"), None, None),
        P(("ctx", "exp"), None, None),
        P(("ctx", "exp"), None),
        P(("ctx", "exp"), None),
    )
    return jax.shard_map(
        shards, mesh=mesh, in_specs=placed, out_specs=P(("ctx", "exp"), None), check_vma=False
    )
```

```python
import functools
import math

import jax
import jax.numpy as jnp
from jax import lax
from jax.experimental import pallas as pl
from jax.experimental.pallas import tpu as pltpu
from jax.sharding import PartitionSpec as P

AXES = ("ctx", "exp")
MIB = 1024 * 1024
VMEM = pl.BlockSpec(memory_space=pltpu.VMEM)
SMEM = pl.BlockSpec(memory_space=pltpu.SMEM)
ANY = pl.BlockSpec(memory_space=pl.ANY)
HBM = pl.BlockSpec(memory_space=pltpu.HBM)
PAD_ROWS = 16
LANES = 128


def move(block, target):
    ctx_count, exp_count = lax.axis_size("ctx"), lax.axis_size("exp")
    route = []
    for ctx in range(ctx_count):
        for exp in range(exp_count):
            z, x, y, c = target(ctx // 2, ctx % 2, exp // 2, exp % 2)
            route.append((ctx * exp_count + exp, (z * 2 + x) * exp_count + y * 2 + c))
    return lax.ppermute(block, AXES, route)


def swap_core(block):
    return move(block, lambda z, x, y, c: (z, x, y, c ^ 1))


def swap_layer(block, hop):
    return move(block, lambda z, x, y, c: (z, x ^ (hop >> 1), y ^ (hop & 1), c))


def turn_z(block, turn):
    depth = lax.axis_size("ctx") // 2
    return move(block, lambda z, x, y, c: ((z + turn) % depth, x, y, c))


def gather_z(block):
    depth = lax.axis_size("ctx") // 2
    column = [block] + [None] * (depth - 1)
    for turn in range(1, depth // 2 + 1):
        column[turn] = turn_z(column[turn - 1], 1)
    for turn in range(depth - 1, depth // 2, -1):
        column[turn] = turn_z(column[(turn + 1) % depth], -1)
    return column


def head_out(block, turn):
    depth = lax.axis_size("ctx") // 2
    return move(block, lambda z, x, y, c: ((z + turn) % depth, c, y, x))


def head_back(block, turn):
    depth = lax.axis_size("ctx") // 2
    return move(block, lambda z, x, y, c: ((z - turn) % depth, c, y, x))


def normalize(values, gain_vec):
    floats = values.astype(jnp.float32)
    factor = lax.rsqrt(jnp.mean(floats * floats, axis=-1, keepdims=True) + 1e-06)
    return (floats * factor * gain_vec).astype(jnp.bfloat16)


def f32_dot(left, right):
    return jnp.dot(left, right, preferred_element_type=jnp.float32)


def struct(*shape, dtype=jnp.bfloat16):
    return pltpu.VMEM(shape, dtype)


def call(kernel, outs, operands, scratch=(), flops=0, smem=1, anywhere=0, hbm=0, limit=16 * MIB):
    far = len(operands) - hbm
    last = far - anywhere
    operands = [
        pltpu.with_memory_space_constraint(a, pltpu.VMEM if i < last else pltpu.HBM)
        if smem <= i < last or i >= far
        else a
        for i, a in enumerate(operands)
    ]
    return pl.pallas_call(
        kernel,
        out_shape=outs,
        in_specs=[SMEM] * smem + [VMEM] * (last - smem) + [ANY] * anywhere + [HBM] * hbm,
        out_specs=jax.tree.map(lambda _: VMEM, outs),
        scratch_shapes=list(scratch),
        compiler_params=pltpu.CompilerParams(vmem_limit_bytes=limit),
        cost_estimate=pl.CostEstimate(
            flops=flops,
            bytes_accessed=sum(a.size * a.dtype.itemsize for a in operands),
            transcendentals=0,
        ),
    )(*operands)


def after(value, *others):
    return lax.optimization_barrier((value, *others))[0]


def load_kernel(count, *refs):
    sources, targets, sems = refs[:count], refs[count : 2 * count], refs[2 * count]
    copies = [
        pltpu.make_async_copy(sources[i], targets[i], sems.at[i]) for i in range(count)
    ]
    for copy in copies:
        copy.start()
    for copy in copies:
        copy.wait()


def load(received, held):
    arrays = [*received, *held]
    return call(
        functools.partial(load_kernel, len(arrays)),
        [struct(*a.shape) for a in arrays],
        arrays,
        [pltpu.SemaphoreType.DMA((len(arrays),))],
        smem=0,
        anywhere=len(received),
        hbm=len(held),
        limit=MIB,
    )


def project_kernel(hops, depth, head_dim, place, marks, *refs):
    sources, outs = refs[: hops + 4], refs[hops + 4 : hops + 4 + depth]
    given, rows, mixed, gain, held, sems = refs[hops + 4 + depth :]
    exp_index, z_index = place[0], place[1]
    tok_rows = given.shape[1]
    block_len = hops * tok_rows
    targets = [*(given.at[i] for i in range(1, hops)), gain, given.at[0], *(held.at[i] for i in range(3))]
    copies = [pltpu.make_async_copy(sources[i], targets[i], sems.at[i]) for i in range(hops + 4)]
    for copy in copies:
        copy.start()
    for copy in copies[: hops + 1]:
        copy.wait()
    for hop in range(hops):
        start = pl.multiple_of((exp_index ^ hop) * tok_rows, 16)
        rows[pl.ds(start, tok_rows), :] = normalize(given[hop], gain[...])
    for part, copy in enumerate(copies[hops + 1 :]):
        copy.wait()
        mixed[part] = f32_dot(rows[...], held[part]).astype(jnp.bfloat16)
    for turn in range(depth):
        head = lax.rem(z_index + turn, depth)
        columns = pl.ds(pl.multiple_of(head * head_dim, head_dim), head_dim)
        for part in range(3):
            outs[turn][0:block_len, part * head_dim : (part + 1) * head_dim] = mixed[part, :, columns]
        outs[turn][block_len : block_len + PAD_ROWS, :] = marks[head]


def attend_kernel(depth, block_len, head_dim, place, *refs):
    own_refs, near_refs = refs[:depth], refs[depth : 2 * depth]
    outs, (own, near, mixed) = refs[2 * depth : 3 * depth], refs[3 * depth :]
    z_index, core = place[1], place[2]
    scaling = math.log2(math.e) / math.sqrt(head_dim)
    for turn in range(depth):
        source = lax.rem(z_index + depth - turn, depth)
        own[source] = own_refs[turn][...]
        near[source] = near_refs[turn][0:block_len, head_dim : 3 * head_dim]
    key_pos = lax.broadcasted_iota(jnp.int32, (block_len, block_len), 0)
    query_pos = lax.broadcasted_iota(jnp.int32, (block_len, block_len), 1)
    causal = jnp.where(key_pos <= query_pos, 0.0, -1e30)
    for level in range(depth):
        query = own[level, 0:block_len, 0:head_dim]
        marks = own[level, block_len : block_len + PAD_ROWS, 0:block_len].astype(jnp.float32)
        marks = marks[0:1].astype(jnp.int32)
        run_max = run_sum = total = None
        order = [(level, True)] + [(c, True) for c in range(level)] + [(c, False) for c in range(level + 1)]
        for c, mine in order:
            if mine:
                key = own[c, 0:block_len, head_dim : 2 * head_dim]
                value = own[c, 0:block_len, 2 * head_dim : 3 * head_dim]
            else:
                key, value = near[c, :, 0:head_dim], near[c, :, head_dim : 2 * head_dim]
            scores = lax.dot_general(
                key, query, (((1,), (1,)), ((), ())), preferred_element_type=jnp.float32
            )
            if run_max is None:
                scores = scores + causal
                shift = run_max = jnp.max(scores, axis=0, keepdims=True)
            else:
                bit = 2 * c + (core if mine else 1 - core)
                chosen = lax.shift_right_logical(marks, jnp.broadcast_to(bit, marks.shape)) & 1
                top = jnp.where(chosen == 1, jnp.max(scores, axis=0, keepdims=True), -1e30)
                new_max = jnp.maximum(run_max, top)
                rescale = jnp.exp2((run_max - new_max) * scaling)
                run_max = new_max
                shift = jnp.where(chosen == 1, new_max, 1e30)
            weights = jnp.exp2((scores - shift) * scaling)
            added = jnp.sum(weights, axis=0, keepdims=True)
            product = lax.dot_general(
                value,
                weights.astype(jnp.bfloat16),
                (((0,), (0,)), ((), ())),
                preferred_element_type=jnp.float32,
            )
            if total is None:
                run_sum, total = added, product
            else:
                run_sum, total = run_sum * rescale + added, total * rescale + product
        mixed[level] = (total / run_sum).T.astype(jnp.bfloat16)
    for turn in range(depth):
        outs[turn][...] = mixed[lax.rem(z_index + depth - turn, depth)]


def attend_gathered(normed_block, w_query, w_key, w_value, sel_blocks):
    block_len, heads_here, _ = sel_blocks.shape
    hidden_cols = w_query.shape[1]
    head_dim = hidden_cols // heads_here
    ctx_count, ctx_index = lax.axis_size("ctx"), lax.axis_index("ctx")
    query_part, key_part, value_part = (
        f32_dot(normed_block, weight).astype(jnp.bfloat16) for weight in (w_query, w_key, w_value)
    )
    queries = query_part.reshape(block_len, heads_here, head_dim)
    keys_values = jnp.stack([key_part, value_part], axis=1)
    block_ids = jnp.arange(ctx_count, dtype=jnp.int32)
    chosen = jnp.any(sel_blocks[:, :, :, None] == block_ids, axis=2) & (block_ids < ctx_index)
    position = jnp.arange(block_len, dtype=jnp.int32)
    causal = position[None, :] <= position[:, None]
    scaling = 1.0 / math.sqrt(head_dim)

    def fold_step(running, operands):
        run_max, run_sum, totals = running
        piece, block = operands
        key_rows = piece[:, 0].reshape(block_len, heads_here, head_dim)
        value_rows = piece[:, 1].reshape(block_len, heads_here, head_dim)
        scores = (
            jnp.einsum("qhd,khd->hqk", queries, key_rows, preferred_element_type=jnp.float32)
            * scaling
        )
        picked = jnp.take(chosen, block, axis=2).T[:, :, None]
        allowed = picked | ((block == ctx_index) & causal)[None]
        new_max = jnp.maximum(run_max, jnp.max(jnp.where(allowed, scores, -jnp.inf), axis=-1))
        weights = jnp.where(allowed, jnp.exp(scores - new_max[..., None]), 0.0)
        rescale = jnp.exp(run_max - new_max)
        run_sum = run_sum * rescale + jnp.sum(weights, axis=-1)
        totals = totals * rescale[..., None] + jnp.einsum(
            "hqk,khd->hqd",
            weights.astype(jnp.bfloat16),
            value_rows,
            preferred_element_type=jnp.float32,
        )
        return (new_max, run_sum, totals), None

    initial = (
        jnp.full((heads_here, block_len), -1e30, jnp.float32),
        jnp.zeros((heads_here, block_len), jnp.float32),
        jnp.zeros((heads_here, block_len, head_dim), jnp.float32),
    )
    gathered = lax.all_gather(keys_values, "ctx", axis=0)
    (_, run_sum, totals), _ = lax.scan(fold_step, initial, (gathered, block_ids))
    attended = (totals / run_sum[..., None]).astype(jnp.bfloat16)
    return [attended[head] for head in range(heads_here)]


def mix_kernel(hops, heads, head_dim, place, *refs):
    head_refs, w_out = refs[:heads], refs[heads]
    kept, given, attended, mixed = refs[heads + 1 :]
    exp_index, turned = place[0], place[3]
    tok_rows = kept.shape[1]
    for turn, head_ref in enumerate(head_refs):
        head = lax.rem(turned + turn, heads)
        attended[:, pl.ds(pl.multiple_of(head * head_dim, head_dim), head_dim)] = head_ref[...]
    mixed[...] = f32_dot(attended[...], w_out[...]).astype(jnp.bfloat16)
    for hop in range(hops):
        start = pl.multiple_of((exp_index ^ hop) * tok_rows, 16)
        (given if hop & 1 else kept)[hop >> 1] = mixed[pl.ds(start, tok_rows), :]


def halves_kernel(inputs, kept, given, here, beyond):
    summed = kept[0].astype(jnp.float32) + given[0].astype(jnp.float32)
    here[...] = inputs[...].astype(jnp.float32) + summed
    beyond[...] = (kept[1].astype(jnp.float32) + given[1].astype(jnp.float32)).astype(jnp.bfloat16)


def residual_kernel(top_count, here, far, gain, noted, residual, ffn_in):
    rounded = (here[...] + far[...].astype(jnp.float32)).astype(jnp.bfloat16)
    residual[...] = rounded
    model_width = rounded.shape[1]
    ffn_in[:, 0:model_width] = normalize(rounded, gain[...])
    lane = lax.broadcasted_iota(jnp.int32, noted.shape, 1)
    left = noted[...]
    upper = left.astype(jnp.bfloat16).astype(jnp.float32)
    left = left - upper
    middle = left.astype(jnp.bfloat16).astype(jnp.float32)
    lower = left - middle
    parts = jnp.where(lane < 2 * top_count, upper, jnp.where(lane < 3 * top_count, middle, lower))
    ffn_in[:, model_width:] = parts.astype(jnp.bfloat16)


def pack_kernel(count, capacity, top_count, place, *refs):
    sources, outs, (notes, rows) = refs[:count], refs[count : count + 4], refs[count + 4 :]
    expert = place[4]
    tok_rows = sources[0].shape[0]
    total = count * tok_rows
    model_width = rows.shape[1]
    for turn in range(count):
        part = slice(turn * tok_rows, (turn + 1) * tok_rows)
        rows[part, :] = sources[turn][:, 0:model_width]
        notes[part, :] = sources[turn][:, model_width:]
    routes = notes[...].astype(jnp.float32).T[0:8]
    routes = jnp.where(lax.broadcasted_iota(jnp.int32, routes.shape, 0) < top_count, routes, -1.0)
    earlier = lax.broadcasted_iota(jnp.int32, (total, total), 0)
    later = lax.broadcasted_iota(jnp.int32, (total, total), 1)
    before = ((earlier < later) & (earlier // tok_rows == later // tok_rows)).astype(jnp.bfloat16)
    first_slot = lax.broadcasted_iota(jnp.int32, (1, total), 1) // tok_rows * capacity
    slot = lax.broadcasted_iota(jnp.int32, (count * capacity, total), 0)
    for hop in range(4):
        hit = jnp.where(routes == (expert ^ hop).astype(jnp.float32), 1.0, 0.0)
        member = jnp.sum(hit, axis=0, keepdims=True)
        place_in = f32_dot(jnp.broadcast_to(member, (16, total)).astype(jnp.bfloat16), before)[0:1]
        target = jnp.where(member > 0.5, place_in.astype(jnp.int32) + first_slot, -1)
        placing = jnp.where(slot == target, 1.0, 0.0).astype(jnp.bfloat16)
        outs[hop][...] = f32_dot(placing, rows[...]).astype(jnp.bfloat16)


def expert_kernel(starts, *refs):
    parts = len(starts)
    row_refs, weights = refs[:parts], refs[parts : parts + 6]
    outs, (held,) = refs[parts + 6 : 2 * parts + 6], refs[2 * parts + 6 :]
    across = (((1,), (1,)), ((), ()))
    for start, row_ref in zip(starts, row_refs):
        held[start : start + row_ref.shape[0], :] = row_ref[...]
    rows = held[...]
    result = None
    for w_gate, w_up, w_down in (weights[:3], weights[3:]):
        gate_part = lax.dot_general(rows, w_gate[...], across, preferred_element_type=jnp.float32)
        up_part = lax.dot_general(rows, w_up[...], across, preferred_element_type=jnp.float32)
        hidden = (gate_part / (1.0 + jnp.exp(-gate_part)) * up_part).astype(jnp.bfloat16)
        product = f32_dot(hidden, w_down[...])
        result = product if result is None else result + product
    for start, out in zip(starts, outs):
        out[...] = result[start : start + out.shape[0]].astype(jnp.bfloat16)


def combine_kernel(count, capacity, top_count, place, notes, *refs):
    returned, outs = refs[:4], refs[4 : 4 + count]
    expert = place[4]
    total = notes.shape[0]
    tok_rows = total // count
    row = lax.broadcasted_iota(jnp.int32, (LANES, LANES), 0)
    lane = lax.broadcasted_iota(jnp.int32, (LANES, LANES), 1)
    added = (lane < top_count) & (row >= top_count) & (row < 4 * top_count) & (row % top_count == lane)
    gates = f32_dot(notes[...], jnp.where(added, 1.0, 0.0).astype(jnp.bfloat16))
    routes = notes[...].astype(jnp.float32)
    routes = jnp.where(lax.broadcasted_iota(jnp.int32, routes.shape, 1) < top_count, routes, -1.0)
    later = lax.broadcasted_iota(jnp.int32, (total, total), 0)
    earlier = lax.broadcasted_iota(jnp.int32, (total, total), 1)
    before = ((earlier < later) & (earlier // tok_rows == later // tok_rows)).astype(jnp.bfloat16)
    first_slot = lax.broadcasted_iota(jnp.int32, (total, 1), 0) // tok_rows * capacity
    slot = lax.broadcasted_iota(jnp.int32, (total, count * capacity), 1)
    mixed = jnp.zeros((total, returned[0].shape[1]), jnp.float32)
    for hop in range(4):
        hit = routes == (expert ^ hop).astype(jnp.float32)
        member = jnp.sum(jnp.where(hit, 1.0, 0.0), axis=1, keepdims=True)
        factor = jnp.sum(jnp.where(hit, gates, 0.0), axis=1, keepdims=True)
        place_in = f32_dot(before, jnp.broadcast_to(member, (total, LANES)).astype(jnp.bfloat16))[:, 0:1]
        target = jnp.where(member > 0.5, place_in.astype(jnp.int32) + first_slot, -1)
        placing = jnp.where(slot == target, factor, 0.0)
        upper = placing.astype(jnp.bfloat16)
        lower = (placing - upper.astype(jnp.float32)).astype(jnp.bfloat16)
        mixed = mixed + f32_dot(upper, returned[hop][...]) + f32_dot(lower, returned[hop][...])
    for turn in range(count):
        outs[turn][...] = mixed[turn * tok_rows : (turn + 1) * tok_rows].astype(jnp.bfloat16)


def shards(
    inputs,
    attn_gain,
    w_query,
    w_key,
    w_value,
    w_out,
    sel_blocks,
    ffn_gain,
    w_gate,
    w_up,
    w_down,
    routes,
    gate_weights,
):
    tok_rows, model_width = inputs.shape
    block_len, heads_here, pick_count = sel_blocks.shape
    hidden_cols = w_query.shape[1]
    head_dim = hidden_cols // heads_here
    ctx_count, exp_count = lax.axis_size("ctx"), lax.axis_size("exp")
    depth = ctx_count // 2
    ctx_index, exp_index = lax.axis_index("ctx"), lax.axis_index("exp")
    z_index, x_index = ctx_index // 2, ctx_index % 2
    expert = (ctx_index * exp_count + exp_index) // 2
    by_head = heads_here == depth and block_len <= 3 * head_dim and head_dim == LANES
    place = jnp.stack(
        [exp_index, z_index, exp_index % 2, z_index if by_head else jnp.zeros_like(z_index), expert]
    ).astype(jnp.int32)

    far = move(inputs, lambda z, x, y, c: (z, x, y ^ 1, c))
    near = swap_core(inputs)
    far_near = swap_core(far)
    weights = (w_gate, w_up, w_down)
    other_gate, other_up, other_down = swap_core(w_gate), None, swap_core(w_down)
    far_near, other_gate, other_down = lax.optimization_barrier((far_near, other_gate, other_down))
    top_count = routes.shape[1]
    noted = jnp.concatenate([routes.astype(jnp.float32)] + [gate_weights] * 3, axis=1)
    noted = jnp.pad(noted, ((0, 0), (0, LANES - noted.shape[1])))
    if by_head:
        marks = jnp.sum(
            jnp.where(sel_blocks < ctx_index, jnp.left_shift(1, jnp.minimum(sel_blocks, 30)), 0), axis=2
        )
        marks = jnp.pad(marks.T.astype(jnp.bfloat16), ((0, 0), (0, 3 * head_dim - block_len)))
        marks = jnp.broadcast_to(marks[:, None], (heads_here, PAD_ROWS, 3 * head_dim))
        payload = struct(block_len + PAD_ROWS, 3 * head_dim)
        sent = call(
            functools.partial(project_kernel, exp_count, depth, head_dim),
            [payload] * depth,
            [
                place,
                marks,
                *(near, far, far_near),
                *(attn_gain.reshape(1, -1), inputs, w_query, w_key, w_value),
            ],
            [
                pltpu.VMEM((exp_count, tok_rows, model_width), jnp.bfloat16),
                pltpu.VMEM((block_len, model_width), jnp.bfloat16),
                pltpu.VMEM((3, block_len, hidden_cols), jnp.bfloat16),
                pltpu.VMEM((1, model_width), jnp.float32),
                pltpu.VMEM((3, model_width, hidden_cols), jnp.bfloat16),
                pltpu.SemaphoreType.DMA((exp_count + 4,)),
            ],
            flops=6 * block_len * model_width * hidden_cols,
            anywhere=exp_count - 1,
            hbm=5,
        )
        own = [head_out(sent[turn], turn) for turn in range(depth)]
        beside = [swap_core(block) for block in own]
        mixed = call(
            functools.partial(attend_kernel, depth, block_len, head_dim),
            [struct(block_len, head_dim)] * depth,
            [place, *own, *beside],
            [
                pltpu.VMEM((depth, block_len + PAD_ROWS, 3 * head_dim), jnp.bfloat16),
                pltpu.VMEM((depth, block_len, 2 * head_dim), jnp.bfloat16),
                pltpu.VMEM((depth, block_len, head_dim), jnp.bfloat16),
            ],
            flops=4 * depth * ctx_count * block_len * block_len * head_dim,
        )
        heads = [head_back(mixed[turn], turn) for turn in range(depth)]
    else:
        block = jnp.stack([inputs, near, far, far_near])[exp_index ^ jnp.arange(exp_count)]
        normed = normalize(block.reshape(block_len, model_width), attn_gain)
        heads = attend_gathered(normed, w_query, w_key, w_value, sel_blocks)

    halves = struct(exp_count // 2, tok_rows, model_width)
    kept, given = call(
        functools.partial(mix_kernel, exp_count, heads_here, head_dim),
        [halves, halves],
        [place, *heads, w_out],
        [
            pltpu.VMEM((block_len, hidden_cols), jnp.bfloat16),
            pltpu.VMEM((block_len, model_width), jnp.bfloat16),
        ],
        flops=2 * block_len * model_width * hidden_cols,
    )
    given = swap_core(given)
    here, beyond = call(
        halves_kernel,
        [struct(tok_rows, model_width, dtype=jnp.float32), struct(tok_rows, model_width)],
        [inputs, kept, given],
        smem=0,
    )
    other_up = swap_core(after(w_up, beyond))
    own_weights, other_weights = (
        [gate[0].T, up[0].T, down[0]] for gate, up, down in (weights, (other_gate, other_up, other_down))
    )
    g, u, d = other_weights
    *own, g, d = load([], [after(weight, beyond) for weight in [*own_weights, g, d]])
    expert_weights = [*own, g, u, d]
    beyond = move(beyond, lambda z, x, y, c: (z, x, y ^ 1, c))
    beyond, expert_weights = lax.optimization_barrier((beyond, expert_weights))
    residual, ffn_in = call(
        functools.partial(residual_kernel, top_count),
        [struct(tok_rows, model_width), struct(tok_rows, model_width + LANES)],
        [here, beyond, ffn_gain.reshape(1, -1), noted],
        smem=0,
    )

    experts = ctx_count * exp_count // 2
    capacity = 2 * max(1, (tok_rows * top_count + experts - 1) // experts * 2 // 3)
    column = gather_z(ffn_in)
    groups = [[0], [1, depth - 1], list(range(2, depth - 1))]
    arrived, notes = [], []
    for group in groups:
        count = len(group)
        first = column[group[0]]
        if len(arrived) == 1:
            first = after(first, *arrived[0])
        elif arrived:
            first = after(first, arrived[-1][0])
        *packed, note = call(
            functools.partial(pack_kernel, count, capacity, top_count),
            [struct(count * capacity, model_width)] * 4 + [struct(count * tok_rows, LANES)],
            [place, first, *[column[t] for t in group[1:]]],
            [pltpu.VMEM((count * tok_rows, model_width), jnp.bfloat16)],
            flops=8 * count * capacity * count * tok_rows * model_width,
            limit=8 * MIB + 16 * (count * tok_rows) ** 2 + 8 * count * tok_rows * model_width,
        )
        arrived.append([packed[0]] + [swap_layer(packed[hop], hop) for hop in range(1, 4)])
        notes.append(note)

    def expert_rows(rows):
        starts, total = [], 0
        for row in rows:
            starts.append(total)
            total += -(-row.shape[0] // 16) * 16
        return call(
            functools.partial(expert_kernel, starts),
            [struct(*row.shape) for row in rows],
            [*rows, *expert_weights],
            [pltpu.VMEM((total, model_width), jnp.bfloat16)],
            flops=12 * total * model_width * w_gate.shape[2],
            smem=0,
            limit=4 * MIB + 32 * 1024 * total,
        )

    results = [None, expert_rows(arrived[1]), None]
    far_rows = [after(arrived[2][0], results[1][0])] + arrived[2][1:]
    both = expert_rows(arrived[0] + far_rows)
    results[0], results[2] = both[:4], both[4:]
    sums = [None] * depth
    for index in (1, 2, 0):
        group, rows = groups[index], list(results[index])
        if index == 0:
            rows[1:] = [after(row, sums[1]) for row in rows[1:]]
        rows = [rows[0]] + [swap_layer(rows[hop], hop) for hop in range(1, 4)]
        count = len(group)
        total = count * tok_rows
        parts = call(
            functools.partial(combine_kernel, count, capacity, top_count),
            [struct(tok_rows, model_width)] * count,
            [place, notes[index], *rows],
            flops=16 * count * capacity * total * model_width,
            limit=8 * MIB + 16 * total * total + 16 * total * model_width,
        )
        for turn, part in zip(group, parts):
            sums[turn] = part
    layer_out = residual.astype(jnp.float32) + sums[0].astype(jnp.float32)
    for turn in range(1, depth):
        layer_out = layer_out + turn_z(sums[turn], -turn).astype(jnp.float32)
    return layer_out.astype(jnp.bfloat16)


def solution(mesh):
    placed = (
        P(("ctx", "exp"), None),
        P(),
        P(None, "exp"),
        P(None, "exp"),
        P(None, "exp"),
        P("exp", None),
        P("ctx", "exp", None),
        P(),
        P(("ctx", "exp"), None, None),
        P(("ctx", "exp"), None, None),
        P(("ctx", "exp"), None, None),
        P(("ctx", "exp"), None),
        P(("ctx", "exp"), None),
    )
    return jax.shard_map(
        shards, mesh=mesh, in_specs=placed, out_specs=P(("ctx", "exp"), None), check_vma=False
    )
```

```python
import functools
import math

import jax
import jax.numpy as jnp
from jax import lax
from jax.experimental import pallas as pl
from jax.experimental.pallas import tpu as pltpu
from jax.sharding import PartitionSpec as P

AXES = ("ctx", "exp")
MIB = 1024 * 1024
VMEM = pl.BlockSpec(memory_space=pltpu.VMEM)
SMEM = pl.BlockSpec(memory_space=pltpu.SMEM)
ANY = pl.BlockSpec(memory_space=pl.ANY)
HBM = pl.BlockSpec(memory_space=pltpu.HBM)
PAD_ROWS = 16
LANES = 128


def move(block, target):
    ctx_count, exp_count = lax.axis_size("ctx"), lax.axis_size("exp")
    route = []
    for ctx in range(ctx_count):
        for exp in range(exp_count):
            z, x, y, c = target(ctx // 2, ctx % 2, exp // 2, exp % 2)
            route.append((ctx * exp_count + exp, (z * 2 + x) * exp_count + y * 2 + c))
    return lax.ppermute(block, AXES, route)


def swap_core(block):
    return move(block, lambda z, x, y, c: (z, x, y, c ^ 1))


def swap_layer(block, hop):
    return move(block, lambda z, x, y, c: (z, x ^ (hop >> 1), y ^ (hop & 1), c))


def turn_z(block, turn):
    depth = lax.axis_size("ctx") // 2
    return move(block, lambda z, x, y, c: ((z + turn) % depth, x, y, c))


def gather_z(block):
    depth = lax.axis_size("ctx") // 2
    column = [block] + [None] * (depth - 1)
    for turn in range(1, depth // 2 + 1):
        column[turn] = turn_z(column[turn - 1], 1)
    for turn in range(depth - 1, depth // 2, -1):
        column[turn] = turn_z(column[(turn + 1) % depth], -1)
    return column


def head_out(block, turn):
    depth = lax.axis_size("ctx") // 2
    return move(block, lambda z, x, y, c: ((z + turn) % depth, c, y, x))


def head_back(block, turn):
    depth = lax.axis_size("ctx") // 2
    return move(block, lambda z, x, y, c: ((z - turn) % depth, c, y, x))


def normalize(values, gain_vec):
    floats = values.astype(jnp.float32)
    factor = lax.rsqrt(jnp.mean(floats * floats, axis=-1, keepdims=True) + 1e-06)
    return (floats * factor * gain_vec).astype(jnp.bfloat16)


def f32_dot(left, right):
    return jnp.dot(left, right, preferred_element_type=jnp.float32)


def struct(*shape, dtype=jnp.bfloat16):
    return pltpu.VMEM(shape, dtype)


def call(kernel, outs, operands, scratch=(), flops=0, smem=1, anywhere=0, hbm=0, limit=16 * MIB):
    far = len(operands) - hbm
    last = far - anywhere
    operands = [
        pltpu.with_memory_space_constraint(a, pltpu.VMEM if i < last else pltpu.HBM)
        if smem <= i < last or i >= far
        else a
        for i, a in enumerate(operands)
    ]
    return pl.pallas_call(
        kernel,
        out_shape=outs,
        in_specs=[SMEM] * smem + [VMEM] * (last - smem) + [ANY] * anywhere + [HBM] * hbm,
        out_specs=jax.tree.map(lambda _: VMEM, outs),
        scratch_shapes=list(scratch),
        compiler_params=pltpu.CompilerParams(vmem_limit_bytes=limit),
        cost_estimate=pl.CostEstimate(
            flops=flops,
            bytes_accessed=sum(a.size * a.dtype.itemsize for a in operands),
            transcendentals=0,
        ),
    )(*operands)


def after(value, *others):
    return lax.optimization_barrier((value, *others))[0]


def load_kernel(count, *refs):
    sources, targets, sems = refs[:count], refs[count : 2 * count], refs[2 * count]
    copies = [
        pltpu.make_async_copy(sources[i], targets[i], sems.at[i]) for i in range(count)
    ]
    for copy in copies:
        copy.start()
    for copy in copies:
        copy.wait()


def load(received, held):
    arrays = [*received, *held]
    return call(
        functools.partial(load_kernel, len(arrays)),
        [struct(*a.shape) for a in arrays],
        arrays,
        [pltpu.SemaphoreType.DMA((len(arrays),))],
        smem=0,
        anywhere=len(received),
        hbm=len(held),
        limit=MIB,
    )


def project_kernel(hops, depth, head_dim, place, marks, *refs):
    sources, outs = refs[: hops + 4], refs[hops + 4 : hops + 4 + depth]
    given, rows, mixed, gain, held, sems = refs[hops + 4 + depth :]
    exp_index, z_index = place[0], place[1]
    tok_rows = given.shape[1]
    block_len = hops * tok_rows
    targets = [*(given.at[i] for i in range(1, hops)), gain, given.at[0], *(held.at[i] for i in range(3))]
    copies = [pltpu.make_async_copy(sources[i], targets[i], sems.at[i]) for i in range(hops + 4)]
    for copy in copies:
        copy.start()
    for copy in copies[: hops + 1]:
        copy.wait()
    for hop in range(hops):
        start = pl.multiple_of((exp_index ^ hop) * tok_rows, 16)
        rows[pl.ds(start, tok_rows), :] = normalize(given[hop], gain[...])
    for part, copy in enumerate(copies[hops + 1 :]):
        copy.wait()
        mixed[part] = f32_dot(rows[...], held[part]).astype(jnp.bfloat16)
    for turn in range(depth):
        head = lax.rem(z_index + turn, depth)
        columns = pl.ds(pl.multiple_of(head * head_dim, head_dim), head_dim)
        for part in range(3):
            outs[turn][0:block_len, part * head_dim : (part + 1) * head_dim] = mixed[part, :, columns]
        outs[turn][block_len : block_len + PAD_ROWS, :] = marks[head]


def attend_kernel(depth, block_len, head_dim, place, *refs):
    own_refs, near_refs, outs = refs[:depth], refs[depth : 2 * depth], refs[2 * depth : 3 * depth]
    queries, keys, values, chosen_rows, scores, mixed = refs[3 * depth :]
    z_index, core = place[1], place[2]
    scaling = math.log2(math.e) / math.sqrt(head_dim)
    width = values.shape[2] // 2
    for turn in range(depth):
        source = lax.rem(z_index + depth - turn, depth)
        queries[source] = own_refs[turn][0:block_len, 0:head_dim]
        chosen_rows[source] = own_refs[turn][block_len : block_len + PAD_ROWS, :]
        for side, ref in enumerate((own_refs[turn], near_refs[turn])):
            keys[source, side * block_len : (side + 1) * block_len] = ref[0:block_len, head_dim : 2 * head_dim]
            values[source, :, side * width : side * width + block_len] = ref[
                0:block_len, 2 * head_dim : 3 * head_dim
            ].T
    key_pos = lax.broadcasted_iota(jnp.int32, (block_len, block_len), 0)
    query_pos = lax.broadcasted_iota(jnp.int32, (block_len, block_len), 1)
    causal = jnp.where(key_pos <= query_pos, 0.0, -1e30)
    for level in range(depth):
        query = queries[level]
        marks = chosen_rows[level, :, 0:block_len].astype(jnp.float32)[0:1].astype(jnp.int32)
        pairs = [(c, side) for c in range(level + 1) for side in range(2)]
        run_max, chosen = None, []
        for index, (c, side) in enumerate(pairs):
            score = lax.dot_general(
                keys[c, side * block_len : (side + 1) * block_len],
                query,
                (((1,), (1,)), ((), ())),
                preferred_element_type=jnp.float32,
            )
            if c == level and side == 0:
                score = score + causal
                chosen.append(None)
                top = jnp.max(score, axis=0, keepdims=True)
            else:
                bit = 2 * c + (core if side == 0 else 1 - core)
                picked = lax.shift_right_logical(marks, jnp.broadcast_to(bit, marks.shape)) & 1
                chosen.append(picked == 1)
                top = jnp.where(chosen[-1], jnp.max(score, axis=0, keepdims=True), -1e30)
            scores[index] = score
            run_max = top if run_max is None else jnp.maximum(run_max, top)
        run_sum = total = None
        for index, (c, side) in enumerate(pairs):
            shift = run_max if chosen[index] is None else jnp.where(chosen[index], run_max, 1e30)
            weights = jnp.exp2((scores[index] - shift) * scaling)
            added = jnp.sum(weights, axis=0, keepdims=True)
            product = f32_dot(
                values[c, :, side * width : side * width + block_len], weights.astype(jnp.bfloat16)
            )
            run_sum = added if run_sum is None else run_sum + added
            total = product if total is None else total + product
        mixed[level] = (total / run_sum).T.astype(jnp.bfloat16)
    for turn in range(depth):
        outs[turn][...] = mixed[lax.rem(z_index + depth - turn, depth)]


def attend_gathered(normed_block, w_query, w_key, w_value, sel_blocks):
    block_len, heads_here, _ = sel_blocks.shape
    hidden_cols = w_query.shape[1]
    head_dim = hidden_cols // heads_here
    ctx_count, ctx_index = lax.axis_size("ctx"), lax.axis_index("ctx")
    query_part, key_part, value_part = (
        f32_dot(normed_block, weight).astype(jnp.bfloat16) for weight in (w_query, w_key, w_value)
    )
    queries = query_part.reshape(block_len, heads_here, head_dim)
    keys_values = jnp.stack([key_part, value_part], axis=1)
    block_ids = jnp.arange(ctx_count, dtype=jnp.int32)
    chosen = jnp.any(sel_blocks[:, :, :, None] == block_ids, axis=2) & (block_ids < ctx_index)
    position = jnp.arange(block_len, dtype=jnp.int32)
    causal = position[None, :] <= position[:, None]
    scaling = 1.0 / math.sqrt(head_dim)

    def fold_step(running, operands):
        run_max, run_sum, totals = running
        piece, block = operands
        key_rows = piece[:, 0].reshape(block_len, heads_here, head_dim)
        value_rows = piece[:, 1].reshape(block_len, heads_here, head_dim)
        scores = (
            jnp.einsum("qhd,khd->hqk", queries, key_rows, preferred_element_type=jnp.float32)
            * scaling
        )
        picked = jnp.take(chosen, block, axis=2).T[:, :, None]
        allowed = picked | ((block == ctx_index) & causal)[None]
        new_max = jnp.maximum(run_max, jnp.max(jnp.where(allowed, scores, -jnp.inf), axis=-1))
        weights = jnp.where(allowed, jnp.exp(scores - new_max[..., None]), 0.0)
        rescale = jnp.exp(run_max - new_max)
        run_sum = run_sum * rescale + jnp.sum(weights, axis=-1)
        totals = totals * rescale[..., None] + jnp.einsum(
            "hqk,khd->hqd",
            weights.astype(jnp.bfloat16),
            value_rows,
            preferred_element_type=jnp.float32,
        )
        return (new_max, run_sum, totals), None

    initial = (
        jnp.full((heads_here, block_len), -1e30, jnp.float32),
        jnp.zeros((heads_here, block_len), jnp.float32),
        jnp.zeros((heads_here, block_len, head_dim), jnp.float32),
    )
    gathered = lax.all_gather(keys_values, "ctx", axis=0)
    (_, run_sum, totals), _ = lax.scan(fold_step, initial, (gathered, block_ids))
    attended = (totals / run_sum[..., None]).astype(jnp.bfloat16)
    return [attended[head] for head in range(heads_here)]


def mix_kernel(heads, head_dim, hop, place, *refs):
    head_refs, w_out = refs[:heads], refs[heads]
    kept, given, attended = refs[heads + 1 :]
    exp_index, turned = place[0], place[3]
    tok_rows = kept.shape[0]
    starts = [pl.multiple_of((exp_index ^ (hop + side)) * tok_rows, 16) for side in range(2)]
    for turn, head_ref in enumerate(head_refs):
        head = lax.rem(turned + turn, heads)
        columns = pl.ds(pl.multiple_of(head * head_dim, head_dim), head_dim)
        for side in range(2):
            attended[side * tok_rows : (side + 1) * tok_rows, columns] = head_ref[pl.ds(starts[side], tok_rows), :]
    mixed = f32_dot(attended[...], w_out[...]).astype(jnp.bfloat16)
    kept[...] = mixed[:tok_rows]
    given[...] = mixed[tok_rows:]


def sum_kernel(kept, given, summed):
    summed[...] = (kept[...].astype(jnp.float32) + given[...].astype(jnp.float32)).astype(summed.dtype)


def residual_kernel(top_count, inputs, kept, given, far, gain, noted, residual, ffn_in):
    summed = kept[...].astype(jnp.float32) + given[...].astype(jnp.float32) + far[...].astype(jnp.float32)
    rounded = (inputs[...].astype(jnp.float32) + summed).astype(jnp.bfloat16)
    residual[...] = rounded
    model_width = rounded.shape[1]
    ffn_in[:, 0:model_width] = normalize(rounded, gain[...])
    lane = lax.broadcasted_iota(jnp.int32, noted.shape, 1)
    left = noted[...]
    upper = left.astype(jnp.bfloat16).astype(jnp.float32)
    left = left - upper
    middle = left.astype(jnp.bfloat16).astype(jnp.float32)
    lower = left - middle
    parts = jnp.where(lane < 2 * top_count, upper, jnp.where(lane < 3 * top_count, middle, lower))
    ffn_in[:, model_width:] = parts.astype(jnp.bfloat16)


def pack_kernel(count, capacity, top_count, place, *refs):
    sources, outs, (notes, rows) = refs[:count], refs[count : count + 4], refs[count + 4 :]
    expert = place[4]
    tok_rows = sources[0].shape[0]
    total = count * tok_rows
    model_width = rows.shape[1]
    for turn in range(count):
        part = slice(turn * tok_rows, (turn + 1) * tok_rows)
        rows[part, :] = sources[turn][:, 0:model_width]
        notes[part, :] = sources[turn][:, model_width:]
    routes = notes[...].astype(jnp.float32).T[0:8]
    routes = jnp.where(lax.broadcasted_iota(jnp.int32, routes.shape, 0) < top_count, routes, -1.0)
    earlier = lax.broadcasted_iota(jnp.int32, (total, total), 0)
    later = lax.broadcasted_iota(jnp.int32, (total, total), 1)
    before = ((earlier < later) & (earlier // tok_rows == later // tok_rows)).astype(jnp.bfloat16)
    first_slot = lax.broadcasted_iota(jnp.int32, (1, total), 1) // tok_rows * capacity
    slot = lax.broadcasted_iota(jnp.int32, (count * capacity, total), 0)
    for hop in range(4):
        hit = jnp.where(routes == (expert ^ hop).astype(jnp.float32), 1.0, 0.0)
        member = jnp.sum(hit, axis=0, keepdims=True)
        place_in = f32_dot(jnp.broadcast_to(member, (16, total)).astype(jnp.bfloat16), before)[0:1]
        target = jnp.where(member > 0.5, place_in.astype(jnp.int32) + first_slot, -1)
        placing = jnp.where(slot == target, 1.0, 0.0).astype(jnp.bfloat16)
        outs[hop][...] = f32_dot(placing, rows[...]).astype(jnp.bfloat16)


def expert_kernel(slabs, *refs):
    parts = sum(len(members) for _, members in slabs)
    row_refs, weights = refs[:parts], refs[parts : parts + 6]
    outs, (held,) = refs[parts + 6 : 2 * parts + 6], refs[2 * parts + 6 :]
    across = (((1,), (1,)), ((), ()))
    for start, members in slabs:
        joined = [row_refs[part][...] for part in members]
        if len(joined) > 1:
            joined = [jnp.concatenate([row.astype(jnp.float32) for row in joined]).astype(jnp.bfloat16)]
        held[start : start + joined[0].shape[0], :] = joined[0]
    rows = held[...]
    result = None
    for w_gate, w_up, w_down in (weights[:3], weights[3:]):
        gate_part = lax.dot_general(rows, w_gate[...], across, preferred_element_type=jnp.float32)
        up_part = lax.dot_general(rows, w_up[...], across, preferred_element_type=jnp.float32)
        hidden = (gate_part / (1.0 + jnp.exp(-gate_part)) * up_part).astype(jnp.bfloat16)
        product = f32_dot(hidden, w_down[...])
        result = product if result is None else result + product
    for start, members in slabs:
        for part in members:
            count = outs[part].shape[0]
            outs[part][...] = result[start : start + count].astype(jnp.bfloat16)
            start += count


def combine_kernel(count, capacity, top_count, place, notes, *refs):
    returned, outs = refs[:4], refs[4 : 4 + count]
    expert = place[4]
    total = notes.shape[0]
    tok_rows = total // count
    row = lax.broadcasted_iota(jnp.int32, (LANES, LANES), 0)
    lane = lax.broadcasted_iota(jnp.int32, (LANES, LANES), 1)
    added = (lane < top_count) & (row >= top_count) & (row < 4 * top_count) & (row % top_count == lane)
    gates = f32_dot(notes[...], jnp.where(added, 1.0, 0.0).astype(jnp.bfloat16))
    routes = notes[...].astype(jnp.float32)
    routes = jnp.where(lax.broadcasted_iota(jnp.int32, routes.shape, 1) < top_count, routes, -1.0)
    later = lax.broadcasted_iota(jnp.int32, (total, total), 0)
    earlier = lax.broadcasted_iota(jnp.int32, (total, total), 1)
    before = ((earlier < later) & (earlier // tok_rows == later // tok_rows)).astype(jnp.bfloat16)
    first_slot = lax.broadcasted_iota(jnp.int32, (total, 1), 0) // tok_rows * capacity
    slot = lax.broadcasted_iota(jnp.int32, (total, count * capacity), 1)
    mixed = jnp.zeros((total, returned[0].shape[1]), jnp.float32)
    for hop in range(4):
        hit = routes == (expert ^ hop).astype(jnp.float32)
        member = jnp.sum(jnp.where(hit, 1.0, 0.0), axis=1, keepdims=True)
        factor = jnp.sum(jnp.where(hit, gates, 0.0), axis=1, keepdims=True)
        place_in = f32_dot(before, jnp.broadcast_to(member, (total, LANES)).astype(jnp.bfloat16))[:, 0:1]
        target = jnp.where(member > 0.5, place_in.astype(jnp.int32) + first_slot, -1)
        placing = jnp.where(slot == target, factor, 0.0)
        upper = placing.astype(jnp.bfloat16)
        lower = (placing - upper.astype(jnp.float32)).astype(jnp.bfloat16)
        mixed = mixed + f32_dot(upper, returned[hop][...]) + f32_dot(lower, returned[hop][...])
    for turn in range(count):
        outs[turn][...] = mixed[turn * tok_rows : (turn + 1) * tok_rows].astype(jnp.bfloat16)


def shards(
    inputs,
    attn_gain,
    w_query,
    w_key,
    w_value,
    w_out,
    sel_blocks,
    ffn_gain,
    w_gate,
    w_up,
    w_down,
    routes,
    gate_weights,
):
    tok_rows, model_width = inputs.shape
    block_len, heads_here, pick_count = sel_blocks.shape
    hidden_cols = w_query.shape[1]
    head_dim = hidden_cols // heads_here
    ctx_count, exp_count = lax.axis_size("ctx"), lax.axis_size("exp")
    depth = ctx_count // 2
    ctx_index, exp_index = lax.axis_index("ctx"), lax.axis_index("exp")
    z_index, x_index = ctx_index // 2, ctx_index % 2
    expert = (ctx_index * exp_count + exp_index) // 2
    by_head = heads_here == depth and block_len <= 3 * head_dim and head_dim == LANES
    place = jnp.stack(
        [exp_index, z_index, exp_index % 2, z_index if by_head else jnp.zeros_like(z_index), expert]
    ).astype(jnp.int32)

    far = move(inputs, lambda z, x, y, c: (z, x, y ^ 1, c))
    near = swap_core(inputs)
    far_near = swap_core(far)
    weights = (w_gate, w_up, w_down)
    other_gate, other_up, other_down = swap_core(w_gate), None, swap_core(w_down)
    far_near, other_gate, other_down = lax.optimization_barrier((far_near, other_gate, other_down))
    top_count = routes.shape[1]
    noted = jnp.concatenate([routes.astype(jnp.float32)] + [gate_weights] * 3, axis=1)
    noted = jnp.pad(noted, ((0, 0), (0, LANES - noted.shape[1])))
    if by_head:
        marks = jnp.sum(
            jnp.where(sel_blocks < ctx_index, jnp.left_shift(1, jnp.minimum(sel_blocks, 30)), 0), axis=2
        )
        marks = jnp.pad(marks.T.astype(jnp.bfloat16), ((0, 0), (0, 3 * head_dim - block_len)))
        marks = jnp.broadcast_to(marks[:, None], (heads_here, PAD_ROWS, 3 * head_dim))
        payload = struct(block_len + PAD_ROWS, 3 * head_dim)
        sent = call(
            functools.partial(project_kernel, exp_count, depth, head_dim),
            [payload] * depth,
            [
                place,
                marks,
                *(near, far, far_near),
                *(attn_gain.reshape(1, -1), inputs, w_query, w_key, w_value),
            ],
            [
                pltpu.VMEM((exp_count, tok_rows, model_width), jnp.bfloat16),
                pltpu.VMEM((block_len, model_width), jnp.bfloat16),
                pltpu.VMEM((3, block_len, hidden_cols), jnp.bfloat16),
                pltpu.VMEM((1, model_width), jnp.float32),
                pltpu.VMEM((3, model_width, hidden_cols), jnp.bfloat16),
                pltpu.SemaphoreType.DMA((exp_count + 4,)),
            ],
            flops=6 * block_len * model_width * hidden_cols,
            anywhere=exp_count - 1,
            hbm=5,
        )
        own = [head_out(sent[turn], turn) for turn in range(depth)]
        beside = [swap_core(block) for block in own]
        mixed = call(
            functools.partial(attend_kernel, depth, block_len, head_dim),
            [struct(block_len, head_dim)] * depth,
            [place, *own, *beside],
            [
                pltpu.VMEM((depth, block_len, head_dim), jnp.bfloat16),
                pltpu.VMEM((depth, 2 * block_len, head_dim), jnp.bfloat16),
                pltpu.VMEM((depth, head_dim, 2 * 3 * head_dim), jnp.bfloat16),
                pltpu.VMEM((depth, PAD_ROWS, 3 * head_dim), jnp.bfloat16),
                pltpu.VMEM((2 * depth, block_len, block_len), jnp.float32),
                pltpu.VMEM((depth, block_len, head_dim), jnp.bfloat16),
            ],
            flops=4 * depth * ctx_count * block_len * block_len * head_dim,
        )
        heads = [head_back(mixed[turn], turn) for turn in range(depth)]
    else:
        block = jnp.stack([inputs, near, far, far_near])[exp_index ^ jnp.arange(exp_count)]
        normed = normalize(block.reshape(block_len, model_width), attn_gain)
        heads = attend_gathered(normed, w_query, w_key, w_value, sel_blocks)

    def mixed_rows(hop, heads):
        return call(
            functools.partial(mix_kernel, heads_here, head_dim, hop),
            [struct(tok_rows, model_width)] * 2,
            [place, *heads, w_out],
            [pltpu.VMEM((2 * tok_rows, hidden_cols), jnp.bfloat16)],
            flops=4 * tok_rows * model_width * hidden_cols,
        )

    far_kept, far_given = mixed_rows(2, heads)
    kept, given = mixed_rows(0, [after(heads[0], far_given)] + heads[1:])
    far_given = swap_core(far_given)
    beyond = call(sum_kernel, struct(tok_rows, model_width), [after(far_kept, kept), far_given], smem=0)
    given = swap_core(after(given, beyond))
    other_up = swap_core(after(w_up, beyond))
    own_weights, other_weights = (
        [gate[0].T, up[0].T, down[0]] for gate, up, down in (weights, (other_gate, other_up, other_down))
    )
    g, u, d = other_weights
    *own, g, d = load([], [after(weight, beyond) for weight in [*own_weights, g, d]])
    expert_weights = [*own, g, u, d]
    beyond = move(beyond, lambda z, x, y, c: (z, x, y ^ 1, c))
    beyond, expert_weights = lax.optimization_barrier((beyond, expert_weights))
    residual, ffn_in = call(
        functools.partial(residual_kernel, top_count),
        [struct(tok_rows, model_width), struct(tok_rows, model_width + LANES)],
        [inputs, kept, given, beyond, ffn_gain.reshape(1, -1), noted],
        smem=0,
    )

    experts = ctx_count * exp_count // 2
    capacity = 2 * max(1, (tok_rows * top_count + experts - 1) // experts * 2 // 3)
    column = gather_z(ffn_in)
    groups = [[0], [1, depth - 1], list(range(2, depth - 1))]
    arrived, notes = [], []
    for group in groups:
        count = len(group)
        first = column[group[0]]
        if len(arrived) == 1:
            (up,) = load([], [after(expert_weights[4], arrived[0][0])])
            expert_weights[4] = up
            first = after(first, up, *arrived[0])
        elif arrived:
            first = after(first, arrived[-1][0])
        *packed, note = call(
            functools.partial(pack_kernel, count, capacity, top_count),
            [struct(count * capacity, model_width)] * 4 + [struct(count * tok_rows, LANES)],
            [place, first, *[column[t] for t in group[1:]]],
            [pltpu.VMEM((count * tok_rows, model_width), jnp.bfloat16)],
            flops=8 * count * capacity * count * tok_rows * model_width,
            limit=8 * MIB + 16 * (count * tok_rows) ** 2 + 8 * count * tok_rows * model_width,
        )
        arrived.append([packed[0]] + [swap_layer(packed[hop], hop) for hop in range(1, 4)])
        notes.append(note)

    def expert_rows(rows):
        slabs, total, part = [], 0, 0
        while part < len(rows):
            count = rows[part].shape[0]
            pair = count % 16 == 8 and part + 1 < len(rows) and rows[part + 1].shape[0] == count
            members = [part, part + 1] if pair else [part]
            slabs.append((total, members))
            total += -(-len(members) * count // 16) * 16
            part += len(members)
        return call(
            functools.partial(expert_kernel, slabs),
            [struct(*row.shape) for row in rows],
            [*rows, *expert_weights],
            [pltpu.VMEM((total, model_width), jnp.bfloat16)],
            flops=12 * total * model_width * w_gate.shape[2],
            smem=0,
            limit=4 * MIB + 32 * 1024 * total,
        )

    results = [None, expert_rows(arrived[1]), None]
    far_rows = [after(arrived[2][0], results[1][0])] + arrived[2][1:]
    both = expert_rows(arrived[0] + far_rows)
    results[0], results[2] = both[:4], both[4:]
    sums = [None] * depth
    for index in (1, 2, 0):
        group, rows = groups[index], list(results[index])
        if index == 0:
            rows[1:] = [after(row, sums[1]) for row in rows[1:]]
        rows = [rows[0]] + [swap_layer(rows[hop], hop) for hop in range(1, 4)]
        count = len(group)
        total = count * tok_rows
        parts = call(
            functools.partial(combine_kernel, count, capacity, top_count),
            [struct(tok_rows, model_width)] * count,
            [place, notes[index], *rows],
            flops=16 * count * capacity * total * model_width,
            limit=8 * MIB + 16 * total * total + 16 * total * model_width,
        )
        for turn, part in zip(group, parts):
            sums[turn] = part
    layer_out = residual.astype(jnp.float32) + sums[0].astype(jnp.float32)
    for turn in range(1, depth):
        layer_out = layer_out + turn_z(sums[turn], -turn).astype(jnp.float32)
    return layer_out.astype(jnp.bfloat16)


def solution(mesh):
    placed = (
        P(("ctx", "exp"), None),
        P(),
        P(None, "exp"),
        P(None, "exp"),
        P(None, "exp"),
        P("exp", None),
        P("ctx", "exp", None),
        P(),
        P(("ctx", "exp"), None, None),
        P(("ctx", "exp"), None, None),
        P(("ctx", "exp"), None, None),
        P(("ctx", "exp"), None),
        P(("ctx", "exp"), None),
    )
    return jax.shard_map(
        shards, mesh=mesh, in_specs=placed, out_specs=P(("ctx", "exp"), None), check_vma=False
    )
```

```python
import functools
import math

import jax
import jax.numpy as jnp
from jax import lax
from jax.experimental import pallas as pl
from jax.experimental.pallas import tpu as pltpu
from jax.sharding import PartitionSpec as P

AXES = ("ctx", "exp")
MIB = 1024 * 1024
VMEM = pl.BlockSpec(memory_space=pltpu.VMEM)
SMEM = pl.BlockSpec(memory_space=pltpu.SMEM)
ANY = pl.BlockSpec(memory_space=pl.ANY)
HBM = pl.BlockSpec(memory_space=pltpu.HBM)
PAD_ROWS = 16
LANES = 128


def move(block, target):
    ctx_count, exp_count = lax.axis_size("ctx"), lax.axis_size("exp")
    route = []
    for ctx in range(ctx_count):
        for exp in range(exp_count):
            z, x, y, c = target(ctx // 2, ctx % 2, exp // 2, exp % 2)
            route.append((ctx * exp_count + exp, (z * 2 + x) * exp_count + y * 2 + c))
    return lax.ppermute(block, AXES, route)


def swap_core(block):
    return move(block, lambda z, x, y, c: (z, x, y, c ^ 1))


def swap_layer(block, hop):
    return move(block, lambda z, x, y, c: (z, x ^ (hop >> 1), y ^ (hop & 1), c))


def turn_z(block, turn):
    depth = lax.axis_size("ctx") // 2
    return move(block, lambda z, x, y, c: ((z + turn) % depth, x, y, c))


def gather_z(block):
    depth = lax.axis_size("ctx") // 2
    column = [block] + [None] * (depth - 1)
    for turn in range(1, depth // 2 + 1):
        column[turn] = turn_z(column[turn - 1], 1)
    for turn in range(depth - 1, depth // 2, -1):
        column[turn] = turn_z(column[(turn + 1) % depth], -1)
    return column


def head_out(block, turn):
    depth = lax.axis_size("ctx") // 2
    return move(block, lambda z, x, y, c: ((z + turn) % depth, c, y, x))


def head_back(block, turn):
    depth = lax.axis_size("ctx") // 2
    return move(block, lambda z, x, y, c: ((z - turn) % depth, c, y, x))


def normalize(values, gain_vec):
    floats = values.astype(jnp.float32)
    factor = lax.rsqrt(jnp.mean(floats * floats, axis=-1, keepdims=True) + 1e-06)
    return (floats * factor * gain_vec).astype(jnp.bfloat16)


def f32_dot(left, right):
    return jnp.dot(left, right, preferred_element_type=jnp.float32)


def struct(*shape, dtype=jnp.bfloat16):
    return pltpu.VMEM(shape, dtype)


def call(kernel, outs, operands, scratch=(), flops=0, smem=1, anywhere=0, hbm=0, limit=16 * MIB):
    far = len(operands) - hbm
    last = far - anywhere
    operands = [
        pltpu.with_memory_space_constraint(a, pltpu.VMEM if i < last else pltpu.HBM)
        if smem <= i < last or i >= far
        else a
        for i, a in enumerate(operands)
    ]
    return pl.pallas_call(
        kernel,
        out_shape=outs,
        in_specs=[SMEM] * smem + [VMEM] * (last - smem) + [ANY] * anywhere + [HBM] * hbm,
        out_specs=jax.tree.map(lambda _: VMEM, outs),
        scratch_shapes=list(scratch),
        compiler_params=pltpu.CompilerParams(vmem_limit_bytes=limit),
        cost_estimate=pl.CostEstimate(
            flops=flops,
            bytes_accessed=sum(a.size * a.dtype.itemsize for a in operands),
            transcendentals=0,
        ),
    )(*operands)


def after(value, *others):
    return lax.optimization_barrier((value, *others))[0]


def load_kernel(count, *refs):
    sources, targets, sems = refs[:count], refs[count : 2 * count], refs[2 * count]
    copies = [
        pltpu.make_async_copy(sources[i], targets[i], sems.at[i]) for i in range(count)
    ]
    for copy in copies:
        copy.start()
    for copy in copies:
        copy.wait()


def load(received, held):
    arrays = [*received, *held]
    return call(
        functools.partial(load_kernel, len(arrays)),
        [struct(*a.shape) for a in arrays],
        arrays,
        [pltpu.SemaphoreType.DMA((len(arrays),))],
        smem=0,
        anywhere=len(received),
        hbm=len(held),
        limit=MIB,
    )


def near_kernel(place, *refs):
    sources, (mixed, *held), (given, gain, rows, sems) = refs[:6], refs[6:10], refs[10:]
    tok_rows = given.shape[1]
    targets = [given.at[1], gain, given.at[0], *held]
    copies = [pltpu.make_async_copy(sources[i], targets[i], sems.at[i]) for i in range(6)]
    for copy in copies:
        copy.start()
    for copy in copies[:3]:
        copy.wait()
    for side in range(2):
        rows[side * tok_rows : (side + 1) * tok_rows, :] = normalize(given[side], gain[...])
    for part, copy in enumerate(copies[3:]):
        copy.wait()
        mixed[part] = f32_dot(rows[...], held[part][...]).astype(jnp.bfloat16)


def project_kernel(depth, head_dim, place, marks, near_mixed, gain, *refs):
    held, sources, outs = refs[:3], refs[3:5], refs[5 : 5 + depth]
    given, rows, mixed, sems = refs[5 + depth :]
    exp_index, z_index = place[0], place[1]
    tok_rows = given.shape[1]
    block_len = 4 * tok_rows
    copies = [pltpu.make_async_copy(sources[i], given.at[i], sems.at[i]) for i in range(2)]
    for copy in copies:
        copy.start()
    starts = [pl.multiple_of((exp_index ^ hop) * tok_rows, 16) for hop in range(4)]
    for side, copy in enumerate(copies):
        copy.wait()
        rows[side * tok_rows : (side + 1) * tok_rows, :] = normalize(given[side], gain[...])
    for part in range(3):
        far_mixed = f32_dot(rows[...], held[part][...]).astype(jnp.bfloat16)
        for side in range(2):
            pick = slice(side * tok_rows, (side + 1) * tok_rows)
            mixed[part, pl.ds(starts[side], tok_rows), :] = near_mixed[part, pick, :]
            mixed[part, pl.ds(starts[2 + side], tok_rows), :] = far_mixed[pick]
    for turn in range(depth):
        head = lax.rem(z_index + turn, depth)
        columns = pl.ds(pl.multiple_of(head * head_dim, head_dim), head_dim)
        for part in range(3):
            outs[turn][0:block_len, part * head_dim : (part + 1) * head_dim] = mixed[part, :, columns]
        outs[turn][block_len : block_len + PAD_ROWS, :] = marks[head]


def attend_kernel(depth, block_len, head_dim, place, *refs):
    own_refs, near_refs, outs = refs[:depth], refs[depth : 2 * depth], refs[2 * depth : 3 * depth]
    queries, keys, values, chosen_rows, scores, mixed = refs[3 * depth :]
    z_index, core = place[1], place[2]
    scaling = math.log2(math.e) / math.sqrt(head_dim)
    width = values.shape[2] // 2
    for turn in range(depth):
        source = lax.rem(z_index + depth - turn, depth)
        queries[source] = own_refs[turn][0:block_len, 0:head_dim]
        chosen_rows[source] = own_refs[turn][block_len : block_len + PAD_ROWS, :]
        for side, ref in enumerate((own_refs[turn], near_refs[turn])):
            keys[source, side * block_len : (side + 1) * block_len] = ref[0:block_len, head_dim : 2 * head_dim]
            values[source, :, side * width : side * width + block_len] = ref[
                0:block_len, 2 * head_dim : 3 * head_dim
            ].T
    key_pos = lax.broadcasted_iota(jnp.int32, (block_len, block_len), 0)
    query_pos = lax.broadcasted_iota(jnp.int32, (block_len, block_len), 1)
    causal = jnp.where(key_pos <= query_pos, 0.0, -1e30)
    for level in range(depth):
        query = queries[level]
        marks = chosen_rows[level, :, 0:block_len].astype(jnp.float32)[0:1].astype(jnp.int32)
        pairs = [(c, side) for c in range(level + 1) for side in range(2)]
        run_max, chosen = None, []
        for index, (c, side) in enumerate(pairs):
            score = lax.dot_general(
                keys[c, side * block_len : (side + 1) * block_len],
                query,
                (((1,), (1,)), ((), ())),
                preferred_element_type=jnp.float32,
            )
            if c == level and side == 0:
                score = score + causal
                chosen.append(None)
                top = jnp.max(score, axis=0, keepdims=True)
            else:
                bit = 2 * c + (core if side == 0 else 1 - core)
                picked = lax.shift_right_logical(marks, jnp.broadcast_to(bit, marks.shape)) & 1
                chosen.append(picked == 1)
                top = jnp.where(chosen[-1], jnp.max(score, axis=0, keepdims=True), -1e30)
            scores[index] = score
            run_max = top if run_max is None else jnp.maximum(run_max, top)
        run_sum = total = None
        for index, (c, side) in enumerate(pairs):
            shift = run_max if chosen[index] is None else jnp.where(chosen[index], run_max, 1e30)
            weights = jnp.exp2((scores[index] - shift) * scaling)
            added = jnp.sum(weights, axis=0, keepdims=True)
            product = f32_dot(
                values[c, :, side * width : side * width + block_len], weights.astype(jnp.bfloat16)
            )
            run_sum = added if run_sum is None else run_sum + added
            total = product if total is None else total + product
        mixed[level] = (total / run_sum).T.astype(jnp.bfloat16)
    for turn in range(depth):
        outs[turn][...] = mixed[lax.rem(z_index + depth - turn, depth)]


def attend_gathered(normed_block, w_query, w_key, w_value, sel_blocks):
    block_len, heads_here, _ = sel_blocks.shape
    hidden_cols = w_query.shape[1]
    head_dim = hidden_cols // heads_here
    ctx_count, ctx_index = lax.axis_size("ctx"), lax.axis_index("ctx")
    query_part, key_part, value_part = (
        f32_dot(normed_block, weight).astype(jnp.bfloat16) for weight in (w_query, w_key, w_value)
    )
    queries = query_part.reshape(block_len, heads_here, head_dim)
    keys_values = jnp.stack([key_part, value_part], axis=1)
    block_ids = jnp.arange(ctx_count, dtype=jnp.int32)
    chosen = jnp.any(sel_blocks[:, :, :, None] == block_ids, axis=2) & (block_ids < ctx_index)
    position = jnp.arange(block_len, dtype=jnp.int32)
    causal = position[None, :] <= position[:, None]
    scaling = 1.0 / math.sqrt(head_dim)

    def fold_step(running, operands):
        run_max, run_sum, totals = running
        piece, block = operands
        key_rows = piece[:, 0].reshape(block_len, heads_here, head_dim)
        value_rows = piece[:, 1].reshape(block_len, heads_here, head_dim)
        scores = (
            jnp.einsum("qhd,khd->hqk", queries, key_rows, preferred_element_type=jnp.float32)
            * scaling
        )
        picked = jnp.take(chosen, block, axis=2).T[:, :, None]
        allowed = picked | ((block == ctx_index) & causal)[None]
        new_max = jnp.maximum(run_max, jnp.max(jnp.where(allowed, scores, -jnp.inf), axis=-1))
        weights = jnp.where(allowed, jnp.exp(scores - new_max[..., None]), 0.0)
        rescale = jnp.exp(run_max - new_max)
        run_sum = run_sum * rescale + jnp.sum(weights, axis=-1)
        totals = totals * rescale[..., None] + jnp.einsum(
            "hqk,khd->hqd",
            weights.astype(jnp.bfloat16),
            value_rows,
            preferred_element_type=jnp.float32,
        )
        return (new_max, run_sum, totals), None

    initial = (
        jnp.full((heads_here, block_len), -1e30, jnp.float32),
        jnp.zeros((heads_here, block_len), jnp.float32),
        jnp.zeros((heads_here, block_len, head_dim), jnp.float32),
    )
    gathered = lax.all_gather(keys_values, "ctx", axis=0)
    (_, run_sum, totals), _ = lax.scan(fold_step, initial, (gathered, block_ids))
    attended = (totals / run_sum[..., None]).astype(jnp.bfloat16)
    return [attended[head] for head in range(heads_here)]


def mix_kernel(heads, head_dim, hop, place, *refs):
    head_refs, w_out = refs[:heads], refs[heads]
    kept, given, attended = refs[heads + 1 :]
    exp_index, turned = place[0], place[3]
    tok_rows = kept.shape[0]
    starts = [pl.multiple_of((exp_index ^ (hop + side)) * tok_rows, 16) for side in range(2)]
    for turn, head_ref in enumerate(head_refs):
        head = lax.rem(turned + turn, heads)
        columns = pl.ds(pl.multiple_of(head * head_dim, head_dim), head_dim)
        for side in range(2):
            attended[side * tok_rows : (side + 1) * tok_rows, columns] = head_ref[pl.ds(starts[side], tok_rows), :]
    mixed = f32_dot(attended[...], w_out[...]).astype(jnp.bfloat16)
    kept[...] = mixed[:tok_rows]
    given[...] = mixed[tok_rows:]


def sum_kernel(kept, given, summed):
    summed[...] = (kept[...].astype(jnp.float32) + given[...].astype(jnp.float32)).astype(summed.dtype)


def residual_kernel(top_count, inputs, kept, given, far, gain, noted, residual, ffn_in):
    summed = kept[...].astype(jnp.float32) + given[...].astype(jnp.float32) + far[...].astype(jnp.float32)
    rounded = (inputs[...].astype(jnp.float32) + summed).astype(jnp.bfloat16)
    residual[...] = rounded
    model_width = rounded.shape[1]
    ffn_in[:, 0:model_width] = normalize(rounded, gain[...])
    lane = lax.broadcasted_iota(jnp.int32, noted.shape, 1)
    left = noted[...]
    upper = left.astype(jnp.bfloat16).astype(jnp.float32)
    left = left - upper
    middle = left.astype(jnp.bfloat16).astype(jnp.float32)
    lower = left - middle
    parts = jnp.where(lane < 2 * top_count, upper, jnp.where(lane < 3 * top_count, middle, lower))
    ffn_in[:, model_width:] = parts.astype(jnp.bfloat16)


def pack_kernel(count, capacity, top_count, place, *refs):
    sources, outs, (notes, rows) = refs[:count], refs[count : count + 4], refs[count + 4 :]
    expert = place[4]
    tok_rows = sources[0].shape[0]
    total = count * tok_rows
    model_width = rows.shape[1]
    for turn in range(count):
        part = slice(turn * tok_rows, (turn + 1) * tok_rows)
        rows[part, :] = sources[turn][:, 0:model_width]
        notes[part, :] = sources[turn][:, model_width:]
    routes = notes[...].astype(jnp.float32).T[0:8]
    routes = jnp.where(lax.broadcasted_iota(jnp.int32, routes.shape, 0) < top_count, routes, -1.0)
    earlier = lax.broadcasted_iota(jnp.int32, (total, total), 0)
    later = lax.broadcasted_iota(jnp.int32, (total, total), 1)
    before = ((earlier < later) & (earlier // tok_rows == later // tok_rows)).astype(jnp.bfloat16)
    first_slot = lax.broadcasted_iota(jnp.int32, (1, total), 1) // tok_rows * capacity
    slot = lax.broadcasted_iota(jnp.int32, (count * capacity, total), 0)
    for hop in range(4):
        hit = jnp.where(routes == (expert ^ hop).astype(jnp.float32), 1.0, 0.0)
        member = jnp.sum(hit, axis=0, keepdims=True)
        place_in = f32_dot(jnp.broadcast_to(member, (16, total)).astype(jnp.bfloat16), before)[0:1]
        target = jnp.where(member > 0.5, place_in.astype(jnp.int32) + first_slot, -1)
        placing = jnp.where(slot == target, 1.0, 0.0).astype(jnp.bfloat16)
        outs[hop][...] = f32_dot(placing, rows[...]).astype(jnp.bfloat16)


def expert_kernel(slabs, *refs):
    parts = sum(len(members) for _, members in slabs)
    row_refs, weights = refs[:parts], refs[parts : parts + 6]
    outs, (held,) = refs[parts + 6 : 2 * parts + 6], refs[2 * parts + 6 :]
    across = (((1,), (1,)), ((), ()))
    for start, members in slabs:
        joined = [row_refs[part][...] for part in members]
        if len(joined) > 1:
            joined = [jnp.concatenate([row.astype(jnp.float32) for row in joined]).astype(jnp.bfloat16)]
        held[start : start + joined[0].shape[0], :] = joined[0]
    rows = held[...]
    result = None
    for w_gate, w_up, w_down in (weights[:3], weights[3:]):
        gate_part = lax.dot_general(rows, w_gate[...], across, preferred_element_type=jnp.float32)
        up_part = lax.dot_general(rows, w_up[...], across, preferred_element_type=jnp.float32)
        hidden = (gate_part / (1.0 + jnp.exp(-gate_part)) * up_part).astype(jnp.bfloat16)
        product = f32_dot(hidden, w_down[...])
        result = product if result is None else result + product
    for start, members in slabs:
        for part in members:
            count = outs[part].shape[0]
            outs[part][...] = result[start : start + count].astype(jnp.bfloat16)
            start += count


def weigh_kernel(count, capacity, top_count, place, notes, upper, lower):
    expert = place[4]
    total = notes.shape[0]
    tok_rows = total // count
    row = lax.broadcasted_iota(jnp.int32, (LANES, LANES), 0)
    lane = lax.broadcasted_iota(jnp.int32, (LANES, LANES), 1)
    added = (lane < top_count) & (row >= top_count) & (row < 4 * top_count) & (row % top_count == lane)
    gates = f32_dot(notes[...], jnp.where(added, 1.0, 0.0).astype(jnp.bfloat16))
    routes = notes[...].astype(jnp.float32)
    routes = jnp.where(lax.broadcasted_iota(jnp.int32, routes.shape, 1) < top_count, routes, -1.0)
    later = lax.broadcasted_iota(jnp.int32, (total, total), 0)
    earlier = lax.broadcasted_iota(jnp.int32, (total, total), 1)
    before = ((earlier < later) & (earlier // tok_rows == later // tok_rows)).astype(jnp.bfloat16)
    first_slot = lax.broadcasted_iota(jnp.int32, (total, 1), 0) // tok_rows * capacity
    slot = lax.broadcasted_iota(jnp.int32, (total, count * capacity), 1)
    for hop in range(4):
        hit = routes == (expert ^ hop).astype(jnp.float32)
        member = jnp.sum(jnp.where(hit, 1.0, 0.0), axis=1, keepdims=True)
        factor = jnp.sum(jnp.where(hit, gates, 0.0), axis=1, keepdims=True)
        place_in = f32_dot(before, jnp.broadcast_to(member, (total, LANES)).astype(jnp.bfloat16))[:, 0:1]
        target = jnp.where(member > 0.5, place_in.astype(jnp.int32) + first_slot, -1)
        placing = jnp.where(slot == target, factor, 0.0)
        upper[hop] = placing.astype(jnp.bfloat16)
        lower[hop] = (placing - upper[hop].astype(jnp.float32)).astype(jnp.bfloat16)


def mix_slots(upper, lower, returned):
    mixed = None
    for hop in range(4):
        rows = returned[hop][...]
        term = f32_dot(upper[hop], rows) + f32_dot(lower[hop], rows)
        mixed = term if mixed is None else mixed + term
    return mixed


def combine_kernel(count, upper, lower, *refs):
    returned, outs = refs[:4], refs[4 : 4 + count]
    tok_rows = upper.shape[1] // count
    mixed = mix_slots(upper, lower, returned)
    for turn in range(count):
        outs[turn][...] = mixed[turn * tok_rows : (turn + 1) * tok_rows].astype(jnp.bfloat16)


def finish_kernel(upper, lower, *refs):
    returned, (residual, *others), out = refs[:4], refs[4:-1], refs[-1]
    total = residual[...].astype(jnp.float32) + mix_slots(upper, lower, returned)
    for other in others:
        total = total + other[...].astype(jnp.float32)
    out[...] = total


def shards(
    inputs,
    attn_gain,
    w_query,
    w_key,
    w_value,
    w_out,
    sel_blocks,
    ffn_gain,
    w_gate,
    w_up,
    w_down,
    routes,
    gate_weights,
):
    tok_rows, model_width = inputs.shape
    block_len, heads_here, pick_count = sel_blocks.shape
    hidden_cols = w_query.shape[1]
    head_dim = hidden_cols // heads_here
    ctx_count, exp_count = lax.axis_size("ctx"), lax.axis_size("exp")
    depth = ctx_count // 2
    ctx_index, exp_index = lax.axis_index("ctx"), lax.axis_index("exp")
    z_index, x_index = ctx_index // 2, ctx_index % 2
    expert = (ctx_index * exp_count + exp_index) // 2
    by_head = heads_here == depth and block_len <= 3 * head_dim and head_dim == LANES
    place = jnp.stack(
        [exp_index, z_index, exp_index % 2, z_index if by_head else jnp.zeros_like(z_index), expert]
    ).astype(jnp.int32)

    far = move(inputs, lambda z, x, y, c: (z, x, y ^ 1, c))
    near = swap_core(inputs)
    weights = (w_gate, w_up, w_down)
    other_gate, other_up, other_down = swap_core(w_gate), None, swap_core(w_down)
    top_count = routes.shape[1]
    noted = jnp.concatenate([routes.astype(jnp.float32)] + [gate_weights] * 3, axis=1)
    noted = jnp.pad(noted, ((0, 0), (0, LANES - noted.shape[1])))
    if by_head:
        marks = jnp.sum(
            jnp.where(sel_blocks < ctx_index, jnp.left_shift(1, jnp.minimum(sel_blocks, 30)), 0), axis=2
        )
        marks = jnp.pad(marks.T.astype(jnp.bfloat16), ((0, 0), (0, 3 * head_dim - block_len)))
        marks = jnp.broadcast_to(marks[:, None], (heads_here, PAD_ROWS, 3 * head_dim))
        payload = struct(block_len + PAD_ROWS, 3 * head_dim)
        gain_row = attn_gain.reshape(1, -1)
        near_mixed, *held = call(
            near_kernel,
            [struct(3, 2 * tok_rows, hidden_cols)] + [struct(model_width, hidden_cols)] * 3,
            [place, near, gain_row, inputs, w_query, w_key, w_value],
            [
                pltpu.VMEM((2, tok_rows, model_width), jnp.bfloat16),
                pltpu.VMEM((1, model_width), jnp.float32),
                pltpu.VMEM((2 * tok_rows, model_width), jnp.bfloat16),
                pltpu.SemaphoreType.DMA((6,)),
            ],
            flops=12 * tok_rows * model_width * hidden_cols,
            anywhere=1,
            hbm=5,
        )
        far_near = swap_core(after(far, near_mixed))
        far_near, other_gate, other_down = lax.optimization_barrier((far_near, other_gate, other_down))
        sent = call(
            functools.partial(project_kernel, depth, head_dim),
            [payload] * depth,
            [place, marks, near_mixed, gain_row, *held, far, far_near],
            [
                pltpu.VMEM((2, tok_rows, model_width), jnp.bfloat16),
                pltpu.VMEM((2 * tok_rows, model_width), jnp.bfloat16),
                pltpu.VMEM((3, block_len, hidden_cols), jnp.bfloat16),
                pltpu.SemaphoreType.DMA((2,)),
            ],
            flops=12 * tok_rows * model_width * hidden_cols,
            anywhere=2,
        )
        own = [head_out(sent[turn], turn) for turn in range(depth)]
        beside = [swap_core(block) for block in own]
        mixed = call(
            functools.partial(attend_kernel, depth, block_len, head_dim),
            [struct(block_len, head_dim)] * depth,
            [place, *own, *beside],
            [
                pltpu.VMEM((depth, block_len, head_dim), jnp.bfloat16),
                pltpu.VMEM((depth, 2 * block_len, head_dim), jnp.bfloat16),
                pltpu.VMEM((depth, head_dim, 2 * 3 * head_dim), jnp.bfloat16),
                pltpu.VMEM((depth, PAD_ROWS, 3 * head_dim), jnp.bfloat16),
                pltpu.VMEM((2 * depth, block_len, block_len), jnp.float32),
                pltpu.VMEM((depth, block_len, head_dim), jnp.bfloat16),
            ],
            flops=4 * depth * ctx_count * block_len * block_len * head_dim,
        )
        heads = [head_back(mixed[turn], turn) for turn in range(depth)]
    else:
        block = jnp.stack([inputs, near, far, swap_core(far)])[exp_index ^ jnp.arange(exp_count)]
        normed = normalize(block.reshape(block_len, model_width), attn_gain)
        heads = attend_gathered(normed, w_query, w_key, w_value, sel_blocks)

    def mixed_rows(hop, heads):
        return call(
            functools.partial(mix_kernel, heads_here, head_dim, hop),
            [struct(tok_rows, model_width)] * 2,
            [place, *heads, w_out],
            [pltpu.VMEM((2 * tok_rows, hidden_cols), jnp.bfloat16)],
            flops=4 * tok_rows * model_width * hidden_cols,
        )

    far_kept, far_given = mixed_rows(2, heads)
    kept, given = mixed_rows(0, [after(heads[0], far_given)] + heads[1:])
    far_given = swap_core(far_given)
    beyond = call(sum_kernel, struct(tok_rows, model_width), [after(far_kept, kept), far_given], smem=0)
    given = swap_core(after(given, beyond))
    other_up = swap_core(after(w_up, beyond))
    own_weights, other_weights = (
        [gate[0].T, up[0].T, down[0]] for gate, up, down in (weights, (other_gate, other_up, other_down))
    )
    g, u, d = other_weights
    *own, g, d = load([], [after(weight, beyond) for weight in [*own_weights, g, d]])
    expert_weights = [*own, g, u, d]
    beyond = move(beyond, lambda z, x, y, c: (z, x, y ^ 1, c))
    beyond, expert_weights = lax.optimization_barrier((beyond, expert_weights))
    residual, ffn_in = call(
        functools.partial(residual_kernel, top_count),
        [struct(tok_rows, model_width), struct(tok_rows, model_width + LANES)],
        [inputs, kept, given, beyond, ffn_gain.reshape(1, -1), noted],
        smem=0,
    )

    experts = ctx_count * exp_count // 2
    capacity = 2 * max(1, (tok_rows * top_count + experts - 1) // experts * 2 // 3)
    column = gather_z(ffn_in)
    groups = [[0], [1, depth - 1], list(range(2, depth - 1))]
    arrived, notes = [], []
    for group in groups:
        count = len(group)
        first = column[group[0]]
        if len(arrived) == 1:
            (up,) = load([], [after(expert_weights[4], arrived[0][0])])
            expert_weights[4] = up
            first = after(first, up, *arrived[0])
        elif arrived:
            first = after(first, arrived[-1][0])
        *packed, note = call(
            functools.partial(pack_kernel, count, capacity, top_count),
            [struct(count * capacity, model_width)] * 4 + [struct(count * tok_rows, LANES)],
            [place, first, *[column[t] for t in group[1:]]],
            [pltpu.VMEM((count * tok_rows, model_width), jnp.bfloat16)],
            flops=8 * count * capacity * count * tok_rows * model_width,
            limit=8 * MIB + 16 * (count * tok_rows) ** 2 + 8 * count * tok_rows * model_width,
        )
        arrived.append([packed[0]] + [swap_layer(packed[hop], hop) for hop in range(1, 4)])
        notes.append(note)

    def expert_rows(rows):
        slabs, total, part = [], 0, 0
        while part < len(rows):
            count = rows[part].shape[0]
            pair = count % 16 == 8 and part + 1 < len(rows) and rows[part + 1].shape[0] == count
            members = [part, part + 1] if pair else [part]
            slabs.append((total, members))
            total += -(-len(members) * count // 16) * 16
            part += len(members)
        return call(
            functools.partial(expert_kernel, slabs),
            [struct(*row.shape) for row in rows],
            [*rows, *expert_weights],
            [pltpu.VMEM((total, model_width), jnp.bfloat16)],
            flops=12 * total * model_width * w_gate.shape[2],
            smem=0,
            limit=4 * MIB + 32 * 1024 * total,
        )

    shares = []
    for group, note in zip(groups, notes):
        count = len(group)
        total = count * tok_rows
        shares.append(
            call(
                functools.partial(weigh_kernel, count, capacity, top_count),
                [struct(4, total, count * capacity)] * 2,
                [place, note],
                flops=8 * total * total * LANES,
                limit=8 * MIB + 16 * total * total,
            )
        )
    arrived[1][1] = after(arrived[1][1], *(part for share in shares for part in share))
    results = [None, expert_rows(arrived[1]), None]
    far_rows = [after(arrived[2][0], results[1][0])] + arrived[2][1:]
    both = expert_rows(arrived[0] + far_rows)
    results[0], results[2] = both[:4], both[4:]
    sums = [None] * depth
    home = [None] * depth
    for index in (1, 2):
        group, rows = groups[index], list(results[index])
        rows = [rows[0]] + [swap_layer(rows[hop], hop) for hop in range(1, 4)]
        count = len(group)
        total = count * tok_rows
        parts = call(
            functools.partial(combine_kernel, count),
            [struct(tok_rows, model_width)] * count,
            [*shares[index], *rows],
            flops=16 * count * capacity * total * model_width,
            smem=0,
            limit=8 * MIB + 16 * total * model_width,
        )
        for turn, part in zip(group, parts):
            sums[turn] = part
            home[turn] = turn_z(part, -turn)
    rows = [results[0][0]] + [swap_layer(after(results[0][hop], sums[1]), hop) for hop in range(1, 4)]
    layer_out = call(
        finish_kernel,
        struct(tok_rows, model_width, dtype=jnp.float32),
        [*shares[0], *rows, residual, *(home[turn] for turn in groups[1])],
        flops=16 * capacity * tok_rows * model_width,
        smem=0,
    )
    for turn in groups[2]:
        layer_out = layer_out + home[turn].astype(jnp.float32)
    return layer_out.astype(jnp.bfloat16)


def solution(mesh):
    placed = (
        P(("ctx", "exp"), None),
        P(),
        P(None, "exp"),
        P(None, "exp"),
        P(None, "exp"),
        P("exp", None),
        P("ctx", "exp", None),
        P(),
        P(("ctx", "exp"), None, None),
        P(("ctx", "exp"), None, None),
        P(("ctx", "exp"), None, None),
        P(("ctx", "exp"), None),
        P(("ctx", "exp"), None),
    )
    return jax.shard_map(
        shards, mesh=mesh, in_specs=placed, out_specs=P(("ctx", "exp"), None), check_vma=False
    )
```

```python
import functools
import math

import jax
import jax.numpy as jnp
from jax import lax
from jax.experimental import pallas as pl
from jax.experimental.pallas import tpu as pltpu
from jax.sharding import PartitionSpec as P

AXES = ("ctx", "exp")
MIB = 1024 * 1024
VMEM = pl.BlockSpec(memory_space=pltpu.VMEM)
SMEM = pl.BlockSpec(memory_space=pltpu.SMEM)
ANY = pl.BlockSpec(memory_space=pl.ANY)
HBM = pl.BlockSpec(memory_space=pltpu.HBM)
PAD_ROWS = 16
LANES = 128


def move(block, target):
    ctx_count, exp_count = lax.axis_size("ctx"), lax.axis_size("exp")
    route = []
    for ctx in range(ctx_count):
        for exp in range(exp_count):
            z, x, y, c = target(ctx // 2, ctx % 2, exp // 2, exp % 2)
            route.append((ctx * exp_count + exp, (z * 2 + x) * exp_count + y * 2 + c))
    return lax.ppermute(block, AXES, route)


def swap_core(block):
    return move(block, lambda z, x, y, c: (z, x, y, c ^ 1))


def swap_layer(block, hop):
    return move(block, lambda z, x, y, c: (z, x ^ (hop >> 1), y ^ (hop & 1), c))


def turn_z(block, turn):
    depth = lax.axis_size("ctx") // 2
    return move(block, lambda z, x, y, c: ((z + turn) % depth, x, y, c))


def gather_z(block):
    depth = lax.axis_size("ctx") // 2
    column = [block] + [None] * (depth - 1)
    for turn in range(1, depth // 2 + 1):
        column[turn] = turn_z(column[turn - 1], 1)
    for turn in range(depth - 1, depth // 2, -1):
        column[turn] = turn_z(column[(turn + 1) % depth], -1)
    return column


def head_out(block, turn):
    depth = lax.axis_size("ctx") // 2
    return move(block, lambda z, x, y, c: ((z + turn) % depth, c, y, x))


def head_back(block, turn):
    depth = lax.axis_size("ctx") // 2
    return move(block, lambda z, x, y, c: ((z - turn) % depth, c, y, x))


def normalize(values, gain_vec):
    floats = values.astype(jnp.float32)
    factor = lax.rsqrt(jnp.mean(floats * floats, axis=-1, keepdims=True) + 1e-06)
    return (floats * factor * gain_vec).astype(jnp.bfloat16)


def f32_dot(left, right):
    return jnp.dot(left, right, preferred_element_type=jnp.float32)


def struct(*shape, dtype=jnp.bfloat16):
    return pltpu.VMEM(shape, dtype)


def call(kernel, outs, operands, scratch=(), flops=0, smem=1, anywhere=0, hbm=0, limit=16 * MIB):
    far = len(operands) - hbm
    last = far - anywhere
    operands = [
        pltpu.with_memory_space_constraint(a, pltpu.VMEM if i < last else pltpu.HBM)
        if smem <= i < last or i >= far
        else a
        for i, a in enumerate(operands)
    ]
    return pl.pallas_call(
        kernel,
        out_shape=outs,
        in_specs=[SMEM] * smem + [VMEM] * (last - smem) + [ANY] * anywhere + [HBM] * hbm,
        out_specs=jax.tree.map(lambda _: VMEM, outs),
        scratch_shapes=list(scratch),
        compiler_params=pltpu.CompilerParams(vmem_limit_bytes=limit),
        cost_estimate=pl.CostEstimate(
            flops=flops,
            bytes_accessed=sum(a.size * a.dtype.itemsize for a in operands),
            transcendentals=0,
        ),
    )(*operands)


def after(value, *others):
    return lax.optimization_barrier((value, *others))[0]


def load_kernel(count, *refs):
    sources, targets, sems = refs[:count], refs[count : 2 * count], refs[2 * count]
    copies = [
        pltpu.make_async_copy(sources[i], targets[i], sems.at[i]) for i in range(count)
    ]
    for copy in copies:
        copy.start()
    for copy in copies:
        copy.wait()


def load(received, held):
    arrays = [*received, *held]
    return call(
        functools.partial(load_kernel, len(arrays)),
        [struct(*a.shape) for a in arrays],
        arrays,
        [pltpu.SemaphoreType.DMA((len(arrays),))],
        smem=0,
        anywhere=len(received),
        hbm=len(held),
        limit=MIB,
    )


def near_kernel(place, *refs):
    sources, (mixed, *held), (given, gain, rows, sems) = refs[:6], refs[6:10], refs[10:]
    tok_rows = given.shape[1]
    targets = [given.at[1], gain, given.at[0], *held]
    copies = [pltpu.make_async_copy(sources[i], targets[i], sems.at[i]) for i in range(6)]
    for copy in copies:
        copy.start()
    for copy in copies[:3]:
        copy.wait()
    for side in range(2):
        rows[side * tok_rows : (side + 1) * tok_rows, :] = normalize(given[side], gain[...])
    for part, copy in enumerate(copies[3:]):
        copy.wait()
        mixed[part] = f32_dot(rows[...], held[part][...]).astype(jnp.bfloat16)


def project_kernel(depth, head_dim, place, marks, near_mixed, gain, *refs):
    held, sources, outs = refs[:3], refs[3:5], refs[5 : 5 + depth]
    given, rows, mixed, sems = refs[5 + depth :]
    exp_index, z_index = place[0], place[1]
    tok_rows = given.shape[1]
    block_len = 4 * tok_rows
    copies = [pltpu.make_async_copy(sources[i], given.at[i], sems.at[i]) for i in range(2)]
    for copy in copies:
        copy.start()
    starts = [pl.multiple_of((exp_index ^ hop) * tok_rows, 16) for hop in range(4)]
    for side, copy in enumerate(copies):
        copy.wait()
        rows[side * tok_rows : (side + 1) * tok_rows, :] = normalize(given[side], gain[...])
    for part in range(3):
        far_mixed = f32_dot(rows[...], held[part][...]).astype(jnp.bfloat16)
        for side in range(2):
            pick = slice(side * tok_rows, (side + 1) * tok_rows)
            mixed[part, pl.ds(starts[side], tok_rows), :] = near_mixed[part, pick, :]
            mixed[part, pl.ds(starts[2 + side], tok_rows), :] = far_mixed[pick]
    for turn in range(depth):
        head = lax.rem(z_index + turn, depth)
        columns = pl.ds(pl.multiple_of(head * head_dim, head_dim), head_dim)
        for part in range(3):
            outs[turn][0:block_len, part * head_dim : (part + 1) * head_dim] = mixed[part, :, columns]
        outs[turn][block_len : block_len + PAD_ROWS, :] = marks[head]


def attend_kernel(depth, block_len, head_dim, place, *refs):
    own_refs, near_refs, outs = refs[:depth], refs[depth : 2 * depth], refs[2 * depth : 3 * depth]
    queries, keys, values, chosen_rows, scores, mixed = refs[3 * depth :]
    z_index, core = place[1], place[2]
    scaling = math.log2(math.e) / math.sqrt(head_dim)
    width = values.shape[2] // 2
    for turn in range(depth):
        source = lax.rem(z_index + depth - turn, depth)
        queries[source] = own_refs[turn][0:block_len, 0:head_dim]
        chosen_rows[source] = own_refs[turn][block_len : block_len + PAD_ROWS, :]
        for side, ref in enumerate((own_refs[turn], near_refs[turn])):
            keys[source, side * block_len : (side + 1) * block_len] = ref[0:block_len, head_dim : 2 * head_dim]
            values[source, :, side * width : side * width + block_len] = ref[
                0:block_len, 2 * head_dim : 3 * head_dim
            ].T
    key_pos = lax.broadcasted_iota(jnp.int32, (block_len, block_len), 0)
    query_pos = lax.broadcasted_iota(jnp.int32, (block_len, block_len), 1)
    causal = jnp.where(key_pos <= query_pos, 0.0, -1e30)
    for level in range(depth):
        query = queries[level]
        marks = chosen_rows[level, :, 0:block_len].astype(jnp.float32)[0:1].astype(jnp.int32)
        pairs = [(c, side) for c in range(level + 1) for side in range(2)]
        run_max, chosen = None, []
        for index, (c, side) in enumerate(pairs):
            score = lax.dot_general(
                keys[c, side * block_len : (side + 1) * block_len],
                query,
                (((1,), (1,)), ((), ())),
                preferred_element_type=jnp.float32,
            )
            if c == level and side == 0:
                score = score + causal
                chosen.append(None)
                top = jnp.max(score, axis=0, keepdims=True)
            else:
                bit = 2 * c + (core if side == 0 else 1 - core)
                picked = lax.shift_right_logical(marks, jnp.broadcast_to(bit, marks.shape)) & 1
                chosen.append(picked == 1)
                top = jnp.where(chosen[-1], jnp.max(score, axis=0, keepdims=True), -1e30)
            scores[index] = score
            run_max = top if run_max is None else jnp.maximum(run_max, top)
        run_sum = total = None
        for index, (c, side) in enumerate(pairs):
            shift = run_max if chosen[index] is None else jnp.where(chosen[index], run_max, 1e30)
            weights = jnp.exp2((scores[index] - shift) * scaling)
            added = jnp.sum(weights, axis=0, keepdims=True)
            product = f32_dot(
                values[c, :, side * width : side * width + block_len], weights.astype(jnp.bfloat16)
            )
            run_sum = added if run_sum is None else run_sum + added
            total = product if total is None else total + product
        mixed[level] = (total / run_sum).T.astype(jnp.bfloat16)
    for turn in range(depth):
        outs[turn][...] = mixed[lax.rem(z_index + depth - turn, depth)]


def attend_gathered(normed_block, w_query, w_key, w_value, sel_blocks):
    block_len, heads_here, _ = sel_blocks.shape
    hidden_cols = w_query.shape[1]
    head_dim = hidden_cols // heads_here
    ctx_count, ctx_index = lax.axis_size("ctx"), lax.axis_index("ctx")
    query_part, key_part, value_part = (
        f32_dot(normed_block, weight).astype(jnp.bfloat16) for weight in (w_query, w_key, w_value)
    )
    queries = query_part.reshape(block_len, heads_here, head_dim)
    keys_values = jnp.stack([key_part, value_part], axis=1)
    block_ids = jnp.arange(ctx_count, dtype=jnp.int32)
    chosen = jnp.any(sel_blocks[:, :, :, None] == block_ids, axis=2) & (block_ids < ctx_index)
    position = jnp.arange(block_len, dtype=jnp.int32)
    causal = position[None, :] <= position[:, None]
    scaling = 1.0 / math.sqrt(head_dim)

    def fold_step(running, operands):
        run_max, run_sum, totals = running
        piece, block = operands
        key_rows = piece[:, 0].reshape(block_len, heads_here, head_dim)
        value_rows = piece[:, 1].reshape(block_len, heads_here, head_dim)
        scores = (
            jnp.einsum("qhd,khd->hqk", queries, key_rows, preferred_element_type=jnp.float32)
            * scaling
        )
        picked = jnp.take(chosen, block, axis=2).T[:, :, None]
        allowed = picked | ((block == ctx_index) & causal)[None]
        new_max = jnp.maximum(run_max, jnp.max(jnp.where(allowed, scores, -jnp.inf), axis=-1))
        weights = jnp.where(allowed, jnp.exp(scores - new_max[..., None]), 0.0)
        rescale = jnp.exp(run_max - new_max)
        run_sum = run_sum * rescale + jnp.sum(weights, axis=-1)
        totals = totals * rescale[..., None] + jnp.einsum(
            "hqk,khd->hqd",
            weights.astype(jnp.bfloat16),
            value_rows,
            preferred_element_type=jnp.float32,
        )
        return (new_max, run_sum, totals), None

    initial = (
        jnp.full((heads_here, block_len), -1e30, jnp.float32),
        jnp.zeros((heads_here, block_len), jnp.float32),
        jnp.zeros((heads_here, block_len, head_dim), jnp.float32),
    )
    gathered = lax.all_gather(keys_values, "ctx", axis=0)
    (_, run_sum, totals), _ = lax.scan(fold_step, initial, (gathered, block_ids))
    attended = (totals / run_sum[..., None]).astype(jnp.bfloat16)
    return [attended[head] for head in range(heads_here)]


def mix_kernel(heads, head_dim, hop, place, *refs):
    head_refs, w_out = refs[:heads], refs[heads]
    kept, given, attended = refs[heads + 1 :]
    exp_index, turned = place[0], place[3]
    tok_rows = kept.shape[0]
    starts = [pl.multiple_of((exp_index ^ (hop + side)) * tok_rows, 16) for side in range(2)]
    for turn, head_ref in enumerate(head_refs):
        head = lax.rem(turned + turn, heads)
        columns = pl.ds(pl.multiple_of(head * head_dim, head_dim), head_dim)
        for side in range(2):
            attended[side * tok_rows : (side + 1) * tok_rows, columns] = head_ref[pl.ds(starts[side], tok_rows), :]
    mixed = f32_dot(attended[...], w_out[...]).astype(jnp.bfloat16)
    kept[...] = mixed[:tok_rows]
    given[...] = mixed[tok_rows:]


def sum_kernel(kept, given, summed):
    summed[...] = (kept[...].astype(jnp.float32) + given[...].astype(jnp.float32)).astype(summed.dtype)


def residual_kernel(inputs, kept, given, far, gain, noted, residual, ffn_in):
    summed = kept[...].astype(jnp.float32) + given[...].astype(jnp.float32) + far[...].astype(jnp.float32)
    rounded = (inputs[...].astype(jnp.float32) + summed).astype(jnp.bfloat16)
    residual[...] = rounded
    model_width = rounded.shape[1]
    ffn_in[:, 0:model_width] = normalize(rounded, gain[...])
    ffn_in[:, model_width:] = noted[...].astype(jnp.bfloat16)


def pack_kernel(count, capacity, top_count, place, *refs):
    sources, outs, (notes, rows) = refs[:count], refs[count : count + 4], refs[count + 4 :]
    expert = place[4]
    tok_rows = sources[0].shape[0]
    total = count * tok_rows
    model_width = rows.shape[1]
    for turn in range(count):
        part = slice(turn * tok_rows, (turn + 1) * tok_rows)
        rows[part, :] = sources[turn][:, 0:model_width]
        notes[part, :] = sources[turn][:, model_width:]
    routes = notes[...].astype(jnp.float32).T[0:8]
    routes = jnp.where(lax.broadcasted_iota(jnp.int32, routes.shape, 0) < top_count, routes, -1.0)
    earlier = lax.broadcasted_iota(jnp.int32, (total, total), 0)
    later = lax.broadcasted_iota(jnp.int32, (total, total), 1)
    before = ((earlier < later) & (earlier // tok_rows == later // tok_rows)).astype(jnp.bfloat16)
    first_slot = lax.broadcasted_iota(jnp.int32, (1, total), 1) // tok_rows * capacity
    slot = lax.broadcasted_iota(jnp.int32, (count * capacity, total), 0)
    for hop in range(4):
        hit = jnp.where(routes == (expert ^ hop).astype(jnp.float32), 1.0, 0.0)
        member = jnp.sum(hit, axis=0, keepdims=True)
        place_in = f32_dot(jnp.broadcast_to(member, (16, total)).astype(jnp.bfloat16), before)[0:1]
        target = jnp.where(member > 0.5, place_in.astype(jnp.int32) + first_slot, -1)
        placing = jnp.where(slot == target, 1.0, 0.0).astype(jnp.bfloat16)
        outs[hop][...] = f32_dot(placing, rows[...]).astype(jnp.bfloat16)


def expert_kernel(slabs, *refs):
    parts = sum(len(members) for _, members in slabs)
    row_refs, weights = refs[:parts], refs[parts : parts + 6]
    outs, (held,) = refs[parts + 6 : 2 * parts + 6], refs[2 * parts + 6 :]
    across = (((1,), (1,)), ((), ()))
    for start, members in slabs:
        joined = [row_refs[part][...] for part in members]
        if len(joined) > 1:
            joined = [jnp.concatenate([row.astype(jnp.float32) for row in joined]).astype(jnp.bfloat16)]
        held[start : start + joined[0].shape[0], :] = joined[0]
    rows = held[...]
    result = None
    for w_gate, w_up, w_down in (weights[:3], weights[3:]):
        gate_part = lax.dot_general(rows, w_gate[...], across, preferred_element_type=jnp.float32)
        up_part = lax.dot_general(rows, w_up[...], across, preferred_element_type=jnp.float32)
        hidden = (gate_part / (1.0 + jnp.exp(-gate_part)) * up_part).astype(jnp.bfloat16)
        product = f32_dot(hidden, w_down[...])
        result = product if result is None else result + product
    for start, members in slabs:
        for part in members:
            count = outs[part].shape[0]
            outs[part][...] = result[start : start + count].astype(jnp.bfloat16)
            start += count


def weigh_kernel(count, capacity, top_count, place, notes, shares):
    expert = place[4]
    total = notes.shape[0]
    tok_rows = total // count
    row = lax.broadcasted_iota(jnp.int32, (LANES, LANES), 0)
    lane = lax.broadcasted_iota(jnp.int32, (LANES, LANES), 1)
    added = (lane < top_count) & (row == lane + top_count)
    gates = f32_dot(notes[...], jnp.where(added, 1.0, 0.0).astype(jnp.bfloat16))
    routes = notes[...].astype(jnp.float32)
    routes = jnp.where(lax.broadcasted_iota(jnp.int32, routes.shape, 1) < top_count, routes, -1.0)
    later = lax.broadcasted_iota(jnp.int32, (total, total), 0)
    earlier = lax.broadcasted_iota(jnp.int32, (total, total), 1)
    before = ((earlier < later) & (earlier // tok_rows == later // tok_rows)).astype(jnp.bfloat16)
    first_slot = lax.broadcasted_iota(jnp.int32, (total, 1), 0) // tok_rows * capacity
    slot = lax.broadcasted_iota(jnp.int32, (total, count * capacity), 1)
    for hop in range(4):
        hit = routes == (expert ^ hop).astype(jnp.float32)
        member = jnp.sum(jnp.where(hit, 1.0, 0.0), axis=1, keepdims=True)
        factor = jnp.sum(jnp.where(hit, gates, 0.0), axis=1, keepdims=True)
        place_in = f32_dot(before, jnp.broadcast_to(member, (total, LANES)).astype(jnp.bfloat16))[:, 0:1]
        target = jnp.where(member > 0.5, place_in.astype(jnp.int32) + first_slot, -1)
        placing = jnp.where(slot == target, factor, 0.0)
        shares[hop] = placing.astype(jnp.bfloat16)


def mix_slots(shares, returned):
    mixed = None
    for hop in range(4):
        term = f32_dot(shares[hop], returned[hop][...])
        mixed = term if mixed is None else mixed + term
    return mixed


def combine_kernel(count, shares, *refs):
    returned, outs = refs[:4], refs[4 : 4 + count]
    tok_rows = shares.shape[1] // count
    mixed = mix_slots(shares, returned)
    for turn in range(count):
        outs[turn][...] = mixed[turn * tok_rows : (turn + 1) * tok_rows].astype(jnp.bfloat16)


def finish_kernel(shares, *refs):
    returned, (residual, *others), out = refs[:4], refs[4:-1], refs[-1]
    total = residual[...].astype(jnp.float32) + mix_slots(shares, returned)
    for other in others:
        total = total + other[...].astype(jnp.float32)
    out[...] = total


def shards(
    inputs,
    attn_gain,
    w_query,
    w_key,
    w_value,
    w_out,
    sel_blocks,
    ffn_gain,
    w_gate,
    w_up,
    w_down,
    routes,
    gate_weights,
):
    tok_rows, model_width = inputs.shape
    block_len, heads_here, pick_count = sel_blocks.shape
    hidden_cols = w_query.shape[1]
    head_dim = hidden_cols // heads_here
    ctx_count, exp_count = lax.axis_size("ctx"), lax.axis_size("exp")
    depth = ctx_count // 2
    ctx_index, exp_index = lax.axis_index("ctx"), lax.axis_index("exp")
    z_index, x_index = ctx_index // 2, ctx_index % 2
    expert = (ctx_index * exp_count + exp_index) // 2
    by_head = heads_here == depth and block_len <= 3 * head_dim and head_dim == LANES
    place = jnp.stack(
        [exp_index, z_index, exp_index % 2, z_index if by_head else jnp.zeros_like(z_index), expert]
    ).astype(jnp.int32)

    far = move(inputs, lambda z, x, y, c: (z, x, y ^ 1, c))
    near = swap_core(inputs)
    weights = (w_gate, w_up, w_down)
    other_gate, other_up, other_down = swap_core(w_gate), None, swap_core(w_down)
    top_count = routes.shape[1]
    noted = jnp.concatenate([routes.astype(jnp.float32), gate_weights], axis=1)
    noted = jnp.pad(noted, ((0, 0), (0, LANES - noted.shape[1])))
    if by_head:
        marks = jnp.sum(
            jnp.where(sel_blocks < ctx_index, jnp.left_shift(1, jnp.minimum(sel_blocks, 30)), 0), axis=2
        )
        marks = jnp.pad(marks.T.astype(jnp.bfloat16), ((0, 0), (0, 3 * head_dim - block_len)))
        marks = jnp.broadcast_to(marks[:, None], (heads_here, PAD_ROWS, 3 * head_dim))
        payload = struct(block_len + PAD_ROWS, 3 * head_dim)
        gain_row = attn_gain.reshape(1, -1)
        near_mixed, *held = call(
            near_kernel,
            [struct(3, 2 * tok_rows, hidden_cols)] + [struct(model_width, hidden_cols)] * 3,
            [place, near, gain_row, inputs, w_query, w_key, w_value],
            [
                pltpu.VMEM((2, tok_rows, model_width), jnp.bfloat16),
                pltpu.VMEM((1, model_width), jnp.float32),
                pltpu.VMEM((2 * tok_rows, model_width), jnp.bfloat16),
                pltpu.SemaphoreType.DMA((6,)),
            ],
            flops=12 * tok_rows * model_width * hidden_cols,
            anywhere=1,
            hbm=5,
        )
        far_near = swap_core(after(far, near_mixed))
        far_near, other_gate, other_down = lax.optimization_barrier((far_near, other_gate, other_down))
        sent = call(
            functools.partial(project_kernel, depth, head_dim),
            [payload] * depth,
            [place, marks, near_mixed, gain_row, *held, far, far_near],
            [
                pltpu.VMEM((2, tok_rows, model_width), jnp.bfloat16),
                pltpu.VMEM((2 * tok_rows, model_width), jnp.bfloat16),
                pltpu.VMEM((3, block_len, hidden_cols), jnp.bfloat16),
                pltpu.SemaphoreType.DMA((2,)),
            ],
            flops=12 * tok_rows * model_width * hidden_cols,
            anywhere=2,
        )
        own = [head_out(sent[turn], turn) for turn in range(depth)]
        beside = [swap_core(block) for block in own]
        mixed = call(
            functools.partial(attend_kernel, depth, block_len, head_dim),
            [struct(block_len, head_dim)] * depth,
            [place, *own, *beside],
            [
                pltpu.VMEM((depth, block_len, head_dim), jnp.bfloat16),
                pltpu.VMEM((depth, 2 * block_len, head_dim), jnp.bfloat16),
                pltpu.VMEM((depth, head_dim, 2 * 3 * head_dim), jnp.bfloat16),
                pltpu.VMEM((depth, PAD_ROWS, 3 * head_dim), jnp.bfloat16),
                pltpu.VMEM((2 * depth, block_len, block_len), jnp.float32),
                pltpu.VMEM((depth, block_len, head_dim), jnp.bfloat16),
            ],
            flops=4 * depth * ctx_count * block_len * block_len * head_dim,
        )
        heads = [head_back(mixed[turn], turn) for turn in range(depth)]
    else:
        block = jnp.stack([inputs, near, far, swap_core(far)])[exp_index ^ jnp.arange(exp_count)]
        normed = normalize(block.reshape(block_len, model_width), attn_gain)
        heads = attend_gathered(normed, w_query, w_key, w_value, sel_blocks)

    def mixed_rows(hop, heads):
        return call(
            functools.partial(mix_kernel, heads_here, head_dim, hop),
            [struct(tok_rows, model_width)] * 2,
            [place, *heads, w_out],
            [pltpu.VMEM((2 * tok_rows, hidden_cols), jnp.bfloat16)],
            flops=4 * tok_rows * model_width * hidden_cols,
        )

    far_kept, far_given = mixed_rows(2, heads)
    kept, given = mixed_rows(0, [after(heads[0], far_given)] + heads[1:])
    far_given = swap_core(far_given)
    beyond = call(sum_kernel, struct(tok_rows, model_width), [after(far_kept, kept), far_given], smem=0)
    given = swap_core(after(given, beyond))
    other_up = swap_core(after(w_up, beyond))
    own_weights, other_weights = (
        [gate[0].T, up[0].T, down[0]] for gate, up, down in (weights, (other_gate, other_up, other_down))
    )
    g, u, d = other_weights
    *own, g, d = load([], [after(weight, beyond) for weight in [*own_weights, g, d]])
    expert_weights = [*own, g, u, d]
    beyond = move(beyond, lambda z, x, y, c: (z, x, y ^ 1, c))
    beyond, expert_weights = lax.optimization_barrier((beyond, expert_weights))
    residual, ffn_in = call(
        residual_kernel,
        [struct(tok_rows, model_width), struct(tok_rows, model_width + LANES)],
        [inputs, kept, given, beyond, ffn_gain.reshape(1, -1), noted],
        smem=0,
    )

    experts = ctx_count * exp_count // 2
    capacity = 2 * max(1, (tok_rows * top_count + experts - 1) // experts * 2 // 3)
    column = gather_z(ffn_in)
    groups = [[0], [1, depth - 1], list(range(2, depth - 1))]
    arrived, notes = [], []
    for group in groups:
        count = len(group)
        first = column[group[0]]
        if len(arrived) == 1:
            (up,) = load([], [after(expert_weights[4], arrived[0][0])])
            expert_weights[4] = up
            first = after(first, up, *arrived[0])
        elif arrived:
            first = after(first, arrived[-1][0])
        *packed, note = call(
            functools.partial(pack_kernel, count, capacity, top_count),
            [struct(count * capacity, model_width)] * 4 + [struct(count * tok_rows, LANES)],
            [place, first, *[column[t] for t in group[1:]]],
            [pltpu.VMEM((count * tok_rows, model_width), jnp.bfloat16)],
            flops=8 * count * capacity * count * tok_rows * model_width,
            limit=8 * MIB + 16 * (count * tok_rows) ** 2 + 8 * count * tok_rows * model_width,
        )
        arrived.append([packed[0]] + [swap_layer(packed[hop], hop) for hop in range(1, 4)])
        notes.append(note)

    def expert_rows(rows):
        slabs, total, part = [], 0, 0
        while part < len(rows):
            count = rows[part].shape[0]
            pair = count % 16 == 8 and part + 1 < len(rows) and rows[part + 1].shape[0] == count
            members = [part, part + 1] if pair else [part]
            slabs.append((total, members))
            total += -(-len(members) * count // 16) * 16
            part += len(members)
        return call(
            functools.partial(expert_kernel, slabs),
            [struct(*row.shape) for row in rows],
            [*rows, *expert_weights],
            [pltpu.VMEM((total, model_width), jnp.bfloat16)],
            flops=12 * total * model_width * w_gate.shape[2],
            smem=0,
            limit=4 * MIB + 32 * 1024 * total,
        )

    shares = []
    for group, note in zip(groups, notes):
        count = len(group)
        total = count * tok_rows
        shares.append(
            call(
                functools.partial(weigh_kernel, count, capacity, top_count),
                struct(4, total, count * capacity),
                [place, note],
                flops=8 * total * total * LANES,
                limit=8 * MIB + 16 * total * total,
            )
        )
    arrived[1][1] = after(arrived[1][1], *shares)
    own_results = expert_rows(arrived[0])
    next_results = expert_rows([after(arrived[1][0], own_results[0])] + arrived[1][1:])
    far_results = expert_rows([after(arrived[2][0], next_results[0])] + arrived[2][1:])
    results = [own_results, next_results, far_results]
    sums = [None] * depth
    home = [None] * depth
    for index in (1, 2):
        group, rows = groups[index], list(results[index])
        rows = [rows[0]] + [swap_layer(rows[hop], hop) for hop in range(1, 4)]
        count = len(group)
        total = count * tok_rows
        parts = call(
            functools.partial(combine_kernel, count),
            [struct(tok_rows, model_width)] * count,
            [shares[index], *rows],
            flops=16 * count * capacity * total * model_width,
            smem=0,
            limit=8 * MIB + 16 * total * model_width,
        )
        for turn, part in zip(group, parts):
            sums[turn] = part
            home[turn] = turn_z(part, -turn)
    rows = [results[0][0]] + [swap_layer(after(results[0][hop], sums[1]), hop) for hop in range(1, 4)]
    layer_out = call(
        finish_kernel,
        struct(tok_rows, model_width, dtype=jnp.float32),
        [shares[0], *rows, residual, *(home[turn] for turn in groups[1])],
        flops=16 * capacity * tok_rows * model_width,
        smem=0,
    )
    for turn in groups[2]:
        layer_out = layer_out + home[turn].astype(jnp.float32)
    return layer_out.astype(jnp.bfloat16)


def solution(mesh):
    placed = (
        P(("ctx", "exp"), None),
        P(),
        P(None, "exp"),
        P(None, "exp"),
        P(None, "exp"),
        P("exp", None),
        P("ctx", "exp", None),
        P(),
        P(("ctx", "exp"), None, None),
        P(("ctx", "exp"), None, None),
        P(("ctx", "exp"), None, None),
        P(("ctx", "exp"), None),
        P(("ctx", "exp"), None),
    )
    return jax.shard_map(
        shards, mesh=mesh, in_specs=placed, out_specs=P(("ctx", "exp"), None), check_vma=False
    )
```
